128 devices in a mesh: dp: 64 (over y, z_hi, x, core), pair: 2 (over z_lo).
Axes of the slice: x: 4, y: 4, z: 4 (z_hi: 2, z_lo: 2; z = z_hi * 2 + z_lo), core: 2. Of those that a mesh axis runs over, the one named last changes fastest.
Arguments:
- events: bfloat16 [65536, 2048], P(('dp', 'pair')), may hold values from -6 to 6
- w_uvqk: bfloat16 [2048, 4096], P(None, 'dp'), may hold values from -0.125 to 0.125
- w_out: bfloat16 [1024, 2048], P('dp'), may hold values from -0.1875 to 0.1875
- targets: bfloat16 [65536, 2048], P(('dp', 'pair')), may hold values from -0.125 to 0.125
- item_ids: int32 [65536], P(('dp', 'pair')), may hold values from 0 to 4095
- uniform_flags: int32 [65536], P(('dp', 'pair')), may hold values from 0 to 1, as said below
- lengths: int32 [128, 8], P(('dp', 'pair')), may hold values from 1 to 128, 512 in all within a row
- seq_weights: float32 [1024], P(('dp', 'pair')), may hold values from 0.2 to 5
Outputs:
- hyper: float32 [1024], P(('dp', 'pair'))
- weighted_grad: float32 [1024, 2048], P(('dp', 'pair'))
The draws below stay inside these ranges and needn't reach their ends.
Inputs may be any that keep to these rules, and one draw needn't show every extreme that they name: `uniform_flags`: in every block of 512 events the first is flagged 1 and the last 0. Each row holds the lengths of one block's 8 sequences and sums to 512.
All inputs are finite; a program needn't handle non-finite values.
Results may differ from the reference program's by a relative error of at most 0.015.
Values may be sent and summed in bfloat16 or wider, within the bound.
No kernel may reach another device: no remote copies, remote signals or barrier semaphores. Data moves between devices by JAX's collectives and lax.ppermute only.
A program may use at most 128 MiB of HBM per device.

```python
import math
import jax
import jax.numpy as jnp
import numpy as np
from jax import lax

D = 2048
HEADS = 8
DH = 128
HD = 1024
EV_DEV = 512
SEQ_DEV = 8
SEQ_MAX = 128
ITEMS = 4096
EVENTS = 65536
NSEQ = 1024
N_DP = 64
N_PAIR = 2


def draw_uniform_flags(key, part):
    key = jax.random.fold_in(key, 11)
    rolls = jax.random.randint(key, (EVENTS,), 0, 1000)
    place = jnp.arange(EVENTS, dtype=jnp.int32)
    block = place // EV_DEV
    blocks = EVENTS // EV_DEV
    limit = 100 + 600 * block // max(blocks - 1, 1)
    flags = (rolls < limit).astype(jnp.int32)
    inner = place % EV_DEV
    flags = jnp.where(inner == 0, 1, jnp.where(inner == EV_DEV - 1, 0, flags))
    return flags.astype(jnp.int32)


def with_ends(entries, own_key, low, high):
    shape = entries.shape
    index_at = [jax.random.randint(jax.random.fold_in(own_key, axis), (), 0, shape[axis]) for axis in range(len(shape))]
    entries = entries.at[tuple(index_at)].set(low)
    longest = shape.index(max(shape))
    index_at[longest] = (index_at[longest] + 1) % shape[longest]
    return entries.at[tuple(index_at)].set(high)


def block_levels(key, extent, pieces, least, high):
    def one(position, parts):
        steps = jax.random.uniform(jax.random.fold_in(jax.random.fold_in(key, 6), position), (parts,), jnp.float32, least / len(pieces), high / len(pieces))
        return jnp.repeat(jnp.exp(steps), extent[position] // parts).reshape((-1,) + (1,) * (len(extent) - position - 1))

    gain = one(*pieces[0])
    for cut in pieces[1:]:
        gain = gain * one(*cut)
    return gain


def cumulative_ranks(amount, lean):
    loads = [(1 << 20) // math.isqrt(rank ** lean) + 1 for rank in range(1, amount + 1)]
    scale = 1 + sum(loads) // (1 << 30)
    return np.cumsum(np.array([max(1, weight // scale) for weight in loads]))


def ranked(rng, extent, count, slope):
    table = cumulative_ranks(count, slope)
    ticket = jax.random.randint(jax.random.fold_in(rng, 1), extent, 0, int(table[count - 1]))
    standing = jnp.searchsorted(jnp.asarray(table, jnp.int32), ticket, side="right")
    return jax.random.permutation(jax.random.fold_in(rng, 2), count)[standing].astype(jnp.int32)


def split_up(count, total, bound, lean):
    weights = [(1 << 20) // math.isqrt(rank ** lean) + 1 for rank in range(2, count + 1)]
    surplus, holding = total - bound - (count - 1), [1] * (count - 1)
    while surplus > 0:
        free = [i for i in range(count - 1) if holding[i] < bound]
        mass, left = sum([weights[i] for i in free]), surplus
        for i in free:
            extra = min(bound - holding[i], max(1, left * weights[i] // mass), surplus)
            holding[i] = holding[i] + extra
            surplus = surplus - extra
    return np.array([bound] + holding)


def uneven(stream_key, number_of, total, most, skew):
    if number_of == 2:
        one = jax.random.randint(stream_key, (), max(1, total - most), min(most, total - 1) + 1)
        return jnp.stack([one, total - one])
    tallies = jnp.asarray(split_up(number_of, total, most, skew), jnp.int32)
    couples = (number_of - 1) // 2
    giver, receiver = tallies[1:1 + 2 * couples:2], tallies[2:2 + 2 * couples:2]
    margin = jnp.minimum(giver - 1, most - receiver)
    moved = jax.random.randint(jax.random.fold_in(stream_key, 1), (couples,), 0, 1 << 20) % (margin + 1)
    tallies = tallies.at[1:1 + 2 * couples:2].set(giver - moved).at[2:2 + 2 * couples:2].set(receiver + moved)
    return tallies[jax.random.permutation(jax.random.fold_in(stream_key, 2), number_of)]


def scatter_about(own_key, shape, spread, most, shards=(), kind=jnp.bfloat16):
    values = jax.random.normal(own_key, shape, jnp.float32) * spread
    if len(shards) > 0:
        values = block_levels(own_key, shape, shards, -0.22, 0.18) * values
    return jnp.clip(values, min=-most, max=most).astype(kind)


def setup_inputs(seed: int = 0) -> dict:
    seeds = jax.random.split(jax.random.key(seed), 9)
    events = scatter_about(seeds[0], (EVENTS, D), 1.0, 6.0, ((0, 128),))
    w_uvqk = scatter_about(seeds[1], (D, 4 * HD), D ** -0.5, 0.125, ((1, 64),))
    w_out = scatter_about(seeds[2], (HD, D), HD ** -0.5, 0.1875, ((0, 64),))
    targets = scatter_about(seeds[3], (EVENTS, D), D ** -0.5, 0.125, ((0, 128),))
    item_ids = with_ends(ranked(seeds[4], (EVENTS,), ITEMS, 2), jax.random.fold_in(seeds[4], 3), 0, ITEMS - 1).astype(jnp.int32)
    uniform_flags = draw_uniform_flags(jax.random.fold_in(seeds[8], 71), 0)
    lengths = jax.vmap(lambda own: uneven(own, SEQ_DEV, EV_DEV, SEQ_MAX, 1))(jax.random.split(seeds[6], (N_DP * N_PAIR))).reshape((N_DP * N_PAIR, SEQ_DEV)).astype(jnp.int32)
    seq_weights = jnp.clip(jnp.exp(math.log(5.0) - 3.218876 * jax.random.uniform(seeds[7], (NSEQ,), jnp.float32) ** block_levels(seeds[7], (NSEQ,), ((0, 128),), -0.2, 0.2)), 0.2, 5.0)
    return dict(events=events, w_uvqk=w_uvqk, w_out=w_out, targets=targets, item_ids=item_ids, uniform_flags=uniform_flags, lengths=lengths, seq_weights=seq_weights)


def block_pass(items):
    rows, proj_in, proj_out, goal, ident, lens = items
    count = rows.shape[0]
    pre = jnp.dot(rows, proj_in, preferred_element_type=jnp.float32)
    uvqk = jax.nn.silu(pre).astype(jnp.bfloat16)
    width = proj_out.shape[0]
    gate_u = uvqk[:, 0:width]
    vals = uvqk[:, width:2 * width]
    query = uvqk[:, 2 * width:3 * width]
    keys = uvqk[:, 3 * width:4 * width]
    place = jnp.arange(count, dtype=jnp.int32)
    ends = jnp.cumsum(lens).astype(jnp.int32)
    seqid = lax.optimization_barrier(jnp.sum((place[:, None] >= ends[None, :]).astype(jnp.int32), axis=1))
    allowed = (seqid[:, None] == seqid[None, :]) & (place[:, None] >= place[None, :])
    qh = query.reshape(count, HEADS, DH).astype(jnp.float32)
    kh = keys.reshape(count, HEADS, DH).astype(jnp.float32)
    vh = vals.reshape(count, HEADS, DH).astype(jnp.float32)
    sc = jnp.einsum('ihd,jhd->hij', qh, kh) / jnp.sqrt(jnp.float32(DH))
    probs = jnp.where(allowed[None], jax.nn.silu(sc) / SEQ_MAX, 0.0).astype(jnp.bfloat16)
    attn = jnp.einsum('hij,jhd->ihd', probs.astype(jnp.float32), vh).reshape(count, width)
    mean = lax.optimization_barrier(jnp.mean(attn, axis=1, keepdims=True))
    var = lax.optimization_barrier(jnp.mean((attn - mean) ** 2, axis=1, keepdims=True))
    mixed = ((attn - mean) * lax.rsqrt(var + 1e-05) * gate_u.astype(jnp.float32)).astype(jnp.bfloat16)
    outs = (rows.astype(jnp.float32) + jnp.dot(mixed, proj_out, preferred_element_type=jnp.float32)).astype(jnp.bfloat16)
    scores = jnp.dot(outs, goal.T, preferred_element_type=jnp.float32)
    diag = place[:, None] == place[None, :]
    other = ident[:, None] != ident[None, :]
    coef = jnp.where(diag, -jax.nn.sigmoid(-scores), jnp.where(other, jax.nn.sigmoid(scores) / count, 0.0)).astype(jnp.bfloat16)
    grad_out = jnp.dot(coef, goal, preferred_element_type=jnp.float32).astype(jnp.bfloat16)
    return (mixed, grad_out, seqid)

def reference(events, w_uvqk, w_out, targets, item_ids, uniform_flags, lengths, seq_weights):
    blocks = N_DP * N_PAIR
    rows = events.reshape(blocks, EV_DEV, D)
    goal = targets.reshape(blocks, EV_DEV, D)
    ident = item_ids.reshape(blocks, EV_DEV)
    mixed, grad_out, seqid = lax.map(lambda it: block_pass((it[0], w_uvqk, w_out, it[1], it[2], it[3])), (rows, goal, ident, lengths))
    mixed = mixed.reshape(EVENTS, HD)
    grad_out = grad_out.reshape(EVENTS, D)
    seq_all = (seqid + SEQ_DEV * jnp.arange(blocks, dtype=jnp.int32)[:, None]).reshape(EVENTS).astype(jnp.int32)
    flag = uniform_flags.astype(jnp.float32)
    n_unif = jnp.sum(flag)
    n_train = jnp.float32(EVENTS) - n_unif
    unif_rows = grad_out * uniform_flags[:, None].astype(jnp.bfloat16)
    unif_grad = lax.dot_general(mixed, unif_rows, (((0,), (0,)), ((), ())), preferred_element_type=jnp.float32) / n_unif
    unif_hi = unif_grad.astype(jnp.bfloat16)
    unif_lo = (unif_grad - unif_hi.astype(jnp.float32)).astype(jnp.bfloat16)
    proj = jnp.dot(grad_out, unif_hi.T, preferred_element_type=jnp.float32) + jnp.dot(grad_out, unif_lo.T, preferred_element_type=jnp.float32)
    per_row = -lax.optimization_barrier(jnp.sum(mixed.astype(jnp.float32) * proj, axis=1)) * (1.0 - flag)
    hyper = jax.ops.segment_sum(per_row, seq_all, num_segments=NSEQ)
    weight_row = seq_weights[seq_all] * (1.0 - flag)
    scaled = (grad_out.astype(jnp.float32) * weight_row[:, None]).astype(jnp.bfloat16)
    weighted_grad = lax.dot_general(mixed, scaled, (((0,), (0,)), ((), ())), preferred_element_type=jnp.float32) / n_train
    return (hyper, weighted_grad)
```

```python
import jax
import jax.numpy as jnp
from jax import lax
from jax.sharding import Mesh
from jax.sharding import PartitionSpec as P

HEADS = 8
DH = 128
AXES = ("y", "zh", "x", "c", "zl")
CHIPS = ("y", "zh", "x", "zl")
SWAP = [(0, 1), (1, 0)]


def split_core(parts):
    core = lax.axis_index("c")
    away = lax.dynamic_index_in_dim(parts, 1 - core, 0, keepdims=False)
    mine = lax.dynamic_index_in_dim(parts, core, 0, keepdims=False)
    came = lax.ppermute(away, "c", SWAP)
    return (mine.astype(jnp.float32) + came.astype(jnp.float32)).astype(jnp.bfloat16)


def scatter_chips(half):
    rows = half.shape[0] // 64
    got = lax.all_to_all(half.reshape(64, rows, -1), CHIPS, 0, 0, tiled=True)
    return jnp.sum(got.astype(jnp.float32), axis=0)


def gather_chips(rows):
    got = lax.all_to_all(jnp.broadcast_to(rows[None], (64,) + rows.shape), CHIPS, 0, 0, tiled=True)
    return got.reshape(64 * rows.shape[0], -1)


def on_device(events, w_uvqk, w_out, targets, item_ids, uniform_flags, lengths, seq_weights):
    count = events.shape[0]
    width = HEADS * DH
    seq_max = count // 4
    core = lax.axis_index("c")
    flag = uniform_flags.astype(jnp.float32)
    counts = lax.all_to_all(jnp.broadcast_to(jnp.sum(flag), (128, 128)), AXES, 0, 0, tiled=True)
    n_unif = jnp.sum(counts[:, 0])
    n_train = jnp.float32(count * 128) - n_unif
    dp = ("y", "zh", "x", "c")
    pre = jnp.dot(
        events, lax.all_gather(w_uvqk, dp, axis=1, tiled=True), preferred_element_type=jnp.float32
    )
    uvqk = jax.nn.silu(pre).astype(jnp.bfloat16)
    gate_u = uvqk[:, 0:width]
    vals = uvqk[:, width : 2 * width].reshape(count, HEADS, DH)
    query = uvqk[:, 2 * width : 3 * width].reshape(count, HEADS, DH)
    keys = uvqk[:, 3 * width : 4 * width].reshape(count, HEADS, DH)
    place = jnp.arange(count, dtype=jnp.int32)
    ends = jnp.cumsum(lengths[0])
    seqid = jnp.sum((place[:, None] >= ends[None, :]).astype(jnp.int32), axis=1)
    allowed = (seqid[:, None] == seqid[None, :]) & (place[:, None] >= place[None, :])
    scores_att = jnp.einsum(
        "ihd,jhd->hij", query, keys, preferred_element_type=jnp.float32
    ) / jnp.sqrt(jnp.float32(DH))
    probs = jnp.where(allowed[None], jax.nn.silu(scores_att) / seq_max, 0.0).astype(jnp.bfloat16)
    attn = jnp.einsum("hij,jhd->ihd", probs, vals, preferred_element_type=jnp.float32).reshape(
        count, width
    )
    mean = jnp.mean(attn, axis=1, keepdims=True)
    var = jnp.mean((attn - mean) ** 2, axis=1, keepdims=True)
    mixed = ((attn - mean) * lax.rsqrt(var + 1e-05) * gate_u.astype(jnp.float32)).astype(
        jnp.bfloat16
    )
    summed = jnp.dot(
        mixed, lax.all_gather(w_out, dp, axis=0, tiled=True), preferred_element_type=jnp.float32
    )
    outputs = (events.astype(jnp.float32) + summed).astype(jnp.bfloat16)
    scores = jnp.dot(outputs, targets.T, preferred_element_type=jnp.float32)
    diag = place[:, None] == place[None, :]
    other = item_ids[:, None] != item_ids[None, :]
    coef = jnp.where(
        diag, -jax.nn.sigmoid(-scores), jnp.where(other, jax.nn.sigmoid(scores) / count, 0.0)
    ).astype(jnp.bfloat16)
    grad_out = jnp.dot(coef, targets, preferred_element_type=jnp.float32).astype(jnp.bfloat16)
    member = (seqid[:, None] == jnp.arange(seq_weights.shape[0], dtype=jnp.int32)[None, :]).astype(
        jnp.float32
    )
    weight_row = jnp.sum(member * seq_weights[None, :], axis=1) * (1.0 - flag)
    scaled = (grad_out.astype(jnp.float32) * weight_row[:, None]).astype(jnp.bfloat16)
    unif_rows = grad_out * uniform_flags[:, None].astype(jnp.bfloat16)
    contract = (((0,), (0,)), ((), ()))
    local_unif = lax.dot_general(mixed, unif_rows, contract, preferred_element_type=jnp.float32)
    half_unif = split_core(local_unif.astype(jnp.bfloat16).reshape(2, 512, -1))
    unif_rows_sum = scatter_chips(half_unif).astype(jnp.bfloat16)
    unif_mine = gather_chips(unif_rows_sum)
    unif_away = lax.ppermute(unif_mine, "c", SWAP)
    mixed_mine = lax.dynamic_slice_in_dim(mixed, core * 512, 512, 1)
    mixed_away = lax.dynamic_slice_in_dim(mixed, (1 - core) * 512, 512, 1)
    proj_mine = jnp.dot(grad_out, unif_mine.T, preferred_element_type=jnp.float32)
    proj_away = jnp.dot(grad_out, unif_away.T, preferred_element_type=jnp.float32)
    per_row = jnp.sum(mixed_mine.astype(jnp.float32) * proj_mine, axis=1) + jnp.sum(
        mixed_away.astype(jnp.float32) * proj_away, axis=1
    )
    per_row = -per_row * (1.0 - flag) / n_unif
    hyper = jnp.sum(member * per_row[:, None], axis=0)
    local_w = lax.dot_general(mixed, scaled, contract, preferred_element_type=jnp.float32)
    parts_w = local_w.astype(jnp.bfloat16).reshape(32, 2, 16, -1).transpose(1, 0, 2, 3)
    half_w = split_core(parts_w.reshape(2, 512, -1))
    weighted_grad = scatter_chips(half_w) / n_train
    return (hyper, weighted_grad)


def solution(mesh):
    fine = Mesh(mesh.devices.reshape(4, 2, 4, 2, 2), AXES)
    dp = ("y", "zh", "x", "c")
    return jax.shard_map(
        on_device,
        mesh=fine,
        in_specs=(
            P(AXES, None),
            P(None, dp),
            P(dp, None),
            P(AXES, None),
            P(AXES),
            P(AXES),
            P(AXES, None),
            P(AXES),
        ),
        out_specs=(P(AXES), P(AXES, None)),
        check_vma=False,
    )
```

```python
import jax
import jax.numpy as jnp
from jax import lax
from jax.experimental import pallas as pl
from jax.experimental.pallas import tpu as pltpu
from jax.sharding import Mesh
from jax.sharding import PartitionSpec as P

HEADS = 8
DH = 128
AXES = ("y", "zh", "x", "c", "zl")
CHIPS = ("y", "zh", "x", "zl")
SWAP = [(0, 1), (1, 0)]


def split_core(parts):
    core = lax.axis_index("c")
    away = lax.dynamic_index_in_dim(parts, 1 - core, 0, keepdims=False)
    mine = lax.dynamic_index_in_dim(parts, core, 0, keepdims=False)
    came = lax.ppermute(away, "c", SWAP)
    return (mine.astype(jnp.float32) + came.astype(jnp.float32)).astype(jnp.bfloat16)


def scatter_chips(half):
    rows = half.shape[0] // 64
    got = lax.all_to_all(half.reshape(64, rows, -1), CHIPS, 0, 0, tiled=True)
    return jnp.sum(got.astype(jnp.float32), axis=0)


def gather_chips(rows):
    got = lax.all_to_all(jnp.broadcast_to(rows[None], (64,) + rows.shape), CHIPS, 0, 0, tiled=True)
    return got.reshape(64 * rows.shape[0], -1)


def hop(array, axis, step):
    return lax.ppermute(array, axis, [(i, (i + step) % 4) for i in range(4)])


def around(mine):
    def ring(axis):
        below, above = hop(mine, axis, 1), hop(mine, axis, -1)
        far = (hop(below[: mine.shape[0] // 2], axis, 1), hop(above[mine.shape[0] // 2 :], axis, -1))
        return (mine, above, far, below)

    return ring


def gather_proj(w_uvqk):
    core = lax.axis_index("c")
    half = w_uvqk.shape[0] // 2
    rows = w_uvqk.T
    away = lax.dynamic_slice_in_dim(rows, (1 - core) * half, half, 1)
    mine = lax.dynamic_slice_in_dim(rows, core * half, half, 1)
    came = lax.ppermute(away, "c", SWAP)
    block = jnp.where(
        core == 0, jnp.concatenate([mine, came], 0), jnp.concatenate([came, mine], 0)
    )
    other = lax.ppermute(block, ("zh", "zl"), [(0, 3), (3, 0), (1, 2), (2, 1)])
    both = jnp.stack([block, other])

    def line(part, axis):
        flat = part.reshape((4, part.shape[0] * part.shape[1] // 4, part.shape[2]))
        own, above, far, below = around(flat)(axis)
        return jnp.stack([v.reshape(part.shape) for v in (own, above, jnp.concatenate(far, 0), below)])

    a_line = line(both[:, :, : half // 2], "x")
    b_line = line(both[:, :, half // 2 :], "y")
    return around(a_line)("y"), around(b_line)("x")


def place_of(pieces, major, minor):
    flat = [pieces[0], pieces[1], pieces[2][0], pieces[2][1], pieces[3]]
    if major == 2:
        return flat[2 + minor // 2], minor % 2
    return flat[(0, 1, 2, 4)[major]], minor


def run_uvqk(steps, weights, place, events, tail):
    out, w_buf, o_buf, w_sem, o_sem = tail
    here = [place[i] for i in range(4)]
    half = events.shape[1] // 2
    quarter = half // 2

    def copies(n):
        slot = n % 2
        made = []
        for part in range(4):
            src, index = steps[n][1][part]
            made.append(
                pltpu.make_async_copy(
                    weights[src].at[index], w_buf.at[slot, part], w_sem.at[slot, part]
                )
            )
        return made

    for c in copies(0):
        c.start()
    outs = [None, None]
    for n, ((y_off, x_off), _) in enumerate(steps):
        slot = n % 2
        if n + 1 < len(steps):
            for c in copies(n + 1):
                c.start()
        for c in copies(n):
            c.wait()
        acc = None
        for part in range(4):
            side = here[3] if part < 2 else 1 - here[3]
            start = pl.multiple_of(side * half + (part % 2) * quarter, quarter)
            rows = w_buf[slot, part].reshape(256, quarter)
            term = lax.dot_general(
                events[:, pl.ds(start, quarter)],
                rows,
                (((1,), (1,)), ((), ())),
                preferred_element_type=jnp.float32,
            )
            acc = term if acc is None else acc + term
        act = (0.5 * acc * (1.0 + jnp.tanh(0.5 * acc))).astype(jnp.bfloat16)
        if outs[slot] is not None:
            for c in outs[slot]:
                c.wait()
        outs[slot] = []
        for z_off in range(2):
            o_buf[slot, z_off] = act[:, z_off * 128 : (z_off + 1) * 128]
            z_at = here[1] if z_off == 0 else 1 - here[1]
            c = pltpu.make_async_copy(
                o_buf.at[slot, z_off],
                out.at[lax.rem(here[0] + y_off, 4), z_at, lax.rem(here[2] + x_off, 4)],
                o_sem.at[slot, z_off],
            )
            c.start()
            outs[slot].append(c)
    for pending in outs:
        for c in pending or []:
            c.wait()


def uvqk_call(place, events, a_own, b_own, a_away, b_away, offsets, onto=None):
    count = events.shape[0]
    arrays, steps = [], []

    def seat(array):
        for i, seen in enumerate(arrays):
            if seen is array:
                return i
        arrays.append(array)
        return len(arrays) - 1

    for y_off, x_off in offsets:
        found = (
            place_of(a_own, y_off, x_off),
            place_of(b_own, x_off, y_off),
            place_of(a_away, y_off, x_off),
            place_of(b_away, x_off, y_off),
        )
        steps.append(((y_off, x_off), [(seat(array), index) for array, index in found]))
    near = len(arrays)
    extra = [] if onto is None else [onto]
    any_spec = pl.BlockSpec(memory_space=pl.ANY)

    def kernel(place_ref, events_ref, *refs):
        weights, tail = refs[:near], refs[near + len(extra) :]
        run_uvqk(steps, weights, place_ref, events_ref, tail)

    return pl.pallas_call(
        kernel,
        out_shape=jax.ShapeDtypeStruct((4, 2, 4, count, 128), jnp.bfloat16),
        in_specs=[
            pl.BlockSpec(memory_space=pltpu.SMEM),
            pl.BlockSpec(memory_space=pltpu.VMEM),
        ]
        + [any_spec] * (near + len(extra)),
        out_specs=any_spec,
        scratch_shapes=[
            pltpu.VMEM((2, 4) + a_own[0].shape[1:], jnp.bfloat16),
            pltpu.VMEM((2, 2, count, 128), jnp.bfloat16),
            pltpu.SemaphoreType.DMA((2, 4)),
            pltpu.SemaphoreType.DMA((2, 2)),
        ],
        input_output_aliases={} if onto is None else {2 + near: 0},
        cost_estimate=pl.CostEstimate(
            flops=2 * count * events.shape[1] * 256 * len(steps),
            bytes_accessed=events.shape[1] * 512 * len(steps),
            transcendentals=count * 256 * len(steps),
        ),
        compiler_params=pltpu.CompilerParams(vmem_limit_bytes=32 * 1024 * 1024),
    )(place, events, *arrays, *extra)


def on_device(events, w_uvqk, w_out, targets, item_ids, uniform_flags, lengths, seq_weights):
    count = events.shape[0]
    width = HEADS * DH
    seq_max = count // 4
    core = lax.axis_index("c")
    flag = uniform_flags.astype(jnp.float32)
    counts = lax.all_to_all(jnp.broadcast_to(jnp.sum(flag), (128, 128)), AXES, 0, 0, tiled=True)
    n_unif = jnp.sum(counts[:, 0])
    n_train = jnp.float32(count * 128) - n_unif
    dp = ("y", "zh", "x", "c")
    a_own, b_own = gather_proj(w_uvqk)
    a_away, b_away = jax.tree.map(lambda v: lax.ppermute(v, "c", SWAP), (a_own, b_own))
    spot = jnp.stack([lax.axis_index(n) for n in ("y", "zh", "x", "c")]).astype(jnp.int32)
    grid = [(i, j) for i in (0, 1, 3, 2) for j in (0, 1, 3, 2)]
    early = [ij for ij in grid if 2 not in ij]
    late = [ij for ij in grid if 2 in ij]
    sides = (a_own, b_own, a_away, b_away)
    uvqk = uvqk_call(spot, events, *sides, early)
    uvqk = uvqk_call(spot, events, *sides, late, uvqk).reshape(4, HEADS, count, DH)
    gate_u = uvqk[0].transpose(1, 0, 2).reshape(count, width)
    vals, query, keys = uvqk[1], uvqk[2], uvqk[3]
    place = jnp.arange(count, dtype=jnp.int32)
    ends = jnp.cumsum(lengths[0])
    seqid = jnp.sum((place[:, None] >= ends[None, :]).astype(jnp.int32), axis=1)
    allowed = (seqid[:, None] == seqid[None, :]) & (place[:, None] >= place[None, :])
    scores_att = jnp.einsum(
        "hid,hjd->hij", query, keys, preferred_element_type=jnp.float32
    ) / jnp.sqrt(jnp.float32(DH))
    probs = jnp.where(allowed[None], jax.nn.silu(scores_att) / seq_max, 0.0).astype(jnp.bfloat16)
    attn = jnp.einsum("hij,hjd->ihd", probs, vals, preferred_element_type=jnp.float32).reshape(
        count, width
    )
    mean = jnp.mean(attn, axis=1, keepdims=True)
    var = jnp.mean((attn - mean) ** 2, axis=1, keepdims=True)
    mixed = ((attn - mean) * lax.rsqrt(var + 1e-05) * gate_u.astype(jnp.float32)).astype(
        jnp.bfloat16
    )
    summed = jnp.dot(
        mixed, lax.all_gather(w_out, dp, axis=0, tiled=True), preferred_element_type=jnp.float32
    )
    outputs = (events.astype(jnp.float32) + summed).astype(jnp.bfloat16)
    scores = jnp.dot(outputs, targets.T, preferred_element_type=jnp.float32)
    diag = place[:, None] == place[None, :]
    other = item_ids[:, None] != item_ids[None, :]
    coef = jnp.where(
        diag, -jax.nn.sigmoid(-scores), jnp.where(other, jax.nn.sigmoid(scores) / count, 0.0)
    ).astype(jnp.bfloat16)
    grad_out = jnp.dot(coef, targets, preferred_element_type=jnp.float32).astype(jnp.bfloat16)
    member = (seqid[:, None] == jnp.arange(seq_weights.shape[0], dtype=jnp.int32)[None, :]).astype(
        jnp.float32
    )
    weight_row = jnp.sum(member * seq_weights[None, :], axis=1) * (1.0 - flag)
    scaled = (grad_out.astype(jnp.float32) * weight_row[:, None]).astype(jnp.bfloat16)
    unif_rows = grad_out * uniform_flags[:, None].astype(jnp.bfloat16)
    contract = (((0,), (0,)), ((), ()))
    local_unif = lax.dot_general(mixed, unif_rows, contract, preferred_element_type=jnp.float32)
    half_unif = split_core(local_unif.astype(jnp.bfloat16).reshape(2, 512, -1))
    unif_rows_sum = scatter_chips(half_unif).astype(jnp.bfloat16)
    unif_mine = gather_chips(unif_rows_sum)
    unif_away = lax.ppermute(unif_mine, "c", SWAP)
    mixed_mine = lax.dynamic_slice_in_dim(mixed, core * 512, 512, 1)
    mixed_away = lax.dynamic_slice_in_dim(mixed, (1 - core) * 512, 512, 1)
    proj_mine = jnp.dot(grad_out, unif_mine.T, preferred_element_type=jnp.float32)
    proj_away = jnp.dot(grad_out, unif_away.T, preferred_element_type=jnp.float32)
    per_row = jnp.sum(mixed_mine.astype(jnp.float32) * proj_mine, axis=1) + jnp.sum(
        mixed_away.astype(jnp.float32) * proj_away, axis=1
    )
    per_row = -per_row * (1.0 - flag) / n_unif
    hyper = jnp.sum(member * per_row[:, None], axis=0)
    local_w = lax.dot_general(mixed, scaled, contract, preferred_element_type=jnp.float32)
    parts_w = local_w.astype(jnp.bfloat16).reshape(32, 2, 16, -1).transpose(1, 0, 2, 3)
    half_w = split_core(parts_w.reshape(2, 512, -1))
    weighted_grad = scatter_chips(half_w) / n_train
    return (hyper, weighted_grad)


def solution(mesh):
    fine = Mesh(mesh.devices.reshape(4, 2, 4, 2, 2), AXES)
    dp = ("y", "zh", "x", "c")
    return jax.shard_map(
        on_device,
        mesh=fine,
        in_specs=(
            P(AXES, None),
            P(None, dp),
            P(dp, None),
            P(AXES, None),
            P(AXES),
            P(AXES),
            P(AXES, None),
            P(AXES),
        ),
        out_specs=(P(AXES), P(AXES, None)),
        check_vma=False,
    )
```

```python
import jax
import jax.numpy as jnp
from jax import lax
from jax.experimental import pallas as pl
from jax.experimental.pallas import tpu as pltpu
from jax.sharding import Mesh
from jax.sharding import PartitionSpec as P

HEADS = 8
DH = 128
AXES = ("y", "zh", "x", "c", "zl")
CHIPS = ("y", "zh", "x", "zl")
SWAP = [(0, 1), (1, 0)]
ACROSS = [(0, 3), (3, 0), (1, 2), (2, 1)]
F32 = jnp.float32
BF16 = jnp.bfloat16
MIB = 1024 * 1024
NT = (((1,), (1,)), ((), ()))
NN = (((1,), (0,)), ((), ()))


def hop(array, axis, step):
    return lax.ppermute(array, axis, [(i, (i + step) % 4) for i in range(4)])


def two_rings(a, a_axis, b, b_axis, cut):
    got = lax.optimization_barrier(
        (hop(a, a_axis, 1), hop(a, a_axis, -1), hop(b, b_axis, 1), hop(b, b_axis, -1))
    )
    a_below, a_above, b_below, b_above = got
    far = (
        hop(a_below[:cut], a_axis, 1),
        hop(a_above[cut:], a_axis, -1),
        hop(b_below[:cut], b_axis, 1),
        hop(b_above[cut:], b_axis, -1),
    )
    return (a, a_above, far[:2], a_below), (b, b_above, far[2:], b_below)


def gather_proj(w_uvqk):
    half = w_uvqk.shape[0] // 2
    rows = w_uvqk.T
    other = lax.ppermute(rows, ("zh", "zl"), ACROSS)
    both = jnp.stack([rows, other])
    a_line, b_line = two_rings(both[:, :, :half], "x", both[:, :, half:], "y", 1)

    def line(pieces):
        own, above, far, below = pieces
        return jnp.stack([own, above, jnp.concatenate(far, 0), below])

    return two_rings(line(a_line), "y", line(b_line), "x", 2)


def place_of(pieces, major, minor):
    flat = [pieces[0], pieces[1], pieces[2][0], pieces[2][1], pieces[3]]
    if major == 2:
        return flat[2 + minor // 2], minor % 2
    return flat[(0, 1, 2, 4)[major]], minor


def uvqk_call(place, own, away, a_pieces, b_pieces, offsets, onto=None):
    count, model = own.shape
    half = model // 2
    arrays, steps = [], []

    def seat(array):
        for i, seen in enumerate(arrays):
            if seen is array:
                return i
        arrays.append(array)
        return len(arrays) - 1

    for y_off, x_off in offsets:
        a_from, a_at = place_of(a_pieces, y_off, x_off)
        b_from, b_at = place_of(b_pieces, x_off, y_off)
        steps.append((y_off, x_off, (seat(a_from), a_at), (seat(b_from), b_at)))
    near = len(arrays)
    extra = [] if onto is None else list(onto)

    def kernel(place_ref, own_ref, away_ref, *refs):
        weights, tail = refs[:near], refs[near + len(extra) :]
        out_own, out_away, w_buf, o_buf, w_sem, o_sem = tail
        loads = []
        for n, (_, _, a, b) in enumerate(steps):
            for side, (src, index) in enumerate((a, b)):
                for z_off in range(2):
                    z_at = place_ref[1] if z_off == 0 else 1 - place_ref[1]
                    c = pltpu.make_async_copy(
                        weights[src].at[index, z_off],
                        w_buf.at[n, z_at, :, side * half : (side + 1) * half],
                        w_sem.at[n, side, z_off],
                    )
                    c.start()
                    loads.append(c)
        stores = []
        for first in range(0, len(steps), 2):
            group = range(first, min(first + 2, len(steps)))
            for n in group:
                for c in loads[4 * n : 4 * n + 4]:
                    c.wait()
            rows = w_buf[first : first + len(group)].reshape(len(group) * 128, model)
            for who, (ev_ref, out_ref) in enumerate(((own_ref, out_own), (away_ref, out_away))):
                acc = lax.dot_general(ev_ref[...], rows, NT, preferred_element_type=F32)
                act = (0.5 * acc * (1.0 + jnp.tanh(0.5 * acc))).astype(BF16)
                for i, n in enumerate(group):
                    o_buf[n, who] = act[:, i * 128 : (i + 1) * 128]
                    y_at = lax.rem(place_ref[0] + steps[n][0], 4)
                    x_at = lax.rem(place_ref[2] + steps[n][1], 4)
                    c = pltpu.make_async_copy(
                        o_buf.at[n, who], out_ref.at[y_at, x_at], o_sem.at[n, who]
                    )
                    c.start()
                    stores.append(c)
        for c in stores:
            c.wait()

    any_spec = pl.BlockSpec(memory_space=pl.ANY)
    vmem = pl.BlockSpec(memory_space=pltpu.VMEM)
    shape = jax.ShapeDtypeStruct((4, 4, count, 128), BF16)
    return pl.pallas_call(
        kernel,
        out_shape=(shape, shape),
        in_specs=[pl.BlockSpec(memory_space=pltpu.SMEM), vmem, vmem]
        + [any_spec] * (near + len(extra)),
        out_specs=(any_spec, any_spec),
        scratch_shapes=[
            pltpu.VMEM((len(steps), 2, 64, model), BF16),
            pltpu.VMEM((len(steps), 2, count, 128), BF16),
            pltpu.SemaphoreType.DMA((len(steps), 2, 2)),
            pltpu.SemaphoreType.DMA((len(steps), 2)),
        ],
        input_output_aliases={} if onto is None else {3 + near: 0, 4 + near: 1},
        cost_estimate=pl.CostEstimate(
            flops=4 * count * model * 128 * len(steps),
            bytes_accessed=model * 256 * len(steps),
            transcendentals=2 * count * 128 * len(steps),
        ),
        compiler_params=pltpu.CompilerParams(vmem_limit_bytes=40 * MIB),
    )(place, own, away, *arrays, *extra)


def silu(x):
    return 0.5 * x * (1.0 + jnp.tanh(0.5 * x))


def sigmoid(x):
    return 1.0 / (1.0 + jnp.exp(-x))


def block_kernel(
    place, own, par, events, targets, w_out, col, row, mixed_ref, grad_ref, keep_ref, send_ref,
    w_buf, attn, mixed_t, outs, parts, w_sem, p_sem
):
    core = place[3]
    count = events.shape[0]
    model = events.shape[1]
    tile = count // 4
    loads = []
    for cls in range(2):
        for x in range(4):
            for zh in range(2):
                c = pltpu.make_async_copy(
                    w_out.at[zh * 512 + x * 128 + cls * 64 : zh * 512 + x * 128 + cls * 64 + 64],
                    w_buf.at[cls * 512 + x * 128 + zh * 64 : cls * 512 + x * 128 + zh * 64 + 64],
                    w_sem.at[cls, x, zh],
                )
                c.start()
                loads.append(c)
    lane = lax.broadcasted_iota(jnp.int32, (tile, 256), 1)
    low = lax.rem(lane, 128) < 64
    scale = 1.0 / DH**0.5
    for i in range(4):
        lo, hi = max(0, (i - 1) * tile), (i + 1) * tile
        here = slice(i * tile, hi)
        at_i = i * tile + lax.broadcasted_iota(jnp.int32, (tile, hi - lo), 0)
        at_j = lo + lax.broadcasted_iota(jnp.int32, (tile, hi - lo), 1)
        allowed = (col[here, 0:1] == row[0:1, lo:hi]) & (at_j <= at_i)
        for x in range(4):
            q = jnp.concatenate([own[2, x, here], par[2, x, here]], 1)
            k = jnp.concatenate([own[3, x, lo:hi], par[3, x, lo:hi]], 1)
            v = jnp.concatenate([own[1, x, lo:hi], par[1, x, lo:hi]], 1)
            halves = []
            for pick in (low, ~low):
                qz = jnp.where(pick, q, jnp.zeros_like(q))
                s = lax.dot_general(qz, k, NT, preferred_element_type=F32) * scale
                p = jnp.where(allowed, silu(s) * (1.0 / 128.0), 0.0).astype(BF16)
                halves.append(lax.dot_general(p, v, NN, preferred_element_type=F32))
            o = jnp.where(low, halves[0], halves[1])
            attn[here, x * 128 : (x + 1) * 128] = o[:, :128]
            attn[here, 512 + x * 128 : 512 + (x + 1) * 128] = o[:, 128:]
        a = attn[here, :]
        mean = jnp.mean(a, axis=1, keepdims=True)
        a = a - mean
        a = a * lax.rsqrt(jnp.mean(a * a, axis=1, keepdims=True) + 1e-05)
        for side, src in ((core, own), (1 - core, par)):
            base = 0 if src is own else 512
            u = jnp.concatenate([src[0, x, here] for x in range(4)], 1).astype(F32)
            m = (a[:, base : base + 512] * u).astype(BF16)
            mixed_ref[here, pl.ds(pl.multiple_of(side * 512, 512), 512)] = m
    for c in loads:
        c.wait()
    for n in range(0, model, 512):
        cols = slice(n, n + 512)
        s = jnp.dot(mixed_ref[...], w_buf[:, cols], preferred_element_type=F32)
        outs[:, cols] = (events[:, cols].astype(F32) + s).astype(BF16)
    mixed_t[...] = mixed_ref[...].T
    scores = lax.dot_general(outs[...], targets[...], NT, preferred_element_type=F32)
    at_i = lax.broadcasted_iota(jnp.int32, (count, count), 0)
    at_j = lax.broadcasted_iota(jnp.int32, (count, count), 1)
    other = col[:, 1:2] != row[1:2, :]
    coef = jnp.where(
        at_i == at_j, -sigmoid(-scores), jnp.where(other, sigmoid(scores) * (1.0 / count), 0.0)
    ).astype(BF16)
    stores = [None, None]
    for turn, n in enumerate(range(0, model, 512)):
        cols = slice(n, n + 512)
        slot = turn % 2
        g = jnp.dot(coef, targets[:, cols], preferred_element_type=F32).astype(BF16)
        grad_ref[:, cols] = g
        unif = (g.astype(F32) * col[:, 2:3]).astype(BF16)
        scaled = (g.astype(F32) * col[:, 3:4]).astype(BF16)
        g_u = jnp.dot(mixed_t[...], unif, preferred_element_type=F32)
        g_w = jnp.dot(mixed_t[...], scaled, preferred_element_type=F32)
        if stores[slot] is not None:
            for c in stores[slot]:
                c.wait()
        for to in range(2):
            for q in range(64):
                u_at = to * 512 + q * 8
                r = (q // 2) * 32 + to * 16 + (q % 2) * 8
                w_at = (r // 64 % 2) * 512 + (r // 128 % 4) * 128 + (r // 512) * 64 + r % 64
                both = jnp.concatenate([g_u[u_at : u_at + 8], g_w[w_at : w_at + 8]], 0)
                parts[slot, to, q] = both.astype(BF16)
        stores[slot] = []
        for which, (ref, side) in enumerate(((keep_ref, core), (send_ref, 1 - core))):
            c = pltpu.make_async_copy(
                parts.at[slot, side], ref.at[:, :, cols], p_sem.at[slot, which]
            )
            c.start()
            stores[slot].append(c)
    for pending in stores:
        for c in pending:
            c.wait()


def block_call(place, own, par, events, targets, w_out, col, row):
    count, model = events.shape
    width = w_out.shape[0]
    any_spec = pl.BlockSpec(memory_space=pl.ANY)
    vmem = pl.BlockSpec(memory_space=pltpu.VMEM)
    part = jax.ShapeDtypeStruct((64, 16, model), BF16)
    return pl.pallas_call(
        block_kernel,
        out_shape=(
            jax.ShapeDtypeStruct((count, width), BF16),
            jax.ShapeDtypeStruct((count, model), BF16),
            part,
            part,
        ),
        in_specs=[pl.BlockSpec(memory_space=pltpu.SMEM)] + [vmem] * 4 + [any_spec, vmem, vmem],
        out_specs=(vmem, vmem, any_spec, any_spec),
        scratch_shapes=[
            pltpu.VMEM((width, model), BF16),
            pltpu.VMEM((count, width), F32),
            pltpu.VMEM((width, count), BF16),
            pltpu.VMEM((count, model), BF16),
            pltpu.VMEM((2, 2, 64, 16, 512), BF16),
            pltpu.SemaphoreType.DMA((2, 4, 2)),
            pltpu.SemaphoreType.DMA((2, 2)),
        ],
        cost_estimate=pl.CostEstimate(
            flops=10 * 1024 * MIB, bytes_accessed=24 * MIB, transcendentals=2 * MIB
        ),
        compiler_params=pltpu.CompilerParams(vmem_limit_bytes=56 * MIB),
    )(place, own, par, events, targets, w_out, col, row)


def on_device(events, w_uvqk, w_out, targets, item_ids, uniform_flags, lengths, seq_weights):
    count = events.shape[0]
    core = lax.axis_index("c")
    flag = uniform_flags.astype(F32)
    counts = lax.all_to_all(jnp.broadcast_to(jnp.sum(flag), (128, 128)), AXES, 0, 0, tiled=True)
    n_unif = jnp.sum(counts[:, 0])
    spot = jnp.stack([lax.axis_index(n) for n in ("y", "zh", "x", "c")]).astype(jnp.int32)
    w_out_all = lax.all_gather(w_out, ("y", "zh", "x", "c"), axis=0, tiled=True)
    place = jnp.arange(count, dtype=jnp.int32)
    ends = jnp.cumsum(lengths[0])
    seqid = jnp.sum((place[:, None] >= ends[None, :]).astype(jnp.int32), axis=1)
    member = (seqid[:, None] == jnp.arange(seq_weights.shape[0], dtype=jnp.int32)[None, :]).astype(
        F32
    )
    weight_row = jnp.sum(member * seq_weights[None, :], axis=1) * (1.0 - flag)
    facts = [seqid.astype(F32), item_ids.astype(F32), flag, weight_row]
    row = jnp.stack(facts + [jnp.zeros_like(flag)] * 4)
    col = row.T

    away = lax.ppermute(events, "c", SWAP)
    a_pieces, b_pieces = gather_proj(w_uvqk)
    spot, n_unif = lax.optimization_barrier((spot, n_unif))
    grid = [(i, j) for i in (0, 1, 3, 2) for j in (0, 1, 3, 2)]
    early = [ij for ij in grid if 2 not in ij]
    late = [ij for ij in grid if 2 in ij]
    part = uvqk_call(spot, events, away, a_pieces, b_pieces, early)
    own, for_away = uvqk_call(spot, events, away, a_pieces, b_pieces, late, part)
    par = lax.ppermute(for_away, "c", SWAP)
    mixed, grad_out, keep, send = block_call(
        spot, own, par, events, targets, w_out_all, col, row
    )

    came = lax.ppermute(send, "c", SWAP)
    chip = (keep.astype(F32) + came.astype(F32)).astype(BF16)
    got = lax.all_to_all(chip, CHIPS, 0, 0, tiled=True)
    total = jnp.sum(got.astype(F32), axis=0)
    weighted_grad = total[8:] / (jnp.float32(count * 128) - n_unif)
    unif = jnp.broadcast_to(total[:8].astype(BF16)[None], (64, 8, total.shape[1]))
    unif_mine = lax.all_to_all(unif, CHIPS, 0, 0, tiled=True).reshape(512, -1)
    unif_away = lax.ppermute(unif_mine, "c", SWAP)
    mixed_mine = lax.dynamic_slice_in_dim(mixed, core * 512, 512, 1)
    mixed_away = lax.dynamic_slice_in_dim(mixed, (1 - core) * 512, 512, 1)
    proj_mine = jnp.dot(grad_out, unif_mine.T, preferred_element_type=F32)
    proj_away = jnp.dot(grad_out, unif_away.T, preferred_element_type=F32)
    per_row = jnp.sum(mixed_mine.astype(F32) * proj_mine, axis=1) + jnp.sum(
        mixed_away.astype(F32) * proj_away, axis=1
    )
    per_row = -per_row * (1.0 - flag) / n_unif
    hyper = jnp.sum(member * per_row[:, None], axis=0)
    return (hyper, weighted_grad)


def solution(mesh):
    fine = Mesh(mesh.devices.reshape(4, 2, 4, 2, 2), AXES)
    dp = ("y", "zh", "x", "c")
    return jax.shard_map(
        on_device,
        mesh=fine,
        in_specs=(
            P(AXES, None),
            P(None, dp),
            P(dp, None),
            P(AXES, None),
            P(AXES),
            P(AXES),
            P(AXES, None),
            P(AXES),
        ),
        out_specs=(P(AXES), P(AXES, None)),
        check_vma=False,
    )
```

```python
import jax
import jax.numpy as jnp
from jax import lax
from jax.experimental import pallas as pl
from jax.experimental.pallas import tpu as pltpu
from jax.sharding import Mesh
from jax.sharding import PartitionSpec as P

HEADS = 8
DH = 128
AXES = ("y", "zh", "x", "c", "zl")
CHIPS = ("y", "zh", "x", "zl")
SWAP = [(0, 1), (1, 0)]
ACROSS = [(0, 3), (3, 0), (1, 2), (2, 1)]
F32 = jnp.float32
BF16 = jnp.bfloat16
MIB = 1024 * 1024
NT = (((1,), (1,)), ((), ()))
NN = (((1,), (0,)), ((), ()))


def hop(array, axis, step):
    return lax.ppermute(array, axis, [(i, (i + step) % 4) for i in range(4)])


def two_rings(a, a_axis, b, b_axis):
    got = lax.optimization_barrier(
        tuple(hop(v[0], axis, 1) for v, axis in ((a, a_axis), (b, b_axis)))
        + tuple(hop(v[1], axis, -1) for v, axis in ((a, a_axis), (b, b_axis)))
        + tuple(hop(v[1], axis, 1) for v, axis in ((a, a_axis), (b, b_axis)))
        + tuple(hop(v[0], axis, -1) for v, axis in ((a, a_axis), (b, b_axis)))
    )
    a_far = (hop(got[0], a_axis, 1), hop(got[2], a_axis, -1))
    b_far = (hop(got[1], b_axis, 1), hop(got[3], b_axis, -1))
    return (a, (got[6], got[2]), a_far, (got[0], got[4])), (b, (got[7], got[3]), b_far, (got[1], got[5]))


def first_rings(a, a_axis, b, b_axis, cut):
    got = lax.optimization_barrier(
        (hop(a, a_axis, 1), hop(a, a_axis, -1), hop(b, b_axis, 1), hop(b, b_axis, -1))
    )
    a_below, a_above, b_below, b_above = got
    far = (
        hop(a_below[:cut], a_axis, 1),
        hop(a_above[cut:], a_axis, -1),
        hop(b_below[:cut], b_axis, 1),
        hop(b_above[cut:], b_axis, -1),
    )
    return (a, a_above, far[:2], a_below), (b, b_above, far[2:], b_below)


def gather_proj(w_uvqk):
    half = w_uvqk.shape[0] // 2
    rows = w_uvqk.T
    other = lax.ppermute(rows, ("zh", "zl"), ACROSS)
    both = jnp.stack([rows, other])
    a_line, b_line = first_rings(both[:, :, :half], "x", both[:, :, half:], "y", 1)

    def halves(pieces):
        own, above, far, below = pieces
        return jnp.stack([own, above]), jnp.stack([jnp.concatenate(far, 0), below])

    return two_rings(halves(a_line), "y", halves(b_line), "x")


def place_of(pieces, major, minor):
    return pieces[major][minor // 2], minor % 2


def uvqk_call(place, own, away, a_pieces, b_pieces, offsets, onto=None):
    count, model = own.shape
    half = model // 2
    arrays, steps = [], []

    def seat(array):
        for i, seen in enumerate(arrays):
            if seen is array:
                return i
        arrays.append(array)
        return len(arrays) - 1

    for y_off, x_off in offsets:
        a_from, a_at = place_of(a_pieces, y_off, x_off)
        b_from, b_at = place_of(b_pieces, x_off, y_off)
        steps.append((y_off, x_off, (seat(a_from), a_at), (seat(b_from), b_at)))
    near = len(arrays)
    extra = [] if onto is None else list(onto)

    def kernel(place_ref, own_ref, away_ref, *refs):
        weights, tail = refs[:near], refs[near + len(extra) :]
        out_own, out_away, w_buf, o_buf, w_sem, o_sem = tail
        loads = []
        for n, (_, _, a, b) in enumerate(steps):
            for side, (src, index) in enumerate((a, b)):
                for z_off in range(2):
                    z_at = place_ref[1] if z_off == 0 else 1 - place_ref[1]
                    c = pltpu.make_async_copy(
                        weights[src].at[index, z_off],
                        w_buf.at[n, z_at, :, side * half : (side + 1) * half],
                        w_sem.at[n, side, z_off],
                    )
                    c.start()
                    loads.append(c)
        stores = []
        for first in range(0, len(steps), 2):
            group = range(first, min(first + 2, len(steps)))
            for n in group:
                for c in loads[4 * n : 4 * n + 4]:
                    c.wait()
            rows = w_buf[first : first + len(group)].reshape(len(group) * 128, model)
            for who, (ev_ref, out_ref) in enumerate(((own_ref, out_own), (away_ref, out_away))):
                acc = lax.dot_general(ev_ref[...], rows, NT, preferred_element_type=F32)
                act = (0.5 * acc * (1.0 + jnp.tanh(0.5 * acc))).astype(BF16)
                for i, n in enumerate(group):
                    o_buf[n, who] = act[:, i * 128 : (i + 1) * 128]
                    y_at = lax.rem(place_ref[0] + steps[n][0], 4)
                    x_at = lax.rem(place_ref[2] + steps[n][1], 4)
                    c = pltpu.make_async_copy(
                        o_buf.at[n, who], out_ref.at[y_at, x_at], o_sem.at[n, who]
                    )
                    c.start()
                    stores.append(c)
        for c in stores:
            c.wait()

    any_spec = pl.BlockSpec(memory_space=pl.ANY)
    vmem = pl.BlockSpec(memory_space=pltpu.VMEM)
    shape = jax.ShapeDtypeStruct((4, 4, count, 128), BF16)
    return pl.pallas_call(
        kernel,
        out_shape=(shape, shape),
        in_specs=[pl.BlockSpec(memory_space=pltpu.SMEM), vmem, vmem]
        + [any_spec] * (near + len(extra)),
        out_specs=(any_spec, any_spec),
        scratch_shapes=[
            pltpu.VMEM((len(steps), 2, 64, model), BF16),
            pltpu.VMEM((len(steps), 2, count, 128), BF16),
            pltpu.SemaphoreType.DMA((len(steps), 2, 2)),
            pltpu.SemaphoreType.DMA((len(steps), 2)),
        ],
        input_output_aliases={} if onto is None else {3 + near: 0, 4 + near: 1},
        cost_estimate=pl.CostEstimate(
            flops=4 * count * model * 128 * len(steps),
            bytes_accessed=model * 256 * len(steps),
            transcendentals=2 * count * 128 * len(steps),
        ),
        compiler_params=pltpu.CompilerParams(vmem_limit_bytes=60 * MIB),
    )(place, own, away, *arrays, *extra)


def silu(x):
    return 0.5 * x * (1.0 + jnp.tanh(0.5 * x))


def sigmoid(x):
    return 1.0 / (1.0 + jnp.exp(-x))


def block_kernel(
    place, own, par, events, targets, w_out, col, row, mixed_ref, grad_ref, keep_ref, send_ref,
    w_buf, attn, mixed_t, outs, parts, w_sem, p_sem
):
    core = place[3]
    count = events.shape[0]
    model = events.shape[1]
    tile = count // 4
    loads = []
    for cls in range(2):
        for x in range(4):
            for zh in range(2):
                c = pltpu.make_async_copy(
                    w_out.at[zh * 512 + x * 128 + cls * 64 : zh * 512 + x * 128 + cls * 64 + 64],
                    w_buf.at[cls * 512 + x * 128 + zh * 64 : cls * 512 + x * 128 + zh * 64 + 64],
                    w_sem.at[cls, x, zh],
                )
                c.start()
                loads.append(c)
    lane = lax.broadcasted_iota(jnp.int32, (tile, 256), 1)
    low = lax.rem(lane, 128) < 64
    scale = 1.0 / DH**0.5
    for i in range(4):
        lo, hi = max(0, (i - 1) * tile), (i + 1) * tile
        here = slice(i * tile, hi)
        at_i = i * tile + lax.broadcasted_iota(jnp.int32, (tile, hi - lo), 0)
        at_j = lo + lax.broadcasted_iota(jnp.int32, (tile, hi - lo), 1)
        allowed = (col[here, 0:1] == row[0:1, lo:hi]) & (at_j <= at_i)
        for x in range(4):
            q = jnp.concatenate([own[2, x, here], par[2, x, here]], 1)
            k = jnp.concatenate([own[3, x, lo:hi], par[3, x, lo:hi]], 1)
            v = jnp.concatenate([own[1, x, lo:hi], par[1, x, lo:hi]], 1)
            halves = []
            for pick in (low, ~low):
                qz = jnp.where(pick, q, jnp.zeros_like(q))
                s = lax.dot_general(qz, k, NT, preferred_element_type=F32) * scale
                p = jnp.where(allowed, silu(s) * (1.0 / 128.0), 0.0).astype(BF16)
                halves.append(lax.dot_general(p, v, NN, preferred_element_type=F32))
            o = jnp.where(low, halves[0], halves[1])
            attn[here, x * 128 : (x + 1) * 128] = o[:, :128]
            attn[here, 512 + x * 128 : 512 + (x + 1) * 128] = o[:, 128:]
        a = attn[here, :]
        mean = jnp.mean(a, axis=1, keepdims=True)
        a = a - mean
        a = a * lax.rsqrt(jnp.mean(a * a, axis=1, keepdims=True) + 1e-05)
        for side, src in ((core, own), (1 - core, par)):
            base = 0 if src is own else 512
            u = jnp.concatenate([src[0, x, here] for x in range(4)], 1).astype(F32)
            m = (a[:, base : base + 512] * u).astype(BF16)
            mixed_ref[here, pl.ds(pl.multiple_of(side * 512, 512), 512)] = m
    for c in loads:
        c.wait()
    for n in range(0, model, 512):
        cols = slice(n, n + 512)
        s = jnp.dot(mixed_ref[...], w_buf[:, cols], preferred_element_type=F32)
        outs[:, cols] = (events[:, cols].astype(F32) + s).astype(BF16)
    mixed_t[...] = mixed_ref[...].T
    scores = lax.dot_general(outs[...], targets[...], NT, preferred_element_type=F32)
    at_i = lax.broadcasted_iota(jnp.int32, (count, count), 0)
    at_j = lax.broadcasted_iota(jnp.int32, (count, count), 1)
    other = col[:, 1:2] != row[1:2, :]
    coef = jnp.where(
        at_i == at_j, -sigmoid(-scores), jnp.where(other, sigmoid(scores) * (1.0 / count), 0.0)
    ).astype(BF16)
    stores = [None, None]
    for turn, n in enumerate(range(0, model, 512)):
        cols = slice(n, n + 512)
        slot = turn % 2
        g = jnp.dot(coef, targets[:, cols], preferred_element_type=F32).astype(BF16)
        grad_ref[:, cols] = g
        unif = (g.astype(F32) * col[:, 2:3]).astype(BF16)
        scaled = (g.astype(F32) * col[:, 3:4]).astype(BF16)
        g_u = jnp.dot(mixed_t[...], unif, preferred_element_type=F32)
        g_w = jnp.dot(mixed_t[...], scaled, preferred_element_type=F32)
        if stores[slot] is not None:
            for c in stores[slot]:
                c.wait()
        for to in range(2):
            for q in range(64):
                u_at = to * 512 + q * 8
                r = (q // 2) * 32 + to * 16 + (q % 2) * 8
                w_at = (r // 64 % 2) * 512 + (r // 128 % 4) * 128 + (r // 512) * 64 + r % 64
                both = jnp.concatenate([g_u[u_at : u_at + 8], g_w[w_at : w_at + 8]], 0)
                parts[slot, to, q] = both.astype(BF16)
        stores[slot] = []
        for which, (ref, side) in enumerate(((keep_ref, core), (send_ref, 1 - core))):
            c = pltpu.make_async_copy(
                parts.at[slot, side], ref.at[:, :, cols], p_sem.at[slot, which]
            )
            c.start()
            stores[slot].append(c)
    for pending in stores:
        for c in pending:
            c.wait()


def block_call(place, own, par, events, targets, w_out, col, row):
    count, model = events.shape
    width = w_out.shape[0]
    any_spec = pl.BlockSpec(memory_space=pl.ANY)
    vmem = pl.BlockSpec(memory_space=pltpu.VMEM)
    part = jax.ShapeDtypeStruct((64, 16, model), BF16)
    return pl.pallas_call(
        block_kernel,
        out_shape=(
            jax.ShapeDtypeStruct((count, width), BF16),
            jax.ShapeDtypeStruct((count, model), BF16),
            part,
            part,
        ),
        in_specs=[pl.BlockSpec(memory_space=pltpu.SMEM)] + [vmem] * 4 + [any_spec, vmem, vmem],
        out_specs=(vmem, vmem, any_spec, any_spec),
        scratch_shapes=[
            pltpu.VMEM((width, model), BF16),
            pltpu.VMEM((count, width), F32),
            pltpu.VMEM((width, count), BF16),
            pltpu.VMEM((count, model), BF16),
            pltpu.VMEM((2, 2, 64, 16, 512), BF16),
            pltpu.SemaphoreType.DMA((2, 4, 2)),
            pltpu.SemaphoreType.DMA((2, 2)),
        ],
        cost_estimate=pl.CostEstimate(
            flops=10 * 1024 * MIB, bytes_accessed=24 * MIB, transcendentals=2 * MIB
        ),
        compiler_params=pltpu.CompilerParams(vmem_limit_bytes=60 * MIB),
    )(place, own, par, events, targets, w_out, col, row)


def on_device(events, w_uvqk, w_out, targets, item_ids, uniform_flags, lengths, seq_weights):
    count = events.shape[0]
    core = lax.axis_index("c")
    flag = uniform_flags.astype(F32)
    counts = lax.all_to_all(jnp.broadcast_to(jnp.sum(flag), (128, 128)), AXES, 0, 0, tiled=True)
    n_unif = jnp.sum(counts[:, 0])
    spot = jnp.stack([lax.axis_index(n) for n in ("y", "zh", "x", "c")]).astype(jnp.int32)
    w_out_all = lax.all_gather(w_out, ("y", "zh", "x", "c"), axis=0, tiled=True)
    place = jnp.arange(count, dtype=jnp.int32)
    ends = jnp.cumsum(lengths[0])
    seqid = jnp.sum((place[:, None] >= ends[None, :]).astype(jnp.int32), axis=1)
    member = (seqid[:, None] == jnp.arange(seq_weights.shape[0], dtype=jnp.int32)[None, :]).astype(
        F32
    )
    weight_row = jnp.sum(member * seq_weights[None, :], axis=1) * (1.0 - flag)
    facts = [seqid.astype(F32), item_ids.astype(F32), flag, weight_row]
    row = jnp.stack(facts + [jnp.zeros_like(flag)] * 4)
    col = row.T

    away = lax.ppermute(events, "c", SWAP)
    a_pieces, b_pieces = gather_proj(w_uvqk)
    spot, n_unif = lax.optimization_barrier((spot, n_unif))
    grid = [(i, j) for i in (0, 1, 3, 2) for j in (0, 1, 3, 2)]
    early = [ij for ij in grid if 2 not in ij]
    late = [ij for ij in grid if 2 in ij]
    part = uvqk_call(spot, events, away, a_pieces, b_pieces, early)
    own, for_away = uvqk_call(spot, events, away, a_pieces, b_pieces, late, part)
    par = lax.ppermute(for_away, "c", SWAP)
    mixed, grad_out, keep, send = block_call(
        spot, own, par, events, targets, w_out_all, col, row
    )

    came = lax.ppermute(send, "c", SWAP)
    chip = (keep.astype(F32) + came.astype(F32)).astype(BF16)
    got = lax.all_to_all(chip, CHIPS, 0, 0, tiled=True)
    total = jnp.sum(got.astype(F32), axis=0)
    weighted_grad = total[8:] / (jnp.float32(count * 128) - n_unif)
    unif = jnp.broadcast_to(total[:8].astype(BF16)[None], (64, 8, total.shape[1]))
    unif_mine = lax.all_to_all(unif, CHIPS, 0, 0, tiled=True).reshape(512, -1)
    unif_away = lax.ppermute(unif_mine, "c", SWAP)
    mixed_mine = lax.dynamic_slice_in_dim(mixed, core * 512, 512, 1)
    mixed_away = lax.dynamic_slice_in_dim(mixed, (1 - core) * 512, 512, 1)
    proj_mine = jnp.dot(grad_out, unif_mine.T, preferred_element_type=F32)
    proj_away = jnp.dot(grad_out, unif_away.T, preferred_element_type=F32)
    per_row = jnp.sum(mixed_mine.astype(F32) * proj_mine, axis=1) + jnp.sum(
        mixed_away.astype(F32) * proj_away, axis=1
    )
    per_row = -per_row * (1.0 - flag) / n_unif
    hyper = jnp.sum(member * per_row[:, None], axis=0)
    return (hyper, weighted_grad)


def solution(mesh):
    fine = Mesh(mesh.devices.reshape(4, 2, 4, 2, 2), AXES)
    dp = ("y", "zh", "x", "c")
    return jax.shard_map(
        on_device,
        mesh=fine,
        in_specs=(
            P(AXES, None),
            P(None, dp),
            P(dp, None),
            P(AXES, None),
            P(AXES),
            P(AXES),
            P(AXES, None),
            P(AXES),
        ),
        out_specs=(P(AXES), P(AXES, None)),
        check_vma=False,
    )
```

```python
import jax
import jax.numpy as jnp
from jax import lax
from jax.experimental import pallas as pl
from jax.experimental.pallas import tpu as pltpu
from jax.sharding import Mesh
from jax.sharding import PartitionSpec as P

HEADS = 8
DH = 128
AXES = ("y", "zh", "x", "c", "zl")
CHIPS = ("y", "zh", "x", "zl")
SWAP = [(0, 1), (1, 0)]
ACROSS = [(0, 3), (3, 0), (1, 2), (2, 1)]
F32 = jnp.float32
BF16 = jnp.bfloat16
MIB = 1024 * 1024
NT = (((1,), (1,)), ((), ()))
NN = (((1,), (0,)), ((), ()))


def hop(array, axis, step):
    return lax.ppermute(array, axis, [(i, (i + step) % 4) for i in range(4)])


def two_rings(a, a_axis, b, b_axis):
    got = lax.optimization_barrier(
        tuple(hop(v[0], axis, 1) for v, axis in ((a, a_axis), (b, b_axis)))
        + tuple(hop(v[1], axis, -1) for v, axis in ((a, a_axis), (b, b_axis)))
        + tuple(hop(v[1], axis, 1) for v, axis in ((a, a_axis), (b, b_axis)))
        + tuple(hop(v[0], axis, -1) for v, axis in ((a, a_axis), (b, b_axis)))
    )
    a_far = (hop(got[0], a_axis, 1), hop(got[2], a_axis, -1))
    b_far = (hop(got[1], b_axis, 1), hop(got[3], b_axis, -1))
    return (a, (got[6], got[2]), a_far, (got[0], got[4])), (b, (got[7], got[3]), b_far, (got[1], got[5]))


def first_rings(a, a_axis, b, b_axis, cut):
    got = lax.optimization_barrier(
        (hop(a, a_axis, 1), hop(a, a_axis, -1), hop(b, b_axis, 1), hop(b, b_axis, -1))
    )
    a_below, a_above, b_below, b_above = got
    far = (
        hop(a_below[:cut], a_axis, 1),
        hop(a_above[cut:], a_axis, -1),
        hop(b_below[:cut], b_axis, 1),
        hop(b_above[cut:], b_axis, -1),
    )
    return (a, a_above, far[:2], a_below), (b, b_above, far[2:], b_below)


def gather_proj(w_uvqk):
    half = w_uvqk.shape[0] // 2
    rows = w_uvqk.T
    other = lax.ppermute(rows, ("zh", "zl"), ACROSS)
    both = jnp.stack([rows, other])
    a_line, b_line = first_rings(both[:, :, :half], "x", both[:, :, half:], "y", 1)

    def halves(pieces):
        own, above, far, below = pieces
        return jnp.stack([own, above]), jnp.stack([jnp.concatenate(far, 0), below])

    return two_rings(halves(a_line), "y", halves(b_line), "x")


def place_of(pieces, major, minor):
    return pieces[major][minor // 2], minor % 2


def uvqk_call(place, own, away, a_pieces, b_pieces, offsets, onto=None):
    count, model = own.shape
    half = model // 2
    arrays, steps = [], []

    def seat(array):
        for i, seen in enumerate(arrays):
            if seen is array:
                return i
        arrays.append(array)
        return len(arrays) - 1

    for y_off, x_off in offsets:
        a_from, a_at = place_of(a_pieces, y_off, x_off)
        b_from, b_at = place_of(b_pieces, x_off, y_off)
        steps.append((y_off, x_off, (seat(a_from), a_at), (seat(b_from), b_at)))
    near = len(arrays)
    extra = [] if onto is None else list(onto)

    def kernel(place_ref, own_ref, away_ref, *refs):
        weights, tail = refs[:near], refs[near + len(extra) :]
        out_own, out_away, w_buf, o_buf, w_sem, o_sem = tail
        loads = []
        for n, (_, _, a, b) in enumerate(steps):
            for side, (src, index) in enumerate((a, b)):
                for z_off in range(2):
                    z_at = place_ref[1] if z_off == 0 else 1 - place_ref[1]
                    c = pltpu.make_async_copy(
                        weights[src].at[index, z_off],
                        w_buf.at[n, z_at, :, side * half : (side + 1) * half],
                        w_sem.at[n, side, z_off],
                    )
                    c.start()
                    loads.append(c)
        stores = []
        for first in range(0, len(steps), 2):
            group = range(first, min(first + 2, len(steps)))
            for n in group:
                for c in loads[4 * n : 4 * n + 4]:
                    c.wait()
            rows = w_buf[first : first + len(group)].reshape(len(group) * 128, model)
            for who, (ev_ref, out_ref) in enumerate(((own_ref, out_own), (away_ref, out_away))):
                acc = lax.dot_general(ev_ref[...], rows, NT, preferred_element_type=F32)
                act = (0.5 * acc * (1.0 + jnp.tanh(0.5 * acc))).astype(BF16)
                for i, n in enumerate(group):
                    o_buf[n, who] = act[:, i * 128 : (i + 1) * 128]
                    y_at = lax.rem(place_ref[0] + steps[n][0], 4)
                    x_at = lax.rem(place_ref[2] + steps[n][1], 4)
                    c = pltpu.make_async_copy(
                        o_buf.at[n, who], out_ref.at[y_at, x_at], o_sem.at[n, who]
                    )
                    c.start()
                    stores.append(c)
        for c in stores:
            c.wait()

    any_spec = pl.BlockSpec(memory_space=pl.ANY)
    vmem = pl.BlockSpec(memory_space=pltpu.VMEM)
    shape = jax.ShapeDtypeStruct((4, 4, count, 128), BF16)
    return pl.pallas_call(
        kernel,
        out_shape=(shape, shape),
        in_specs=[pl.BlockSpec(memory_space=pltpu.SMEM), vmem, vmem]
        + [any_spec] * (near + len(extra)),
        out_specs=(any_spec, any_spec),
        scratch_shapes=[
            pltpu.VMEM((len(steps), 2, 64, model), BF16),
            pltpu.VMEM((len(steps), 2, count, 128), BF16),
            pltpu.SemaphoreType.DMA((len(steps), 2, 2)),
            pltpu.SemaphoreType.DMA((len(steps), 2)),
        ],
        input_output_aliases={} if onto is None else {3 + near: 0, 4 + near: 1},
        cost_estimate=pl.CostEstimate(
            flops=4 * count * model * 128 * len(steps),
            bytes_accessed=model * 256 * len(steps),
            transcendentals=2 * count * 128 * len(steps),
        ),
        compiler_params=pltpu.CompilerParams(vmem_limit_bytes=60 * MIB),
    )(place, own, away, *arrays, *extra)


def silu(x):
    return 0.5 * x * (1.0 + jnp.tanh(0.5 * x))


def sigmoid(x):
    return 1.0 / (1.0 + jnp.exp(-x))


def block_kernel(
    place, own, par, events_hbm, targets_hbm, w_out, col, row, mixed_ref, grad_ref, keep_u, send_u,
    keep_w, send_w, events, targets, w_buf, attn, mixed_t, outs, parts_u, parts_w, digits, w_sem,
    e_sem, p_sem, d_sem
):
    core = place[3]
    count = events.shape[0]
    model = events.shape[1]
    tile = count // 4
    loads = [
        pltpu.make_async_copy(events_hbm, events, e_sem.at[0]),
        pltpu.make_async_copy(targets_hbm, targets, e_sem.at[1]),
    ]
    for c in loads:
        c.start()
    for cls in range(2):
        for x in range(4):
            for zh in range(2):
                c = pltpu.make_async_copy(
                    w_out.at[zh * 512 + x * 128 + cls * 64 : zh * 512 + x * 128 + cls * 64 + 64],
                    w_buf.at[cls * 512 + x * 128 + zh * 64 : cls * 512 + x * 128 + zh * 64 + 64],
                    w_sem.at[cls, x, zh],
                )
                c.start()
                loads.append(c)
    lane = lax.broadcasted_iota(jnp.int32, (tile, 256), 1)
    low = lax.rem(lane, 128) < 64
    scale = 1.0 / DH**0.5
    for i in range(4):
        lo, hi = max(0, (i - 1) * tile), (i + 1) * tile
        here = slice(i * tile, hi)
        at_i = i * tile + lax.broadcasted_iota(jnp.int32, (tile, hi - lo), 0)
        at_j = lo + lax.broadcasted_iota(jnp.int32, (tile, hi - lo), 1)
        allowed = (col[here, 0:1] == row[0:1, lo:hi]) & (at_j <= at_i)
        for x in range(4):
            q = jnp.concatenate([own[2, x, here], par[2, x, here]], 1)
            k = jnp.concatenate([own[3, x, lo:hi], par[3, x, lo:hi]], 1)
            v = jnp.concatenate([own[1, x, lo:hi], par[1, x, lo:hi]], 1)
            halves = []
            for pick in (low, ~low):
                qz = jnp.where(pick, q, jnp.zeros_like(q))
                s = lax.dot_general(qz, k, NT, preferred_element_type=F32) * scale
                p = jnp.where(allowed, silu(s) * (1.0 / 128.0), 0.0).astype(BF16)
                halves.append(lax.dot_general(p, v, NN, preferred_element_type=F32))
            o = jnp.where(low, halves[0], halves[1])
            attn[here, x * 128 : (x + 1) * 128] = o[:, :128]
            attn[here, 512 + x * 128 : 512 + (x + 1) * 128] = o[:, 128:]
        a = attn[here, :]
        mean = jnp.mean(a, axis=1, keepdims=True)
        a = a - mean
        a = a * lax.rsqrt(jnp.mean(a * a, axis=1, keepdims=True) + 1e-05)
        for side, src in ((core, own), (1 - core, par)):
            base = 0 if src is own else 512
            u = jnp.concatenate([src[0, x, here] for x in range(4)], 1).astype(F32)
            m = (a[:, base : base + 512] * u).astype(BF16)
            mixed_ref[here, pl.ds(pl.multiple_of(side * 512, 512), 512)] = m
    for c in loads:
        c.wait()
    for n in range(0, model, 512):
        cols = slice(n, n + 512)
        s = jnp.dot(mixed_ref[...], w_buf[:, cols], preferred_element_type=F32)
        outs[:, cols] = (events[:, cols].astype(F32) + s).astype(BF16)
    mixed_t[...] = mixed_ref[...].T
    scores = lax.dot_general(outs[...], targets[...], NT, preferred_element_type=F32)
    at_i = lax.broadcasted_iota(jnp.int32, (count, count), 0)
    at_j = lax.broadcasted_iota(jnp.int32, (count, count), 1)
    other = col[:, 1:2] != row[1:2, :]
    coef = jnp.where(
        at_i == at_j, -sigmoid(-scores), jnp.where(other, sigmoid(scores) * (1.0 / count), 0.0)
    ).astype(BF16)
    flagged = jnp.sum(row[2:3, :], axis=1, keepdims=True)
    high = jnp.floor(flagged * (1.0 / 32.0))
    at = lax.broadcasted_iota(jnp.int32, (512, 128), 1)
    digits[...] = jnp.where(at == 0, high, jnp.where(at == 1, flagged - 32.0 * high, 0.0)).astype(BF16)
    count_copies = [
        pltpu.make_async_copy(digits, ref.at[:, model : model + 128], d_sem.at[i])
        for i, ref in enumerate((keep_u, send_u))
    ]
    for c in count_copies:
        c.start()
    stores = [None, None]
    for turn, n in enumerate(range(0, model, 512)):
        cols = slice(n, n + 512)
        slot = turn % 2
        g = jnp.dot(coef, targets[:, cols], preferred_element_type=F32).astype(BF16)
        grad_ref[:, cols] = g
        unif = (g.astype(F32) * col[:, 2:3]).astype(BF16)
        scaled = (g.astype(F32) * col[:, 3:4]).astype(BF16)
        g_u = jnp.dot(mixed_t[...], unif, preferred_element_type=F32)
        g_w = jnp.dot(mixed_t[...], scaled, preferred_element_type=F32)
        if stores[slot] is not None:
            for c in stores[slot]:
                c.wait()
        parts_u[slot] = g_u.astype(BF16).reshape(2, 512, 512)
        for to in range(2):
            for q in range(32):
                x, y, zh = q // 8, q // 2 % 4, q % 2
                r = (y * 8 + zh * 4 + x) * 32 + to * 16
                w_at = (r // 64 % 2) * 512 + (r // 128 % 4) * 128 + (r // 512) * 64 + r % 64
                parts_w[slot, to, q * 16 : q * 16 + 16] = g_w[w_at : w_at + 16].astype(BF16)
        stores[slot] = []
        for which, (ref, buf, side) in enumerate(
            (
                (keep_u, parts_u, core),
                (send_u, parts_u, 1 - core),
                (keep_w, parts_w, core),
                (send_w, parts_w, 1 - core),
            )
        ):
            c = pltpu.make_async_copy(buf.at[slot, side], ref.at[:, cols], p_sem.at[slot, which])
            c.start()
            stores[slot].append(c)
    for pending in stores:
        for c in pending:
            c.wait()
    for c in count_copies:
        c.wait()


def block_call(place, own, par, events, targets, w_out, col, row):
    count, model = events.shape
    width = w_out.shape[0]
    any_spec = pl.BlockSpec(memory_space=pl.ANY)
    vmem = pl.BlockSpec(memory_space=pltpu.VMEM)
    part_u = jax.ShapeDtypeStruct((512, model + 128), BF16)
    part_w = jax.ShapeDtypeStruct((512, model), BF16)
    return pl.pallas_call(
        block_kernel,
        out_shape=(
            jax.ShapeDtypeStruct((count, width), BF16),
            jax.ShapeDtypeStruct((count, model), BF16),
            part_u,
            part_u,
            part_w,
            part_w,
        ),
        in_specs=[pl.BlockSpec(memory_space=pltpu.SMEM)] + [vmem] * 2 + [any_spec] * 3 + [vmem] * 2,
        out_specs=(vmem, vmem) + (any_spec,) * 4,
        scratch_shapes=[
            pltpu.VMEM((count, model), BF16),
            pltpu.VMEM((count, model), BF16),
            pltpu.VMEM((width, model), BF16),
            pltpu.VMEM((count, width), F32),
            pltpu.VMEM((width, count), BF16),
            pltpu.VMEM((count, model), BF16),
            pltpu.VMEM((2, 2, 512, 512), BF16),
            pltpu.VMEM((2, 2, 512, 512), BF16),
            pltpu.VMEM((512, 128), BF16),
            pltpu.SemaphoreType.DMA((2, 4, 2)),
            pltpu.SemaphoreType.DMA((2,)),
            pltpu.SemaphoreType.DMA((2, 4)),
            pltpu.SemaphoreType.DMA((2,)),
        ],
        cost_estimate=pl.CostEstimate(
            flops=10 * 1024 * MIB, bytes_accessed=24 * MIB, transcendentals=2 * MIB
        ),
        compiler_params=pltpu.CompilerParams(vmem_limit_bytes=60 * MIB),
    )(place, own, par, events, targets, w_out, col, row)


def on_device(events, w_uvqk, w_out, targets, item_ids, uniform_flags, lengths, seq_weights):
    count = events.shape[0]
    core = lax.axis_index("c")
    flag = uniform_flags.astype(F32)
    spot = jnp.stack([lax.axis_index(n) for n in ("y", "zh", "x", "c")]).astype(jnp.int32)
    w_out_all = lax.all_gather(w_out, ("y", "zh", "x", "c"), axis=0, tiled=True)
    place = jnp.arange(count, dtype=jnp.int32)
    ends = jnp.cumsum(lengths[0])
    seqid = jnp.sum((place[:, None] >= ends[None, :]).astype(jnp.int32), axis=1)
    member = (seqid[:, None] == jnp.arange(seq_weights.shape[0], dtype=jnp.int32)[None, :]).astype(
        F32
    )
    weight_row = jnp.sum(member * seq_weights[None, :], axis=1) * (1.0 - flag)
    facts = [seqid.astype(F32), item_ids.astype(F32), flag, weight_row]
    row = jnp.stack(facts + [jnp.zeros_like(flag)] * 4)
    col = row.T

    away = lax.ppermute(events, "c", SWAP)
    a_pieces, b_pieces = gather_proj(w_uvqk)
    grid = [(i, j) for i in (0, 1, 3, 2) for j in (0, 1, 3, 2)]
    early = [ij for ij in grid if 2 not in ij]
    late = [ij for ij in grid if 2 in ij]
    part = uvqk_call(spot, events, away, a_pieces, b_pieces, early)
    own, for_away = uvqk_call(spot, events, away, a_pieces, b_pieces, late, part)
    par = lax.ppermute(for_away, "c", SWAP)
    mixed, grad_out, keep_u, send_u, keep_w, send_w = block_call(
        spot, own, par, events, targets, w_out_all, col, row
    )

    def add(mine, away):
        return (mine.astype(F32) + lax.ppermute(away, "c", SWAP).astype(F32)).astype(BF16)

    model = events.shape[1]
    chip_u, chip_w = add(keep_u, send_u), add(keep_w, send_w)
    part_w = lax.psum_scatter(chip_w, "x", scatter_dimension=0, tiled=True)
    got = lax.all_to_all(chip_u.reshape(64, 8, -1), CHIPS, 0, 0, tiled=True)
    total = jnp.sum(got.astype(F32), axis=0)
    n_unif = 32.0 * total[0, model] + total[0, model + 1]
    unif = jnp.broadcast_to(total[:, :model].astype(BF16)[None], (64, 8, model))
    unif_mine = lax.all_to_all(unif, CHIPS, 0, 0, tiled=True).reshape(512, -1)
    unif_mine, part_w = lax.optimization_barrier((unif_mine, part_w))
    got_w = lax.all_to_all(part_w.reshape(16, 8, model), ("y", "zh", "zl"), 0, 0, tiled=True)
    weighted_grad = jnp.sum(got_w.astype(F32), axis=0) / (jnp.float32(count * 128) - n_unif)
    unif_away = lax.ppermute(unif_mine, "c", SWAP)
    mixed_mine = lax.dynamic_slice_in_dim(mixed, core * 512, 512, 1)
    mixed_away = lax.dynamic_slice_in_dim(mixed, (1 - core) * 512, 512, 1)
    proj_mine = jnp.dot(grad_out, unif_mine.T, preferred_element_type=F32)
    proj_away = jnp.dot(grad_out, unif_away.T, preferred_element_type=F32)
    per_row = jnp.sum(mixed_mine.astype(F32) * proj_mine, axis=1) + jnp.sum(
        mixed_away.astype(F32) * proj_away, axis=1
    )
    per_row = -per_row * (1.0 - flag) / n_unif
    hyper = jnp.sum(member * per_row[:, None], axis=0)
    return (hyper, weighted_grad)


def solution(mesh):
    fine = Mesh(mesh.devices.reshape(4, 2, 4, 2, 2), AXES)
    dp = ("y", "zh", "x", "c")
    return jax.shard_map(
        on_device,
        mesh=fine,
        in_specs=(
            P(AXES, None),
            P(None, dp),
            P(dp, None),
            P(AXES, None),
            P(AXES),
            P(AXES),
            P(AXES, None),
            P(AXES),
        ),
        out_specs=(P(AXES), P(AXES, None)),
        check_vma=False,
    )
```

```python
import jax
import jax.numpy as jnp
from jax import lax
from jax.experimental import pallas as pl
from jax.experimental.pallas import tpu as pltpu
from jax.sharding import Mesh
from jax.sharding import PartitionSpec as P

HEADS = 8
DH = 128
AXES = ("y", "zh", "x", "c", "zl")
CHIPS = ("y", "zh", "x", "zl")
SWAP = [(0, 1), (1, 0)]
ACROSS = [(0, 3), (3, 0), (1, 2), (2, 1)]
ORDER = (
    ((0, 0), (0, 3), (3, 0), (3, 1), (1, 3)),
    ((0, 1), (1, 0), (1, 1), (3, 3)),
    ((0, 2), (1, 2), (3, 2), (2, 0), (2, 1), (2, 3), (2, 2)),
)
F32 = jnp.float32
BF16 = jnp.bfloat16
MIB = 1024 * 1024
NT = (((1,), (1,)), ((), ()))
NN = (((1,), (0,)), ((), ()))


def hop(array, axis, step):
    return lax.ppermute(array, axis, [(i, (i + step) % 4) for i in range(4)])


def first_rings(a, a_axis, b, b_axis, cut, also):
    got, also = lax.optimization_barrier(
        ((hop(a, a_axis, 1), hop(a, a_axis, -1), hop(b, b_axis, 1), hop(b, b_axis, -1)), also)
    )
    a_below, a_above, b_below, b_above = got
    far = (
        hop(a_below[:cut], a_axis, 1),
        hop(a_above[cut:], a_axis, -1),
        hop(b_below[:cut], b_axis, 1),
        hop(b_above[cut:], b_axis, -1),
    )
    return (a, a_above, far[:2], a_below), (b, b_above, far[2:], b_below), also


def last_rings(a, b):
    one = (hop(a[0], "y", 1), hop(a[1], "y", -1), hop(b[0], "x", 1), hop(b[1], "x", -1))
    (a, b), one = lax.optimization_barrier(((a, b), one))
    none = (None, None)
    first = ((a, (None, one[1]), none, (one[0], None)), (b, (None, one[3]), none, (one[2], None)))
    two = (hop(a[1], "y", 1), hop(a[0], "y", -1), hop(b[1], "x", 1), hop(b[0], "x", -1))
    one, two = lax.optimization_barrier((one, two))
    a_next = (a, (two[1], one[1]), none, (one[0], two[0]))
    b_next = (b, (two[3], one[3]), none, (one[2], two[2]))
    a_far = (hop(one[0], "y", 1), hop(one[1], "y", -1))
    b_far = (hop(one[2], "x", 1), hop(one[3], "x", -1))
    last = (a_next[:2] + (a_far, a_next[3]), b_next[:2] + (b_far, b_next[3]))
    return first, (a_next, b_next), last


def gather_proj(w_uvqk, also):
    half = w_uvqk.shape[0] // 2
    rows = w_uvqk.T
    other = lax.ppermute(rows, ("zh", "zl"), ACROSS)
    both = jnp.stack([rows, other])
    a_line, b_line, also = first_rings(both[:, :, :half], "x", both[:, :, half:], "y", 1, also)

    def halves(pieces):
        own, above, far, below = pieces
        return jnp.stack([own, above]), jnp.stack([jnp.concatenate(far, 0), below])

    return last_rings(halves(a_line), halves(b_line)), also


def place_of(pieces, major, minor):
    return pieces[major][minor // 2], minor % 2


def uvqk_call(place, own, away, a_pieces, b_pieces, offsets):
    count, model = own.shape
    half = model // 2
    arrays, steps = [], []

    def seat(array):
        for i, seen in enumerate(arrays):
            if seen is array:
                return i
        arrays.append(array)
        return len(arrays) - 1

    for y_off, x_off in offsets:
        a_from, a_at = place_of(a_pieces, y_off, x_off)
        b_from, b_at = place_of(b_pieces, x_off, y_off)
        steps.append((y_off, x_off, (seat(a_from), a_at), (seat(b_from), b_at)))
    near = len(arrays)

    def kernel(place_ref, own_ref, away_ref, *refs):
        weights = refs[:near]
        out_own, out_away, w_buf, o_buf, w_sem, o_sem = refs[near:]
        loads = []
        for n, (_, _, a, b) in enumerate(steps):
            for side, (src, index) in enumerate((a, b)):
                for z_off in range(2):
                    z_at = place_ref[1] if z_off == 0 else 1 - place_ref[1]
                    c = pltpu.make_async_copy(
                        weights[src].at[index, z_off],
                        w_buf.at[n, z_at, :, side * half : (side + 1) * half],
                        w_sem.at[n, side, z_off],
                    )
                    c.start()
                    loads.append(c)
        stores = []
        for first in range(0, len(steps), 2):
            group = range(first, min(first + 2, len(steps)))
            for n in group:
                for c in loads[4 * n : 4 * n + 4]:
                    c.wait()
            rows = w_buf[first : first + len(group)].reshape(len(group) * 128, model)
            for who, (ev_ref, out_ref) in enumerate(((own_ref, out_own), (away_ref, out_away))):
                acc = lax.dot_general(ev_ref[...], rows, NT, preferred_element_type=F32)
                act = (0.5 * acc * (1.0 + jnp.tanh(0.5 * acc))).astype(BF16)
                for i, n in enumerate(group):
                    o_buf[n, who] = act[:, i * 128 : (i + 1) * 128]
                    c = pltpu.make_async_copy(o_buf.at[n, who], out_ref.at[n], o_sem.at[n, who])
                    c.start()
                    stores.append(c)
        for c in stores:
            c.wait()

    any_spec = pl.BlockSpec(memory_space=pl.ANY)
    vmem = pl.BlockSpec(memory_space=pltpu.VMEM)
    shape = jax.ShapeDtypeStruct((len(steps), count, 128), BF16)
    return pl.pallas_call(
        kernel,
        out_shape=(shape, shape),
        in_specs=[pl.BlockSpec(memory_space=pltpu.SMEM), vmem, vmem]
        + [any_spec] * near,
        out_specs=(any_spec, any_spec),
        scratch_shapes=[
            pltpu.VMEM((len(steps), 2, 64, model), BF16),
            pltpu.VMEM((len(steps), 2, count, 128), BF16),
            pltpu.SemaphoreType.DMA((len(steps), 2, 2)),
            pltpu.SemaphoreType.DMA((len(steps), 2)),
        ],
        cost_estimate=pl.CostEstimate(
            flops=4 * count * model * 128 * len(steps),
            bytes_accessed=model * 256 * len(steps),
            transcendentals=2 * count * 128 * len(steps),
        ),
        compiler_params=pltpu.CompilerParams(vmem_limit_bytes=60 * MIB),
    )(place, own, away, *arrays)


def silu(x):
    return 0.5 * x * (1.0 + jnp.tanh(0.5 * x))


def sigmoid(x):
    return 1.0 / (1.0 + jnp.exp(-x))


def block_kernel(
    place, own_hbm, par_hbm, events_hbm, targets_hbm, w_out, col, row, mixed_ref, grad_ref, keep_u,
    send_u, all_w, own, par, events, targets, w_buf, attn, mixed_t, outs, parts_u, parts_w, digits,
    b_sem, w_sem, e_sem, p_sem, d_sem
):
    core = place[3]
    count = events.shape[0]
    model = events.shape[1]
    tile = count // 4
    blocks = []
    for who, (groups, held) in enumerate(((own_hbm, own), (par_hbm, par))):
        done = 0
        for offsets, ref in zip(ORDER, groups):
            for n, (y_off, x_off) in enumerate(offsets):
                y_at, x_at = lax.rem(place[0] + y_off, 4), lax.rem(place[2] + x_off, 4)
                c = pltpu.make_async_copy(ref.at[n], held.at[y_at, x_at], b_sem.at[who, done])
                c.start()
                blocks.append(c)
                done += 1
    loads = [
        pltpu.make_async_copy(events_hbm, events, e_sem.at[0]),
        pltpu.make_async_copy(targets_hbm, targets, e_sem.at[1]),
    ]
    for c in loads:
        c.start()
    for cls in range(2):
        for x in range(4):
            for zh in range(2):
                c = pltpu.make_async_copy(
                    w_out.at[zh * 512 + x * 128 + cls * 64 : zh * 512 + x * 128 + cls * 64 + 64],
                    w_buf.at[cls * 512 + x * 128 + zh * 64 : cls * 512 + x * 128 + zh * 64 + 64],
                    w_sem.at[cls, x, zh],
                )
                c.start()
                loads.append(c)
    lane = lax.broadcasted_iota(jnp.int32, (tile, 256), 1)
    low = lax.rem(lane, 128) < 64
    scale = 1.0 / DH**0.5
    for c in blocks:
        c.wait()
    for i in range(4):
        lo, hi = max(0, (i - 1) * tile), (i + 1) * tile
        here = slice(i * tile, hi)
        at_i = i * tile + lax.broadcasted_iota(jnp.int32, (tile, hi - lo), 0)
        at_j = lo + lax.broadcasted_iota(jnp.int32, (tile, hi - lo), 1)
        allowed = (col[here, 0:1] == row[0:1, lo:hi]) & (at_j <= at_i)
        for x in range(4):
            q = jnp.concatenate([own[2, x, here], par[2, x, here]], 1)
            k = jnp.concatenate([own[3, x, lo:hi], par[3, x, lo:hi]], 1)
            v = jnp.concatenate([own[1, x, lo:hi], par[1, x, lo:hi]], 1)
            halves = []
            for pick in (low, ~low):
                qz = jnp.where(pick, q, jnp.zeros_like(q))
                s = lax.dot_general(qz, k, NT, preferred_element_type=F32) * scale
                p = jnp.where(allowed, silu(s) * (1.0 / 128.0), 0.0).astype(BF16)
                halves.append(lax.dot_general(p, v, NN, preferred_element_type=F32))
            o = jnp.where(low, halves[0], halves[1])
            attn[here, x * 128 : (x + 1) * 128] = o[:, :128]
            attn[here, 512 + x * 128 : 512 + (x + 1) * 128] = o[:, 128:]
        a = attn[here, :]
        mean = jnp.mean(a, axis=1, keepdims=True)
        a = a - mean
        a = a * lax.rsqrt(jnp.mean(a * a, axis=1, keepdims=True) + 1e-05)
        for side, src in ((core, own), (1 - core, par)):
            base = 0 if src is own else 512
            u = jnp.concatenate([src[0, x, here] for x in range(4)], 1).astype(F32)
            m = (a[:, base : base + 512] * u).astype(BF16)
            mixed_ref[here, pl.ds(pl.multiple_of(side * 512, 512), 512)] = m
    for c in loads:
        c.wait()
    for n in range(0, model, 512):
        cols = slice(n, n + 512)
        s = jnp.dot(mixed_ref[...], w_buf[:, cols], preferred_element_type=F32)
        outs[:, cols] = (events[:, cols].astype(F32) + s).astype(BF16)
    mixed_t[...] = mixed_ref[...].T
    scores = lax.dot_general(outs[...], targets[...], NT, preferred_element_type=F32)
    at_i = lax.broadcasted_iota(jnp.int32, (count, count), 0)
    at_j = lax.broadcasted_iota(jnp.int32, (count, count), 1)
    other = col[:, 1:2] != row[1:2, :]
    coef = jnp.where(
        at_i == at_j, -sigmoid(-scores), jnp.where(other, sigmoid(scores) * (1.0 / count), 0.0)
    ).astype(BF16)
    flagged = jnp.sum(row[2:3, :], axis=1, keepdims=True)
    high = jnp.floor(flagged * (1.0 / 32.0))
    at = lax.broadcasted_iota(jnp.int32, (512, 128), 1)
    digits[...] = jnp.where(at == 0, high, jnp.where(at == 1, flagged - 32.0 * high, 0.0)).astype(BF16)
    count_copies = [
        pltpu.make_async_copy(digits, ref.at[:, model : model + 128], d_sem.at[i])
        for i, ref in enumerate((keep_u, send_u))
    ]
    for c in count_copies:
        c.start()
    stores = [None, None]
    for turn, n in enumerate(range(0, model, 512)):
        cols = slice(n, n + 512)
        slot = turn % 2
        g = jnp.dot(coef, targets[:, cols], preferred_element_type=F32).astype(BF16)
        grad_ref[:, cols] = g
        unif = (g.astype(F32) * col[:, 2:3]).astype(BF16)
        scaled = (g.astype(F32) * col[:, 3:4]).astype(BF16)
        g_u = jnp.dot(mixed_t[...], unif, preferred_element_type=F32)
        g_w = jnp.dot(mixed_t[...], scaled, preferred_element_type=F32)
        if stores[slot] is not None:
            for c in stores[slot]:
                c.wait()
        parts_u[slot] = g_u.astype(BF16).reshape(2, 512, 512)
        for n16 in range(64):
            x, to, y, zh = n16 // 16, n16 // 8 % 2, n16 // 2 % 4, n16 % 2
            r = (y * 8 + zh * 4 + x) * 32 + to * 16
            w_at = (r // 64 % 2) * 512 + (r // 128 % 4) * 128 + (r // 512) * 64 + r % 64
            parts_w[slot, n16 * 16 : n16 * 16 + 16] = g_w[w_at : w_at + 16].astype(BF16)
        stores[slot] = []
        for which, (ref, src) in enumerate(
            (
                (keep_u, parts_u.at[slot, core]),
                (send_u, parts_u.at[slot, 1 - core]),
                (all_w, parts_w.at[slot]),
            )
        ):
            c = pltpu.make_async_copy(src, ref.at[:, cols], p_sem.at[slot, which])
            c.start()
            stores[slot].append(c)
    for pending in stores:
        for c in pending:
            c.wait()
    for c in count_copies:
        c.wait()


def block_call(place, own, par, events, targets, w_out, col, row):
    count, model = events.shape
    width = w_out.shape[0]
    any_spec = pl.BlockSpec(memory_space=pl.ANY)
    vmem = pl.BlockSpec(memory_space=pltpu.VMEM)
    part_u = jax.ShapeDtypeStruct((512, model + 128), BF16)
    part_w = jax.ShapeDtypeStruct((width, model), BF16)
    groups = len(own)

    def kernel(place_ref, *refs):
        block_kernel(place_ref, refs[:groups], refs[groups : 2 * groups], *refs[2 * groups :])
    return pl.pallas_call(
        kernel,
        out_shape=(
            jax.ShapeDtypeStruct((count, width), BF16),
            jax.ShapeDtypeStruct((count, model), BF16),
            part_u,
            part_u,
            part_w,
        ),
        in_specs=[pl.BlockSpec(memory_space=pltpu.SMEM)]
        + [any_spec] * (2 * groups + 3)
        + [vmem] * 2,
        out_specs=(vmem, vmem) + (any_spec,) * 3,
        scratch_shapes=[
            pltpu.VMEM((4, 4, count, 128), BF16),
            pltpu.VMEM((4, 4, count, 128), BF16),
            pltpu.VMEM((count, model), BF16),
            pltpu.VMEM((count, model), BF16),
            pltpu.VMEM((width, model), BF16),
            pltpu.VMEM((count, width), F32),
            pltpu.VMEM((width, count), BF16),
            pltpu.VMEM((count, model), BF16),
            pltpu.VMEM((2, 2, 512, 512), BF16),
            pltpu.VMEM((2, width, 512), BF16),
            pltpu.VMEM((512, 128), BF16),
            pltpu.SemaphoreType.DMA((2, 16)),
            pltpu.SemaphoreType.DMA((2, 4, 2)),
            pltpu.SemaphoreType.DMA((2,)),
            pltpu.SemaphoreType.DMA((2, 3)),
            pltpu.SemaphoreType.DMA((2,)),
        ],
        cost_estimate=pl.CostEstimate(
            flops=10 * 1024 * MIB, bytes_accessed=24 * MIB, transcendentals=2 * MIB
        ),
        compiler_params=pltpu.CompilerParams(vmem_limit_bytes=60 * MIB),
    )(place, *own, *par, events, targets, w_out, col, row)


def on_device(events, w_uvqk, w_out, targets, item_ids, uniform_flags, lengths, seq_weights):
    count = events.shape[0]
    core = lax.axis_index("c")
    flag = uniform_flags.astype(F32)
    spot = jnp.stack([lax.axis_index(n) for n in ("y", "zh", "x", "c")]).astype(jnp.int32)
    w_out_all = lax.all_gather(w_out, ("y", "zh", "x", "c"), axis=0, tiled=True)
    place = jnp.arange(count, dtype=jnp.int32)
    ends = jnp.cumsum(lengths[0])
    seqid = jnp.sum((place[:, None] >= ends[None, :]).astype(jnp.int32), axis=1)
    member = (seqid[:, None] == jnp.arange(seq_weights.shape[0], dtype=jnp.int32)[None, :]).astype(
        F32
    )
    weight_row = jnp.sum(member * seq_weights[None, :], axis=1) * (1.0 - flag)
    facts = [seqid.astype(F32), item_ids.astype(F32), flag, weight_row]
    row = jnp.stack(facts + [jnp.zeros_like(flag)] * 4)
    col = row.T

    away = lax.ppermute(events, "c", SWAP)
    phases, away = gather_proj(w_uvqk, away)
    own, par = [], []
    for (a_pieces, b_pieces), offsets in zip(phases, ORDER):
        mine, for_away = uvqk_call(spot, events, away, a_pieces, b_pieces, offsets)
        own.append(mine)
        par.append(lax.ppermute(for_away, "c", SWAP))
    mixed, grad_out, keep_u, send_u, all_w = block_call(
        spot, own, par, events, targets, w_out_all, col, row
    )

    def add(mine, away):
        return (mine.astype(F32) + lax.ppermute(away, "c", SWAP).astype(F32)).astype(BF16)

    model = events.shape[1]
    part_w = lax.psum_scatter(all_w, ("x", "c"), scatter_dimension=0, tiled=True)
    chip_u = add(keep_u, send_u)
    got = lax.all_to_all(chip_u.reshape(64, 8, -1), CHIPS, 0, 0, tiled=True)
    total = jnp.sum(got.astype(F32), axis=0)
    n_unif = 32.0 * total[0, model] + total[0, model + 1]
    unif = jnp.broadcast_to(total[:, :model].astype(BF16)[None], (64, 8, model))
    unif_mine = lax.all_to_all(unif, CHIPS, 0, 0, tiled=True).reshape(512, -1)
    unif_mine, part_w = lax.optimization_barrier((unif_mine, part_w))
    got_w = lax.all_to_all(part_w.reshape(16, 8, model), ("y", "zh", "zl"), 0, 0, tiled=True)
    weighted_grad = jnp.sum(got_w.astype(F32), axis=0) / (jnp.float32(count * 128) - n_unif)
    unif_away = lax.ppermute(unif_mine, "c", SWAP)
    mixed_mine = lax.dynamic_slice_in_dim(mixed, core * 512, 512, 1)
    mixed_away = lax.dynamic_slice_in_dim(mixed, (1 - core) * 512, 512, 1)
    proj_mine = jnp.dot(grad_out, unif_mine.T, preferred_element_type=F32)
    proj_away = jnp.dot(grad_out, unif_away.T, preferred_element_type=F32)
    per_row = jnp.sum(mixed_mine.astype(F32) * proj_mine, axis=1) + jnp.sum(
        mixed_away.astype(F32) * proj_away, axis=1
    )
    per_row = -per_row * (1.0 - flag) / n_unif
    hyper = jnp.sum(member * per_row[:, None], axis=0)
    return (hyper, weighted_grad)


def solution(mesh):
    fine = Mesh(mesh.devices.reshape(4, 2, 4, 2, 2), AXES)
    dp = ("y", "zh", "x", "c")
    return jax.shard_map(
        on_device,
        mesh=fine,
        in_specs=(
            P(AXES, None),
            P(None, dp),
            P(dp, None),
            P(AXES, None),
            P(AXES),
            P(AXES),
            P(AXES, None),
            P(AXES),
        ),
        out_specs=(P(AXES), P(AXES, None)),
        check_vma=False,
    )
```

```python
import jax
import jax.numpy as jnp
from jax import lax
from jax.experimental import pallas as pl
from jax.experimental.pallas import tpu as pltpu
from jax.sharding import Mesh
from jax.sharding import PartitionSpec as P

HEADS = 8
DH = 128
AXES = ("y", "zh", "x", "c", "zl")
CHIPS = ("y", "zh", "x", "zl")
SWAP = [(0, 1), (1, 0)]
ACROSS = [(0, 3), (3, 0), (1, 2), (2, 1)]
ORDER = (
    ((0, 0), (0, 1), (0, 3), (1, 0), (1, 1), (1, 3), (3, 0), (3, 1), (3, 3)),
    ((0, 2), (1, 2), (3, 2), (2, 0), (2, 1), (2, 3), (2, 2)),
)
F32 = jnp.float32
BF16 = jnp.bfloat16
MIB = 1024 * 1024
NT = (((1,), (1,)), ((), ()))
NN = (((1,), (0,)), ((), ()))


def hop(array, axis, step):
    return lax.ppermute(array, axis, [(i, (i + step) % 4) for i in range(4)])


def first_rings(a, a_axis, b, b_axis, cut, also):
    got, also = lax.optimization_barrier(
        ((hop(a, a_axis, 1), hop(a, a_axis, -1), hop(b, b_axis, 1), hop(b, b_axis, -1)), also)
    )
    a_below, a_above, b_below, b_above = got
    far = (
        hop(a_below[:cut], a_axis, 1),
        hop(a_above[cut:], a_axis, -1),
        hop(b_below[:cut], b_axis, 1),
        hop(b_above[cut:], b_axis, -1),
    )
    return (a, a_above, far[:2], a_below), (b, b_above, far[2:], b_below), also


def last_rings(a, b):
    one = (hop(a[0], "y", 1), hop(a[1], "y", -1), hop(b[0], "x", 1), hop(b[1], "x", -1))
    two = (hop(a[1], "y", 1), hop(a[0], "y", -1), hop(b[1], "x", 1), hop(b[0], "x", -1))
    one, two = lax.optimization_barrier((one, two))
    a_near = (a, (two[1], one[1]), None, (one[0], two[0]))
    b_near = (b, (two[3], one[3]), None, (one[2], two[2]))
    a_far = (hop(one[0], "y", 1), hop(one[1], "y", -1))
    b_far = (hop(one[2], "x", 1), hop(one[3], "x", -1))
    last = (a_near[:2] + (a_far, a_near[3]), b_near[:2] + (b_far, b_near[3]))
    return (a_near, b_near), last


def gather_proj(w_uvqk, also):
    half = w_uvqk.shape[0] // 2
    rows = w_uvqk.T
    other = lax.ppermute(rows, ("zh", "zl"), ACROSS)
    both = jnp.stack([rows, other])
    a_line, b_line, also = first_rings(both[:, :, :half], "x", both[:, :, half:], "y", 1, also)

    def halves(pieces):
        own, above, far, below = pieces
        return jnp.stack([own, above]), jnp.stack([jnp.concatenate(far, 0), below])

    return last_rings(halves(a_line), halves(b_line)), also


def place_of(pieces, major, minor):
    return pieces[major][minor // 2], minor % 2


def uvqk_call(place, own, away, a_pieces, b_pieces, offsets):
    count, model = own.shape
    half = model // 2
    arrays, steps = [], []

    def seat(array):
        for i, seen in enumerate(arrays):
            if seen is array:
                return i
        arrays.append(array)
        return len(arrays) - 1

    for y_off, x_off in offsets:
        a_from, a_at = place_of(a_pieces, y_off, x_off)
        b_from, b_at = place_of(b_pieces, x_off, y_off)
        steps.append((y_off, x_off, (seat(a_from), a_at), (seat(b_from), b_at)))
    near = len(arrays)

    def kernel(place_ref, own_ref, away_ref, *refs):
        weights = refs[:near]
        out_own, out_away, w_buf, o_buf, w_sem, o_sem = refs[near:]
        loads = []
        for n, (_, _, a, b) in enumerate(steps):
            for side, (src, index) in enumerate((a, b)):
                for z_off in range(2):
                    z_at = place_ref[1] if z_off == 0 else 1 - place_ref[1]
                    c = pltpu.make_async_copy(
                        weights[src].at[index, z_off],
                        w_buf.at[n, z_at, :, side * half : (side + 1) * half],
                        w_sem.at[n, side, z_off],
                    )
                    c.start()
                    loads.append(c)
        stores = []
        for first in range(0, len(steps), 2):
            group = range(first, min(first + 2, len(steps)))
            for n in group:
                for c in loads[4 * n : 4 * n + 4]:
                    c.wait()
            rows = w_buf[first : first + len(group)].reshape(len(group) * 128, model)
            for who, (ev_ref, out_ref) in enumerate(((own_ref, out_own), (away_ref, out_away))):
                acc = lax.dot_general(ev_ref[...], rows, NT, preferred_element_type=F32)
                act = (0.5 * acc * (1.0 + jnp.tanh(0.5 * acc))).astype(BF16)
                for i, n in enumerate(group):
                    o_buf[n, who] = act[:, i * 128 : (i + 1) * 128]
                    c = pltpu.make_async_copy(o_buf.at[n, who], out_ref.at[n], o_sem.at[n, who])
                    c.start()
                    stores.append(c)
        for c in stores:
            c.wait()

    any_spec = pl.BlockSpec(memory_space=pltpu.HBM)
    vmem = pl.BlockSpec(memory_space=pltpu.VMEM)
    shape = jax.ShapeDtypeStruct((len(steps), count, 128), BF16)
    return pl.pallas_call(
        kernel,
        out_shape=(shape, shape),
        in_specs=[pl.BlockSpec(memory_space=pltpu.SMEM), vmem, vmem]
        + [any_spec] * near,
        out_specs=(any_spec, any_spec),
        scratch_shapes=[
            pltpu.VMEM((len(steps), 2, 64, model), BF16),
            pltpu.VMEM((len(steps), 2, count, 128), BF16),
            pltpu.SemaphoreType.DMA((len(steps), 2, 2)),
            pltpu.SemaphoreType.DMA((len(steps), 2)),
        ],
        cost_estimate=pl.CostEstimate(
            flops=4 * count * model * 128 * len(steps),
            bytes_accessed=model * 256 * len(steps),
            transcendentals=2 * count * 128 * len(steps),
        ),
        compiler_params=pltpu.CompilerParams(vmem_limit_bytes=20 * MIB),
    )(place, own, away, *arrays)


def silu(x):
    return 0.5 * x * (1.0 + jnp.tanh(0.5 * x))


def sigmoid(x):
    return 1.0 / (1.0 + jnp.exp(-x))


def block_kernel(
    place, own_hbm, par_hbm, w_out, events, targets, col, row, mixed_hbm, grad_hbm, keep_u, send_u,
    keep_w, send_w, own, par, w_buf, attn, mixed_ref, mixed_t, outs, grad_ref, parts_u, parts_w,
    digits, b_sem, w_sem, m_sem, p_sem, d_sem
):
    core = place[3]
    count = events.shape[0]
    model = events.shape[1]
    tile = count // 4
    blocks = []
    for who, (groups, held) in enumerate(((own_hbm, own), (par_hbm, par))):
        done = 0
        for offsets, ref in zip(ORDER, groups):
            for n, (y_off, x_off) in enumerate(offsets):
                y_at, x_at = lax.rem(place[0] + y_off, 4), lax.rem(place[2] + x_off, 4)
                c = pltpu.make_async_copy(ref.at[n], held.at[y_at, x_at], b_sem.at[who, done])
                c.start()
                blocks.append(c)
                done += 1
    loads = []
    for cls in range(2):
        for x in range(4):
            for zh in range(2):
                c = pltpu.make_async_copy(
                    w_out.at[zh * 512 + x * 128 + cls * 64 : zh * 512 + x * 128 + cls * 64 + 64],
                    w_buf.at[cls * 512 + x * 128 + zh * 64 : cls * 512 + x * 128 + zh * 64 + 64],
                    w_sem.at[cls, x, zh],
                )
                c.start()
                loads.append(c)
    lane = lax.broadcasted_iota(jnp.int32, (tile, 256), 1)
    low = lax.rem(lane, 128) < 64
    scale = 1.0 / DH**0.5
    for c in blocks:
        c.wait()
    for i in range(4):
        lo, hi = max(0, (i - 1) * tile), (i + 1) * tile
        here = slice(i * tile, hi)
        at_i = i * tile + lax.broadcasted_iota(jnp.int32, (tile, hi - lo), 0)
        at_j = lo + lax.broadcasted_iota(jnp.int32, (tile, hi - lo), 1)
        allowed = (col[here, 0:1] == row[0:1, lo:hi]) & (at_j <= at_i)
        for x in range(4):
            q = jnp.concatenate([own[2, x, here], par[2, x, here]], 1)
            k = jnp.concatenate([own[3, x, lo:hi], par[3, x, lo:hi]], 1)
            v = jnp.concatenate([own[1, x, lo:hi], par[1, x, lo:hi]], 1)
            halves = []
            for pick in (low, ~low):
                qz = jnp.where(pick, q, jnp.zeros_like(q))
                s = lax.dot_general(qz, k, NT, preferred_element_type=F32) * scale
                p = jnp.where(allowed, silu(s) * (1.0 / 128.0), 0.0).astype(BF16)
                halves.append(lax.dot_general(p, v, NN, preferred_element_type=F32))
            o = jnp.where(low, halves[0], halves[1])
            attn[here, x * 128 : (x + 1) * 128] = o[:, :128]
            attn[here, 512 + x * 128 : 512 + (x + 1) * 128] = o[:, 128:]
        a = attn[here, :]
        mean = jnp.mean(a, axis=1, keepdims=True)
        a = a - mean
        a = a * lax.rsqrt(jnp.mean(a * a, axis=1, keepdims=True) + 1e-05)
        for side, src in ((core, own), (1 - core, par)):
            base = 0 if src is own else 512
            u = jnp.concatenate([src[0, x, here] for x in range(4)], 1).astype(F32)
            m = (a[:, base : base + 512] * u).astype(BF16)
            mixed_ref[here, pl.ds(pl.multiple_of(side * 512, 512), 512)] = m
    for c in loads:
        c.wait()
    for n in range(0, model, 512):
        cols = slice(n, n + 512)
        s = jnp.dot(mixed_ref[...], w_buf[:, cols], preferred_element_type=F32)
        outs[:, cols] = (events[:, cols].astype(F32) + s).astype(BF16)
    mixed_t[...] = mixed_ref[...].T
    count_copies = [pltpu.make_async_copy(mixed_ref, mixed_hbm, m_sem)]
    scores = lax.dot_general(outs[...], targets[...], NT, preferred_element_type=F32)
    at_i = lax.broadcasted_iota(jnp.int32, (count, count), 0)
    at_j = lax.broadcasted_iota(jnp.int32, (count, count), 1)
    other = col[:, 1:2] != row[1:2, :]
    coef = sigmoid(jnp.where(at_i == at_j, -scores, scores))
    coef = jnp.where(
        at_i == at_j, -coef, jnp.where(other, coef * (1.0 / count), 0.0)
    ).astype(BF16)
    flagged = jnp.sum(row[2:3, :], axis=1, keepdims=True)
    high = jnp.floor(flagged * (1.0 / 32.0))
    at = lax.broadcasted_iota(jnp.int32, (512, 128), 1)
    digits[...] = jnp.where(at == 0, high, jnp.where(at == 1, flagged - 32.0 * high, 0.0)).astype(BF16)
    count_copies += [
        pltpu.make_async_copy(digits, ref.at[:, model : model + 128], d_sem.at[i])
        for i, ref in enumerate((keep_u, send_u))
    ]
    for c in count_copies:
        c.start()
    stores = [None, None]
    for turn, n in enumerate(range(0, model, 512)):
        cols = slice(n, n + 512)
        slot = turn % 2
        g = jnp.dot(coef, targets[:, cols], preferred_element_type=F32).astype(BF16)
        grad_ref[:, cols] = g
        unif = (g.astype(F32) * col[:, 2:3]).astype(BF16)
        scaled = (g.astype(F32) * col[:, 3:4]).astype(BF16)
        g_u = jnp.dot(mixed_t[...], unif, preferred_element_type=F32)
        g_w = jnp.dot(mixed_t[...], scaled, preferred_element_type=F32)
        if stores[slot] is not None:
            for c in stores[slot]:
                c.wait()
        parts_u[slot] = g_u.astype(BF16).reshape(2, 512, 512)
        for to in range(2):
            for q in range(32):
                x, y, zh = q // 8, q // 2 % 4, q % 2
                r = (y * 8 + zh * 4 + x) * 32 + to * 16
                w_at = (r // 64 % 2) * 512 + (r // 128 % 4) * 128 + (r // 512) * 64 + r % 64
                parts_w[slot, to, q * 16 : q * 16 + 16] = g_w[w_at : w_at + 16].astype(BF16)
        stores[slot] = []
        for which, (ref, src) in enumerate(
            (
                (keep_u, parts_u.at[slot, core]),
                (send_u, parts_u.at[slot, 1 - core]),
                (keep_w, parts_w.at[slot, core]),
                (send_w, parts_w.at[slot, 1 - core]),
                (grad_hbm, grad_ref.at[:, cols]),
            )
        ):
            c = pltpu.make_async_copy(src, ref.at[:, cols], p_sem.at[slot, which])
            c.start()
            stores[slot].append(c)
    for pending in stores:
        for c in pending:
            c.wait()
    for c in count_copies:
        c.wait()


def block_call(place, own, par, events, targets, w_out, col, row):
    count, model = events.shape
    width = w_out.shape[0]
    any_spec = pl.BlockSpec(memory_space=pltpu.HBM)
    vmem = pl.BlockSpec(memory_space=pltpu.VMEM)
    part_u = jax.ShapeDtypeStruct((512, model + 128), BF16)
    part_w = jax.ShapeDtypeStruct((512, model), BF16)
    groups = len(own)

    def kernel(place_ref, *refs):
        block_kernel(place_ref, refs[:groups], refs[groups : 2 * groups], *refs[2 * groups :])
    return pl.pallas_call(
        kernel,
        out_shape=(
            jax.ShapeDtypeStruct((count, width), BF16),
            jax.ShapeDtypeStruct((count, model), BF16),
            part_u,
            part_u,
            part_w,
            part_w,
        ),
        in_specs=[pl.BlockSpec(memory_space=pltpu.SMEM)]
        + [any_spec] * (2 * groups + 1)
        + [vmem] * 4,
        out_specs=(any_spec,) * 6,
        scratch_shapes=[
            pltpu.VMEM((4, 4, count, 128), BF16),
            pltpu.VMEM((4, 4, count, 128), BF16),
            pltpu.VMEM((width, model), BF16),
            pltpu.VMEM((count, width), F32),
            pltpu.VMEM((count, width), BF16),
            pltpu.VMEM((width, count), BF16),
            pltpu.VMEM((count, model), BF16),
            pltpu.VMEM((count, model), BF16),
            pltpu.VMEM((2, 2, 512, 512), BF16),
            pltpu.VMEM((2, 2, 512, 512), BF16),
            pltpu.VMEM((512, 128), BF16),
            pltpu.SemaphoreType.DMA((2, 16)),
            pltpu.SemaphoreType.DMA((2, 4, 2)),
            pltpu.SemaphoreType.DMA,
            pltpu.SemaphoreType.DMA((2, 5)),
            pltpu.SemaphoreType.DMA((2,)),
        ],
        cost_estimate=pl.CostEstimate(
            flops=10 * 1024 * MIB, bytes_accessed=24 * MIB, transcendentals=2 * MIB
        ),
        compiler_params=pltpu.CompilerParams(vmem_limit_bytes=36 * MIB),
    )(place, *own, *par, w_out, events, targets, col, row)


def on_device(events, w_uvqk, w_out, targets, item_ids, uniform_flags, lengths, seq_weights):
    count = events.shape[0]
    core = lax.axis_index("c")
    flag = uniform_flags.astype(F32)
    spot = jnp.stack([lax.axis_index(n) for n in ("y", "zh", "x", "c")]).astype(jnp.int32)
    w_out_all = lax.all_gather(w_out, ("y", "zh", "x", "c"), axis=0, tiled=True)
    place = jnp.arange(count, dtype=jnp.int32)
    ends = jnp.cumsum(lengths[0])
    seqid = jnp.sum((place[:, None] >= ends[None, :]).astype(jnp.int32), axis=1)
    member = (seqid[:, None] == jnp.arange(seq_weights.shape[0], dtype=jnp.int32)[None, :]).astype(
        F32
    )
    weight_row = jnp.sum(member * seq_weights[None, :], axis=1) * (1.0 - flag)
    facts = [seqid.astype(F32), item_ids.astype(F32), flag, weight_row]
    row = jnp.stack(facts + [jnp.zeros_like(flag)] * 4)
    col = row.T

    away = lax.ppermute(events, "c", SWAP)
    phases, away = gather_proj(w_uvqk, away)
    own, par = [], []
    for (a_pieces, b_pieces), offsets in zip(phases, ORDER):
        mine, for_away = uvqk_call(spot, events, away, a_pieces, b_pieces, offsets)
        own.append(mine)
        par.append(lax.ppermute(for_away, "c", SWAP))
    mixed, grad_out, keep_u, send_u, keep_w, send_w = block_call(
        spot, own, par, events, targets, w_out_all, col, row
    )

    def add(mine, away):
        return (mine.astype(F32) + lax.ppermute(away, "c", SWAP).astype(F32)).astype(BF16)

    model = events.shape[1]
    chip_u, chip_w = add(keep_u, send_u), add(keep_w, send_w)
    part_w = lax.psum_scatter(chip_w, "x", scatter_dimension=0, tiled=True)
    got = lax.all_to_all(chip_u.reshape(64, 8, -1), CHIPS, 0, 0, tiled=True)
    total = jnp.sum(got.astype(F32), axis=0)
    n_unif = 32.0 * total[0, model] + total[0, model + 1]
    unif = jnp.broadcast_to(total[:, :model].astype(BF16)[None], (64, 8, model))
    unif_mine = lax.all_to_all(unif, CHIPS, 0, 0, tiled=True).reshape(512, -1)
    unif_mine, part_w = lax.optimization_barrier((unif_mine, part_w))
    got_w = lax.all_to_all(part_w.reshape(16, 8, model), ("y", "zh", "zl"), 0, 0, tiled=True)
    weighted_grad = jnp.sum(got_w.astype(F32), axis=0) / (jnp.float32(count * 128) - n_unif)
    unif_away = lax.ppermute(unif_mine, "c", SWAP)
    mixed_mine = lax.dynamic_slice_in_dim(mixed, core * 512, 512, 1)
    mixed_away = lax.dynamic_slice_in_dim(mixed, (1 - core) * 512, 512, 1)
    proj_mine = jnp.dot(grad_out, unif_mine.T, preferred_element_type=F32)
    proj_away = jnp.dot(grad_out, unif_away.T, preferred_element_type=F32)
    per_row = jnp.sum(mixed_mine.astype(F32) * proj_mine, axis=1) + jnp.sum(
        mixed_away.astype(F32) * proj_away, axis=1
    )
    per_row = -per_row * (1.0 - flag) / n_unif
    hyper = jnp.sum(member * per_row[:, None], axis=0)
    return (hyper, weighted_grad)


def solution(mesh):
    fine = Mesh(mesh.devices.reshape(4, 2, 4, 2, 2), AXES)
    dp = ("y", "zh", "x", "c")
    return jax.shard_map(
        on_device,
        mesh=fine,
        in_specs=(
            P(AXES, None),
            P(None, dp),
            P(dp, None),
            P(AXES, None),
            P(AXES),
            P(AXES),
            P(AXES, None),
            P(AXES),
        ),
        out_specs=(P(AXES), P(AXES, None)),
        check_vma=False,
    )
```

```python
import jax
import jax.numpy as jnp
from jax import lax
from jax.experimental import pallas as pl
from jax.experimental.pallas import tpu as pltpu
from jax.sharding import Mesh
from jax.sharding import PartitionSpec as P

HEADS = 8
DH = 128
AXES = ("y", "zh", "x", "c", "zl")
CHIPS = ("y", "zh", "x", "zl")
SWAP = [(0, 1), (1, 0)]
ACROSS = [(0, 3), (3, 0), (1, 2), (2, 1)]
ORDER = (
    ((0, 0), (0, 1), (0, 3), (1, 0), (1, 1), (1, 3), (3, 0), (3, 1), (3, 3)),
    ((0, 2), (1, 2), (3, 2), (2, 0), (2, 1), (2, 3), (2, 2)),
)
F32 = jnp.float32
BF16 = jnp.bfloat16
MIB = 1024 * 1024
NT = (((1,), (1,)), ((), ()))
NN = (((1,), (0,)), ((), ()))


def hop(array, axis, step):
    return lax.ppermute(array, axis, [(i, (i + step) % 4) for i in range(4)])


def first_rings(a, a_axis, b, b_axis, cut):
    got = lax.optimization_barrier(
        (hop(a, a_axis, 1), hop(a, a_axis, -1), hop(b, b_axis, 1), hop(b, b_axis, -1))
    )
    a_below, a_above, b_below, b_above = got
    far = (
        hop(a_below[:cut], a_axis, 1),
        hop(a_above[cut:], a_axis, -1),
        hop(b_below[:cut], b_axis, 1),
        hop(b_above[cut:], b_axis, -1),
    )
    return (a, a_above, far[:2], a_below), (b, b_above, far[2:], b_below)


def last_rings(a, b):
    one = (hop(a[0], "y", 1), hop(a[1], "y", -1), hop(b[0], "x", 1), hop(b[1], "x", -1))
    two = (hop(a[1], "y", 1), hop(a[0], "y", -1), hop(b[1], "x", 1), hop(b[0], "x", -1))
    one, two = lax.optimization_barrier((one, two))
    a_near = (a, (two[1], one[1]), None, (one[0], two[0]))
    b_near = (b, (two[3], one[3]), None, (one[2], two[2]))
    a_far = (hop(one[0], "y", 1), hop(one[1], "y", -1))
    b_far = (hop(one[2], "x", 1), hop(one[3], "x", -1))
    last = (a_near[:2] + (a_far, a_near[3]), b_near[:2] + (b_far, b_near[3]))
    return (a_near, b_near), last


def gather_proj(w_uvqk):
    half = w_uvqk.shape[0] // 2
    rows = w_uvqk.T
    other = lax.ppermute(rows, ("zh", "zl"), ACROSS)
    both = jnp.stack([rows, other])
    a_line, b_line = first_rings(both[:, :, :half], "x", both[:, :, half:], "y", 1)

    def halves(pieces):
        own, above, far, below = pieces
        return jnp.stack([own, above]), jnp.stack([jnp.concatenate(far, 0), below])

    return last_rings(halves(a_line), halves(b_line))


def place_of(pieces, major, minor):
    return pieces[major][minor // 2], minor % 2


def uvqk_call(place, own, away, a_pieces, b_pieces, offsets):
    count, model = own.shape
    half = model // 2
    arrays, steps = [], []

    def seat(array):
        for i, seen in enumerate(arrays):
            if seen is array:
                return i
        arrays.append(array)
        return len(arrays) - 1

    for y_off, x_off in offsets:
        a_from, a_at = place_of(a_pieces, y_off, x_off)
        b_from, b_at = place_of(b_pieces, x_off, y_off)
        steps.append((y_off, x_off, (seat(a_from), a_at), (seat(b_from), b_at)))
    near = len(arrays)

    def kernel(place_ref, own_ref, away_ref, *refs):
        weights = refs[:near]
        out_own, out_away, w_buf, o_buf, w_sem, o_sem = refs[near:]
        loads = []
        for n, (_, _, a, b) in enumerate(steps):
            for side, (src, index) in enumerate((a, b)):
                for z_off in range(2):
                    z_at = place_ref[1] if z_off == 0 else 1 - place_ref[1]
                    c = pltpu.make_async_copy(
                        weights[src].at[index, z_off],
                        w_buf.at[n, z_at, :, side * half : (side + 1) * half],
                        w_sem.at[n, side, z_off],
                    )
                    c.start()
                    loads.append(c)
        stores = []
        for first in range(0, len(steps), 2):
            group = range(first, min(first + 2, len(steps)))
            for n in group:
                for c in loads[4 * n : 4 * n + 4]:
                    c.wait()
            rows = w_buf[first : first + len(group)].reshape(len(group) * 128, model)
            for who, (ev_ref, out_ref) in enumerate(((own_ref, out_own), (away_ref, out_away))):
                acc = lax.dot_general(ev_ref[...], rows, NT, preferred_element_type=F32)
                act = (0.5 * acc * (1.0 + jnp.tanh(0.5 * acc))).astype(BF16)
                for i, n in enumerate(group):
                    o_buf[n, who] = act[:, i * 128 : (i + 1) * 128]
                    c = pltpu.make_async_copy(o_buf.at[n, who], out_ref.at[n], o_sem.at[n, who])
                    c.start()
                    stores.append(c)
        for c in stores:
            c.wait()

    any_spec = pl.BlockSpec(memory_space=pltpu.HBM)
    vmem = pl.BlockSpec(memory_space=pltpu.VMEM)
    shape = jax.ShapeDtypeStruct((len(steps), count, 128), BF16)
    return pl.pallas_call(
        kernel,
        out_shape=(shape, shape),
        in_specs=[pl.BlockSpec(memory_space=pltpu.SMEM), vmem, vmem]
        + [any_spec] * near,
        out_specs=(any_spec, any_spec),
        scratch_shapes=[
            pltpu.VMEM((len(steps), 2, 64, model), BF16),
            pltpu.VMEM((len(steps), 2, count, 128), BF16),
            pltpu.SemaphoreType.DMA((len(steps), 2, 2)),
            pltpu.SemaphoreType.DMA((len(steps), 2)),
        ],
        cost_estimate=pl.CostEstimate(
            flops=4 * count * model * 128 * len(steps),
            bytes_accessed=model * 256 * len(steps),
            transcendentals=2 * count * 128 * len(steps),
        ),
        compiler_params=pltpu.CompilerParams(vmem_limit_bytes=60 * MIB),
    )(place, own, away, *arrays)


def silu(x):
    return 0.5 * x * (1.0 + jnp.tanh(0.5 * x))


def sigmoid(x):
    return 1.0 / (1.0 + jnp.exp(-x))


def block_kernel(
    place, own_hbm, par_hbm, w_out, events_hbm, targets_hbm, col, row, mixed_hbm, grad_hbm, keep_u, send_u,
    keep_w, send_w, own, par, events, targets, w_buf, attn, mixed_ref, mixed_t, outs, grad_ref,
    parts_u, parts_w, digits, b_sem, e_sem, w_sem, m_sem, p_sem, d_sem
):
    core = place[3]
    count, model = events.shape
    tile = count // 4
    blocks = []
    for who, (groups, held) in enumerate(((own_hbm, own), (par_hbm, par))):
        done = 0
        for offsets, ref in zip(ORDER, groups):
            for n, (y_off, x_off) in enumerate(offsets):
                y_at, x_at = lax.rem(place[0] + y_off, 4), lax.rem(place[2] + x_off, 4)
                c = pltpu.make_async_copy(ref.at[n], held.at[y_at, x_at], b_sem.at[who, done])
                c.start()
                blocks.append(c)
                done += 1
    loads = [
        pltpu.make_async_copy(events_hbm, events, e_sem.at[0]),
        pltpu.make_async_copy(targets_hbm, targets, e_sem.at[1]),
    ]
    for c in loads:
        c.start()
    for cls in range(2):
        for x in range(4):
            for zh in range(2):
                c = pltpu.make_async_copy(
                    w_out.at[zh * 512 + x * 128 + cls * 64 : zh * 512 + x * 128 + cls * 64 + 64],
                    w_buf.at[cls * 512 + x * 128 + zh * 64 : cls * 512 + x * 128 + zh * 64 + 64],
                    w_sem.at[cls, x, zh],
                )
                c.start()
                loads.append(c)
    lane = lax.broadcasted_iota(jnp.int32, (tile, 256), 1)
    low = lax.rem(lane, 128) < 64
    scale = 1.0 / DH**0.5
    for c in blocks:
        c.wait()
    for i in range(4):
        lo, hi = max(0, (i - 1) * tile), (i + 1) * tile
        here = slice(i * tile, hi)
        at_i = i * tile + lax.broadcasted_iota(jnp.int32, (tile, hi - lo), 0)
        at_j = lo + lax.broadcasted_iota(jnp.int32, (tile, hi - lo), 1)
        allowed = (col[here, 0:1] == row[0:1, lo:hi]) & (at_j <= at_i)
        for x in range(4):
            q = jnp.concatenate([own[2, x, here], par[2, x, here]], 1)
            k = jnp.concatenate([own[3, x, lo:hi], par[3, x, lo:hi]], 1)
            v = jnp.concatenate([own[1, x, lo:hi], par[1, x, lo:hi]], 1)
            halves = []
            for pick in (low, ~low):
                qz = jnp.where(pick, q, jnp.zeros_like(q))
                s = lax.dot_general(qz, k, NT, preferred_element_type=F32) * scale
                p = jnp.where(allowed, silu(s) * (1.0 / 128.0), 0.0).astype(BF16)
                halves.append(lax.dot_general(p, v, NN, preferred_element_type=F32))
            o = jnp.where(low, halves[0], halves[1])
            attn[here, x * 128 : (x + 1) * 128] = o[:, :128]
            attn[here, 512 + x * 128 : 512 + (x + 1) * 128] = o[:, 128:]
        a = attn[here, :]
        mean = jnp.mean(a, axis=1, keepdims=True)
        a = a - mean
        a = a * lax.rsqrt(jnp.mean(a * a, axis=1, keepdims=True) + 1e-05)
        for side, src in ((core, own), (1 - core, par)):
            base = 0 if src is own else 512
            u = jnp.concatenate([src[0, x, here] for x in range(4)], 1).astype(F32)
            m = (a[:, base : base + 512] * u).astype(BF16)
            mixed_ref[here, pl.ds(pl.multiple_of(side * 512, 512), 512)] = m
    for c in loads:
        c.wait()
    for n in range(0, model, 512):
        cols = slice(n, n + 512)
        s = jnp.dot(mixed_ref[...], w_buf[:, cols], preferred_element_type=F32)
        outs[:, cols] = (events[:, cols].astype(F32) + s).astype(BF16)
    mixed_t[...] = mixed_ref[...].T
    count_copies = [pltpu.make_async_copy(mixed_ref, mixed_hbm, m_sem)]
    scores = lax.dot_general(outs[...], targets[...], NT, preferred_element_type=F32)
    at_i = lax.broadcasted_iota(jnp.int32, (count, count), 0)
    at_j = lax.broadcasted_iota(jnp.int32, (count, count), 1)
    other = col[:, 1:2] != row[1:2, :]
    coef = sigmoid(jnp.where(at_i == at_j, -scores, scores))
    coef = jnp.where(
        at_i == at_j, -coef, jnp.where(other, coef * (1.0 / count), 0.0)
    ).astype(BF16)
    flagged = jnp.sum(row[2:3, :], axis=1, keepdims=True)
    high = jnp.floor(flagged * (1.0 / 32.0))
    at = lax.broadcasted_iota(jnp.int32, (512, 128), 1)
    digits[...] = jnp.where(at == 0, high, jnp.where(at == 1, flagged - 32.0 * high, 0.0)).astype(BF16)
    count_copies += [
        pltpu.make_async_copy(digits, ref.at[:, model : model + 128], d_sem.at[i])
        for i, ref in enumerate((keep_u, send_u))
    ]
    for c in count_copies:
        c.start()
    stores = [None, None]
    for turn, n in enumerate(range(0, model, 512)):
        cols = slice(n, n + 512)
        slot = turn % 2
        g = jnp.dot(coef, targets[:, cols], preferred_element_type=F32).astype(BF16)
        grad_ref[:, cols] = g
        unif = (g.astype(F32) * col[:, 2:3]).astype(BF16)
        scaled = (g.astype(F32) * col[:, 3:4]).astype(BF16)
        g_u = jnp.dot(mixed_t[...], unif, preferred_element_type=F32)
        g_w = jnp.dot(mixed_t[...], scaled, preferred_element_type=F32)
        if stores[slot] is not None:
            for c in stores[slot]:
                c.wait()
        parts_u[slot] = g_u.astype(BF16).reshape(2, 512, 512)
        for to in range(2):
            for q in range(32):
                x, y, zh = q // 8, q // 2 % 4, q % 2
                r = (y * 8 + zh * 4 + x) * 32 + to * 16
                w_at = (r // 64 % 2) * 512 + (r // 128 % 4) * 128 + (r // 512) * 64 + r % 64
                parts_w[slot, to, q * 16 : q * 16 + 16] = g_w[w_at : w_at + 16].astype(BF16)
        stores[slot] = []
        for which, (ref, src) in enumerate(
            (
                (keep_u, parts_u.at[slot, core]),
                (send_u, parts_u.at[slot, 1 - core]),
                (keep_w, parts_w.at[slot, core]),
                (send_w, parts_w.at[slot, 1 - core]),
                (grad_hbm, grad_ref.at[:, cols]),
            )
        ):
            c = pltpu.make_async_copy(src, ref.at[:, cols], p_sem.at[slot, which])
            c.start()
            stores[slot].append(c)
    for pending in stores:
        for c in pending:
            c.wait()
    for c in count_copies:
        c.wait()


def block_call(place, own, par, events, targets, w_out, col, row):
    count, model = events.shape
    width = w_out.shape[0]
    any_spec = pl.BlockSpec(memory_space=pltpu.HBM)
    vmem = pl.BlockSpec(memory_space=pltpu.VMEM)
    part_u = jax.ShapeDtypeStruct((512, model + 128), BF16)
    part_w = jax.ShapeDtypeStruct((512, model), BF16)
    groups = len(own)

    def kernel(place_ref, *refs):
        block_kernel(place_ref, refs[:groups], refs[groups : 2 * groups], *refs[2 * groups :])
    return pl.pallas_call(
        kernel,
        out_shape=(
            jax.ShapeDtypeStruct((count, width), BF16),
            jax.ShapeDtypeStruct((count, model), BF16),
            part_u,
            part_u,
            part_w,
            part_w,
        ),
        in_specs=[pl.BlockSpec(memory_space=pltpu.SMEM)]
        + [any_spec] * (2 * groups + 3)
        + [vmem] * 2,
        out_specs=(any_spec,) * 6,
        scratch_shapes=[
            pltpu.VMEM((4, 4, count, 128), BF16),
            pltpu.VMEM((4, 4, count, 128), BF16),
            pltpu.VMEM((count, model), BF16),
            pltpu.VMEM((count, model), BF16),
            pltpu.VMEM((width, model), BF16),
            pltpu.VMEM((count, width), F32),
            pltpu.VMEM((count, width), BF16),
            pltpu.VMEM((width, count), BF16),
            pltpu.VMEM((count, model), BF16),
            pltpu.VMEM((count, model), BF16),
            pltpu.VMEM((2, 2, 512, 512), BF16),
            pltpu.VMEM((2, 2, 512, 512), BF16),
            pltpu.VMEM((512, 128), BF16),
            pltpu.SemaphoreType.DMA((2, 16)),
            pltpu.SemaphoreType.DMA((2,)),
            pltpu.SemaphoreType.DMA((2, 4, 2)),
            pltpu.SemaphoreType.DMA,
            pltpu.SemaphoreType.DMA((2, 5)),
            pltpu.SemaphoreType.DMA((2,)),
        ],
        cost_estimate=pl.CostEstimate(
            flops=10 * 1024 * MIB, bytes_accessed=24 * MIB, transcendentals=2 * MIB
        ),
        compiler_params=pltpu.CompilerParams(vmem_limit_bytes=60 * MIB),
    )(place, *own, *par, w_out, events, targets, col, row)


def on_device(events, w_uvqk, w_out, targets, item_ids, uniform_flags, lengths, seq_weights):
    count = events.shape[0]
    core = lax.axis_index("c")
    flag = uniform_flags.astype(F32)
    spot = jnp.stack([lax.axis_index(n) for n in ("y", "zh", "x", "c")]).astype(jnp.int32)
    w_out_all = lax.all_gather(w_out, ("y", "zh", "x", "c"), axis=0, tiled=True)
    place = jnp.arange(count, dtype=jnp.int32)
    ends = jnp.cumsum(lengths[0])
    seqid = jnp.sum((place[:, None] >= ends[None, :]).astype(jnp.int32), axis=1)
    member = (seqid[:, None] == jnp.arange(seq_weights.shape[0], dtype=jnp.int32)[None, :]).astype(
        F32
    )
    weight_row = jnp.sum(member * seq_weights[None, :], axis=1) * (1.0 - flag)
    facts = [seqid.astype(F32), item_ids.astype(F32), flag, weight_row]
    row = jnp.stack(facts + [jnp.zeros_like(flag)] * 4)
    col = row.T

    away = lax.ppermute(events, "c", SWAP)
    phases = gather_proj(w_uvqk)
    own, par = [], []
    for (a_pieces, b_pieces), offsets in zip(phases, ORDER):
        mine, for_away = uvqk_call(spot, events, away, a_pieces, b_pieces, offsets)
        own.append(mine)
        par.append(lax.ppermute(for_away, "c", SWAP))
    mixed, grad_out, keep_u, send_u, keep_w, send_w = block_call(
        spot, own, par, events, targets, w_out_all, col, row
    )

    def add(mine, away):
        return (mine.astype(F32) + lax.ppermute(away, "c", SWAP).astype(F32)).astype(BF16)

    model = events.shape[1]
    chip_u, chip_w = add(keep_u, send_u), add(keep_w, send_w)
    part_w = lax.psum_scatter(chip_w, "x", scatter_dimension=0, tiled=True)
    got = lax.all_to_all(chip_u.reshape(64, 8, -1), CHIPS, 0, 0, tiled=True)
    total = jnp.sum(got.astype(F32), axis=0)
    n_unif = 32.0 * total[0, model] + total[0, model + 1]
    unif = jnp.broadcast_to(total[:, :model].astype(BF16)[None], (64, 8, model))
    unif_mine = lax.all_to_all(unif, CHIPS, 0, 0, tiled=True).reshape(512, -1)
    unif_mine, part_w = lax.optimization_barrier((unif_mine, part_w))
    got_w = lax.all_to_all(part_w.reshape(16, 8, model), ("y", "zh", "zl"), 0, 0, tiled=True)
    weighted_grad = jnp.sum(got_w.astype(F32), axis=0) / (jnp.float32(count * 128) - n_unif)
    unif_away = lax.ppermute(unif_mine, "c", SWAP)
    mixed_mine = lax.dynamic_slice_in_dim(mixed, core * 512, 512, 1)
    mixed_away = lax.dynamic_slice_in_dim(mixed, (1 - core) * 512, 512, 1)
    proj_mine = jnp.dot(grad_out, unif_mine.T, preferred_element_type=F32)
    proj_away = jnp.dot(grad_out, unif_away.T, preferred_element_type=F32)
    per_row = jnp.sum(mixed_mine.astype(F32) * proj_mine, axis=1) + jnp.sum(
        mixed_away.astype(F32) * proj_away, axis=1
    )
    per_row = -per_row * (1.0 - flag) / n_unif
    hyper = jnp.sum(member * per_row[:, None], axis=0)
    return (hyper, weighted_grad)


def solution(mesh):
    fine = Mesh(mesh.devices.reshape(4, 2, 4, 2, 2), AXES)
    dp = ("y", "zh", "x", "c")
    return jax.shard_map(
        on_device,
        mesh=fine,
        in_specs=(
            P(AXES, None),
            P(None, dp),
            P(dp, None),
            P(AXES, None),
            P(AXES),
            P(AXES),
            P(AXES, None),
            P(AXES),
        ),
        out_specs=(P(AXES), P(AXES, None)),
        check_vma=False,
    )
```

```python
import jax
import jax.numpy as jnp
from jax import lax
from jax.experimental import pallas as pl
from jax.experimental.pallas import tpu as pltpu
from jax.sharding import Mesh
from jax.sharding import PartitionSpec as P

HEADS = 8
DH = 128
AXES = ("y", "zh", "x", "c", "zl")
CHIPS = ("y", "zh", "x", "zl")
SWAP = [(0, 1), (1, 0)]
ACROSS = [(0, 3), (3, 0), (1, 2), (2, 1)]
ORDER = (
    ((0, 0), (0, 1), (0, 3), (1, 0), (1, 1), (1, 3), (3, 0), (3, 1), (3, 3)),
    ((0, 2), (1, 2), (3, 2), (2, 0), (2, 1), (2, 3), (2, 2)),
)
F32 = jnp.float32
BF16 = jnp.bfloat16
MIB = 1024 * 1024
NT = (((1,), (1,)), ((), ()))
NN = (((1,), (0,)), ((), ()))


def hop(array, axis, step):
    return lax.ppermute(array, axis, [(i, (i + step) % 4) for i in range(4)])


def first_rings(a, a_axis, b, b_axis, cut):
    got = lax.optimization_barrier(
        (hop(a, a_axis, 1), hop(a, a_axis, -1), hop(b, b_axis, 1), hop(b, b_axis, -1))
    )
    a_below, a_above, b_below, b_above = got
    far = (
        hop(a_below[:cut], a_axis, 1),
        hop(a_above[cut:], a_axis, -1),
        hop(b_below[:cut], b_axis, 1),
        hop(b_above[cut:], b_axis, -1),
    )
    return (a, a_above, far[:2], a_below), (b, b_above, far[2:], b_below)


def last_rings(a, b):
    one = (hop(a[0], "y", 1), hop(a[1], "y", -1), hop(b[0], "x", 1), hop(b[1], "x", -1))
    two = (hop(a[1], "y", 1), hop(a[0], "y", -1), hop(b[1], "x", 1), hop(b[0], "x", -1))
    one, two = lax.optimization_barrier((one, two))
    a_near = (a, (two[1], one[1]), None, (one[0], two[0]))
    b_near = (b, (two[3], one[3]), None, (one[2], two[2]))
    a_far = (hop(one[0], "y", 1), hop(one[1], "y", -1))
    b_far = (hop(one[2], "x", 1), hop(one[3], "x", -1))
    last = (a_near[:2] + (a_far, a_near[3]), b_near[:2] + (b_far, b_near[3]))
    return (a_near, b_near), last


def gather_proj(w_uvqk):
    half = w_uvqk.shape[0] // 2
    rows = w_uvqk.T
    other = lax.ppermute(rows, ("zh", "zl"), ACROSS)
    both = jnp.stack([rows, other])
    a_line, b_line = first_rings(both[:, :, :half], "x", both[:, :, half:], "y", 1)

    def halves(pieces):
        own, above, far, below = pieces
        return jnp.stack([own, above]), jnp.stack([jnp.concatenate(far, 0), below])

    return last_rings(halves(a_line), halves(b_line))


def place_of(pieces, major, minor):
    return pieces[major][minor // 2], minor % 2


def uvqk_call(place, own, away, a_pieces, b_pieces, offsets):
    count, model = own.shape
    half = model // 2
    arrays, steps = [], []

    def seat(array):
        for i, seen in enumerate(arrays):
            if seen is array:
                return i
        arrays.append(array)
        return len(arrays) - 1

    for y_off, x_off in offsets:
        a_from, a_at = place_of(a_pieces, y_off, x_off)
        b_from, b_at = place_of(b_pieces, x_off, y_off)
        steps.append((y_off, x_off, (seat(a_from), a_at), (seat(b_from), b_at)))
    near = len(arrays)

    def kernel(place_ref, own_ref, away_ref, *refs):
        weights = refs[:near]
        out_own, out_away, w_buf, o_buf, w_sem, o_sem = refs[near:]
        loads = []
        for n, (_, _, a, b) in enumerate(steps):
            for side, (src, index) in enumerate((a, b)):
                for z_off in range(2):
                    z_at = place_ref[1] if z_off == 0 else 1 - place_ref[1]
                    c = pltpu.make_async_copy(
                        weights[src].at[index, z_off],
                        w_buf.at[n, z_at, :, side * half : (side + 1) * half],
                        w_sem.at[n, side, z_off],
                    )
                    c.start()
                    loads.append(c)
        stores = []
        for first in range(0, len(steps), 2):
            group = range(first, min(first + 2, len(steps)))
            for n in group:
                for c in loads[4 * n : 4 * n + 4]:
                    c.wait()
            rows = w_buf[first : first + len(group)].reshape(len(group) * 128, model)
            for who, (ev_ref, out_ref) in enumerate(((own_ref, out_own), (away_ref, out_away))):
                acc = lax.dot_general(ev_ref[...], rows, NT, preferred_element_type=F32)
                act = (0.5 * acc * (1.0 + jnp.tanh(0.5 * acc))).astype(BF16)
                for i, n in enumerate(group):
                    o_buf[n, who] = act[:, i * 128 : (i + 1) * 128]
                    c = pltpu.make_async_copy(o_buf.at[n, who], out_ref.at[n], o_sem.at[n, who])
                    c.start()
                    stores.append(c)
        for c in stores:
            c.wait()

    any_spec = pl.BlockSpec(memory_space=pltpu.HBM)
    vmem = pl.BlockSpec(memory_space=pltpu.VMEM)
    shape = jax.ShapeDtypeStruct((len(steps), count, 128), BF16)
    return pl.pallas_call(
        kernel,
        out_shape=(shape, shape),
        in_specs=[pl.BlockSpec(memory_space=pltpu.SMEM), vmem, vmem]
        + [any_spec] * near,
        out_specs=(any_spec, any_spec),
        scratch_shapes=[
            pltpu.VMEM((len(steps), 2, 64, model), BF16),
            pltpu.VMEM((len(steps), 2, count, 128), BF16),
            pltpu.SemaphoreType.DMA((len(steps), 2, 2)),
            pltpu.SemaphoreType.DMA((len(steps), 2)),
        ],
        cost_estimate=pl.CostEstimate(
            flops=4 * count * model * 128 * len(steps),
            bytes_accessed=model * 256 * len(steps),
            transcendentals=2 * count * 128 * len(steps),
        ),
        compiler_params=pltpu.CompilerParams(vmem_limit_bytes=60 * MIB),
    )(place, own, away, *arrays)


def silu(x):
    return 0.5 * x * (1.0 + jnp.tanh(0.5 * x))


def sigmoid(x):
    return 1.0 / (1.0 + jnp.exp(-x))


def block_kernel(
    place, own_hbm, par_hbm, w_out, events_hbm, targets_hbm, col, row, mixed_hbm, turned_hbm, grad_hbm, keep_u,
    send_u, own, par, events, targets, w_buf, attn, mixed_ref, mixed_t, outs, grad_ref,
    parts_u, digits, b_sem, e_sem, w_sem, m_sem, p_sem, d_sem
):
    core = place[3]
    count, model = events.shape
    tile = count // 4
    blocks = []
    for who, (groups, held) in enumerate(((own_hbm, own), (par_hbm, par))):
        done = 0
        for offsets, ref in zip(ORDER, groups):
            for n, (y_off, x_off) in enumerate(offsets):
                y_at, x_at = lax.rem(place[0] + y_off, 4), lax.rem(place[2] + x_off, 4)
                c = pltpu.make_async_copy(ref.at[n], held.at[y_at, x_at], b_sem.at[who, done])
                c.start()
                blocks.append(c)
                done += 1
    loads = [
        pltpu.make_async_copy(events_hbm, events, e_sem.at[0]),
        pltpu.make_async_copy(targets_hbm, targets, e_sem.at[1]),
    ]
    for c in loads:
        c.start()
    for cls in range(2):
        for x in range(4):
            for zh in range(2):
                c = pltpu.make_async_copy(
                    w_out.at[zh * 512 + x * 128 + cls * 64 : zh * 512 + x * 128 + cls * 64 + 64],
                    w_buf.at[cls * 512 + x * 128 + zh * 64 : cls * 512 + x * 128 + zh * 64 + 64],
                    w_sem.at[cls, x, zh],
                )
                c.start()
                loads.append(c)
    lane = lax.broadcasted_iota(jnp.int32, (tile, 256), 1)
    low = lax.rem(lane, 128) < 64
    scale = 1.0 / DH**0.5
    for c in blocks:
        c.wait()
    for i in range(4):
        lo, hi = max(0, (i - 1) * tile), (i + 1) * tile
        here = slice(i * tile, hi)
        at_i = i * tile + lax.broadcasted_iota(jnp.int32, (tile, hi - lo), 0)
        at_j = lo + lax.broadcasted_iota(jnp.int32, (tile, hi - lo), 1)
        allowed = (col[here, 0:1] == row[0:1, lo:hi]) & (at_j <= at_i)
        for x in range(4):
            q = jnp.concatenate([own[2, x, here], par[2, x, here]], 1)
            k = jnp.concatenate([own[3, x, lo:hi], par[3, x, lo:hi]], 1)
            v = jnp.concatenate([own[1, x, lo:hi], par[1, x, lo:hi]], 1)
            halves = []
            for pick in (low, ~low):
                qz = jnp.where(pick, q, jnp.zeros_like(q))
                s = lax.dot_general(qz, k, NT, preferred_element_type=F32) * scale
                p = jnp.where(allowed, silu(s) * (1.0 / 128.0), 0.0).astype(BF16)
                halves.append(lax.dot_general(p, v, NN, preferred_element_type=F32))
            o = jnp.where(low, halves[0], halves[1])
            attn[here, x * 128 : (x + 1) * 128] = o[:, :128]
            attn[here, 512 + x * 128 : 512 + (x + 1) * 128] = o[:, 128:]
        a = attn[here, :]
        mean = jnp.mean(a, axis=1, keepdims=True)
        a = a - mean
        a = a * lax.rsqrt(jnp.mean(a * a, axis=1, keepdims=True) + 1e-05)
        for side, src in ((core, own), (1 - core, par)):
            base = 0 if src is own else 512
            u = jnp.concatenate([src[0, x, here] for x in range(4)], 1).astype(F32)
            m = (a[:, base : base + 512] * u).astype(BF16)
            mixed_ref[here, pl.ds(pl.multiple_of(side * 512, 512), 512)] = m
    for c in loads:
        c.wait()
    for n in range(0, model, 512):
        cols = slice(n, n + 512)
        s = jnp.dot(mixed_ref[...], w_buf[:, cols], preferred_element_type=F32)
        outs[:, cols] = (events[:, cols].astype(F32) + s).astype(BF16)
    mixed_t[...] = mixed_ref[...].T
    count_copies = [
        pltpu.make_async_copy(mixed_ref, mixed_hbm, m_sem.at[0]),
        pltpu.make_async_copy(mixed_t, turned_hbm, m_sem.at[1]),
    ]
    scores = lax.dot_general(outs[...], targets[...], NT, preferred_element_type=F32)
    at_i = lax.broadcasted_iota(jnp.int32, (count, count), 0)
    at_j = lax.broadcasted_iota(jnp.int32, (count, count), 1)
    other = col[:, 1:2] != row[1:2, :]
    coef = sigmoid(jnp.where(at_i == at_j, -scores, scores))
    coef = jnp.where(
        at_i == at_j, -coef, jnp.where(other, coef * (1.0 / count), 0.0)
    ).astype(BF16)
    flagged = jnp.sum(row[2:3, :], axis=1, keepdims=True)
    high = jnp.floor(flagged * (1.0 / 32.0))
    at = lax.broadcasted_iota(jnp.int32, (512, 128), 1)
    digits[...] = jnp.where(at == 0, high, jnp.where(at == 1, flagged - 32.0 * high, 0.0)).astype(BF16)
    count_copies += [
        pltpu.make_async_copy(digits, ref.at[:, model : model + 128], d_sem.at[i])
        for i, ref in enumerate((keep_u, send_u))
    ]
    for c in count_copies:
        c.start()
    stores = [None, None]
    for turn, n in enumerate(range(0, model, 512)):
        cols = slice(n, n + 512)
        slot = turn % 2
        g = jnp.dot(coef, targets[:, cols], preferred_element_type=F32).astype(BF16)
        grad_ref[:, cols] = g
        unif = (g.astype(F32) * col[:, 2:3]).astype(BF16)
        g_u = jnp.dot(mixed_t[...], unif, preferred_element_type=F32)
        if stores[slot] is not None:
            for c in stores[slot]:
                c.wait()
        parts_u[slot] = g_u.astype(BF16).reshape(2, 512, 512)
        stores[slot] = []
        for which, (ref, src) in enumerate(
            (
                (keep_u, parts_u.at[slot, core]),
                (send_u, parts_u.at[slot, 1 - core]),
                (grad_hbm, grad_ref.at[:, cols]),
            )
        ):
            c = pltpu.make_async_copy(src, ref.at[:, cols], p_sem.at[slot, which])
            c.start()
            stores[slot].append(c)
    for pending in stores:
        for c in pending:
            c.wait()
    for c in count_copies:
        c.wait()


def block_call(place, own, par, events, targets, w_out, col, row):
    count, model = events.shape
    width = w_out.shape[0]
    any_spec = pl.BlockSpec(memory_space=pltpu.HBM)
    vmem = pl.BlockSpec(memory_space=pltpu.VMEM)
    part_u = jax.ShapeDtypeStruct((512, model + 128), BF16)
    groups = len(own)

    def kernel(place_ref, *refs):
        block_kernel(place_ref, refs[:groups], refs[groups : 2 * groups], *refs[2 * groups :])
    return pl.pallas_call(
        kernel,
        out_shape=(
            jax.ShapeDtypeStruct((count, width), BF16),
            jax.ShapeDtypeStruct((width, count), BF16),
            jax.ShapeDtypeStruct((count, model), BF16),
            part_u,
            part_u,
        ),
        in_specs=[pl.BlockSpec(memory_space=pltpu.SMEM)]
        + [any_spec] * (2 * groups + 3)
        + [vmem] * 2,
        out_specs=(any_spec,) * 5,
        scratch_shapes=[
            pltpu.VMEM((4, 4, count, 128), BF16),
            pltpu.VMEM((4, 4, count, 128), BF16),
            pltpu.VMEM((count, model), BF16),
            pltpu.VMEM((count, model), BF16),
            pltpu.VMEM((width, model), BF16),
            pltpu.VMEM((count, width), F32),
            pltpu.VMEM((count, width), BF16),
            pltpu.VMEM((width, count), BF16),
            pltpu.VMEM((count, model), BF16),
            pltpu.VMEM((count, model), BF16),
            pltpu.VMEM((2, 2, 512, 512), BF16),
            pltpu.VMEM((512, 128), BF16),
            pltpu.SemaphoreType.DMA((2, 16)),
            pltpu.SemaphoreType.DMA((2,)),
            pltpu.SemaphoreType.DMA((2, 4, 2)),
            pltpu.SemaphoreType.DMA((2,)),
            pltpu.SemaphoreType.DMA((2, 3)),
            pltpu.SemaphoreType.DMA((2,)),
        ],
        cost_estimate=pl.CostEstimate(
            flops=10 * 1024 * MIB, bytes_accessed=24 * MIB, transcendentals=2 * MIB
        ),
        compiler_params=pltpu.CompilerParams(vmem_limit_bytes=60 * MIB),
    )(place, *own, *par, w_out, events, targets, col, row)


def weighted_kernel(place, mixed_t, grad, col, keep_w, send_w, parts_w, p_sem):
    core = place[3]
    stores = [None, None]
    for turn, n in enumerate(range(0, grad.shape[1], 512)):
        cols = slice(n, n + 512)
        slot = turn % 2
        scaled = (grad[:, cols].astype(F32) * col[:, 3:4]).astype(BF16)
        g_w = jnp.dot(mixed_t[...], scaled, preferred_element_type=F32)
        if stores[slot] is not None:
            for c in stores[slot]:
                c.wait()
        for to in range(2):
            for q in range(32):
                x, y, zh = q // 8, q // 2 % 4, q % 2
                r = (y * 8 + zh * 4 + x) * 32 + to * 16
                w_at = (r // 64 % 2) * 512 + (r // 128 % 4) * 128 + (r // 512) * 64 + r % 64
                parts_w[slot, to, q * 16 : q * 16 + 16] = g_w[w_at : w_at + 16].astype(BF16)
        stores[slot] = []
        for which, (ref, side) in enumerate(((keep_w, core), (send_w, 1 - core))):
            c = pltpu.make_async_copy(
                parts_w.at[slot, side], ref.at[:, cols], p_sem.at[slot, which]
            )
            c.start()
            stores[slot].append(c)
    for pending in stores:
        for c in pending:
            c.wait()


def weighted_call(place, mixed_t, grad, col):
    any_spec = pl.BlockSpec(memory_space=pltpu.HBM)
    vmem = pl.BlockSpec(memory_space=pltpu.VMEM)
    part = jax.ShapeDtypeStruct((512, grad.shape[1]), BF16)
    return pl.pallas_call(
        weighted_kernel,
        out_shape=(part, part),
        in_specs=[pl.BlockSpec(memory_space=pltpu.SMEM), vmem, vmem, vmem],
        out_specs=(any_spec, any_spec),
        scratch_shapes=[
            pltpu.VMEM((2, 2, 512, 512), BF16),
            pltpu.SemaphoreType.DMA((2, 2)),
        ],
        cost_estimate=pl.CostEstimate(
            flops=2 * 1024 * MIB, bytes_accessed=8 * MIB, transcendentals=0
        ),
        compiler_params=pltpu.CompilerParams(vmem_limit_bytes=40 * MIB),
    )(place, mixed_t, grad, col)


def on_device(events, w_uvqk, w_out, targets, item_ids, uniform_flags, lengths, seq_weights):
    count = events.shape[0]
    core = lax.axis_index("c")
    flag = uniform_flags.astype(F32)
    spot = jnp.stack([lax.axis_index(n) for n in ("y", "zh", "x", "c")]).astype(jnp.int32)
    w_out_all = lax.all_gather(w_out, ("y", "zh", "x", "c"), axis=0, tiled=True)
    place = jnp.arange(count, dtype=jnp.int32)
    ends = jnp.cumsum(lengths[0])
    seqid = jnp.sum((place[:, None] >= ends[None, :]).astype(jnp.int32), axis=1)
    member = (seqid[:, None] == jnp.arange(seq_weights.shape[0], dtype=jnp.int32)[None, :]).astype(
        F32
    )
    weight_row = jnp.sum(member * seq_weights[None, :], axis=1) * (1.0 - flag)
    facts = [seqid.astype(F32), item_ids.astype(F32), flag, weight_row]
    row = jnp.stack(facts + [jnp.zeros_like(flag)] * 4)
    col = row.T

    away = lax.ppermute(events, "c", SWAP)
    phases = gather_proj(w_uvqk)
    own, par = [], []
    for (a_pieces, b_pieces), offsets in zip(phases, ORDER):
        mine, for_away = uvqk_call(spot, events, away, a_pieces, b_pieces, offsets)
        own.append(mine)
        par.append(lax.ppermute(for_away, "c", SWAP))
    mixed, mixed_t, grad_out, keep_u, send_u = block_call(
        spot, own, par, events, targets, w_out_all, col, row
    )

    def add(mine, away):
        return (mine.astype(F32) + lax.ppermute(away, "c", SWAP).astype(F32)).astype(BF16)

    model = events.shape[1]
    chip_u, grad_later = lax.optimization_barrier((add(keep_u, send_u), grad_out))
    chip_w = add(*weighted_call(spot, mixed_t, grad_later, col))
    part_w = lax.psum_scatter(chip_w, "x", scatter_dimension=0, tiled=True)
    got = lax.all_to_all(chip_u.reshape(64, 8, -1), CHIPS, 0, 0, tiled=True)
    total = jnp.sum(got.astype(F32), axis=0)
    n_unif = 32.0 * total[0, model] + total[0, model + 1]
    unif = jnp.broadcast_to(total[:, :model].astype(BF16)[None], (64, 8, model))
    unif_mine = lax.all_to_all(unif, CHIPS, 0, 0, tiled=True).reshape(512, -1)
    unif_mine, part_w = lax.optimization_barrier((unif_mine, part_w))
    got_w = lax.all_to_all(part_w.reshape(16, 8, model), ("y", "zh", "zl"), 0, 0, tiled=True)
    unif_away = lax.ppermute(unif_mine, "c", SWAP)
    mixed_mine = lax.dynamic_slice_in_dim(mixed, core * 512, 512, 1)
    mixed_away = lax.dynamic_slice_in_dim(mixed, (1 - core) * 512, 512, 1)
    proj_mine = jnp.dot(grad_out, unif_mine.T, preferred_element_type=F32)
    proj_away = jnp.dot(grad_out, unif_away.T, preferred_element_type=F32)
    per_row = jnp.sum(mixed_mine.astype(F32) * proj_mine, axis=1) + jnp.sum(
        mixed_away.astype(F32) * proj_away, axis=1
    )
    per_row = -per_row * (1.0 - flag) / n_unif
    hyper = jnp.sum(member * per_row[:, None], axis=0)
    hyper, got_w = lax.optimization_barrier((hyper, got_w))
    weighted_grad = jnp.sum(got_w.astype(F32), axis=0) / (jnp.float32(count * 128) - n_unif)
    return (hyper, weighted_grad)


def solution(mesh):
    fine = Mesh(mesh.devices.reshape(4, 2, 4, 2, 2), AXES)
    dp = ("y", "zh", "x", "c")
    return jax.shard_map(
        on_device,
        mesh=fine,
        in_specs=(
            P(AXES, None),
            P(None, dp),
            P(dp, None),
            P(AXES, None),
            P(AXES),
            P(AXES),
            P(AXES, None),
            P(AXES),
        ),
        out_specs=(P(AXES), P(AXES, None)),
        check_vma=False,
    )
```

```python
import jax
import jax.numpy as jnp
from jax import lax
from jax.experimental import pallas as pl
from jax.experimental.pallas import tpu as pltpu
from jax.sharding import Mesh
from jax.sharding import PartitionSpec as P

HEADS = 8
DH = 128
AXES = ("y", "zh", "x", "c", "zl")
CHIPS = ("y", "zh", "x", "zl")
SWAP = [(0, 1), (1, 0)]
ACROSS = [(0, 3), (3, 0), (1, 2), (2, 1)]
ORDER = (
    ((0, 0), (0, 1), (0, 3), (1, 0), (1, 1), (1, 3), (3, 0), (3, 1), (3, 3)),
    ((0, 2), (1, 2), (3, 2), (2, 0), (2, 1), (2, 3), (2, 2)),
)
F32 = jnp.float32
BF16 = jnp.bfloat16
MIB = 1024 * 1024
NT = (((1,), (1,)), ((), ()))
NN = (((1,), (0,)), ((), ()))


def hop(array, axis, step):
    return lax.ppermute(array, axis, [(i, (i + step) % 4) for i in range(4)])


def first_rings(a, a_axis, b, b_axis, cut, also):
    got, also = lax.optimization_barrier(
        ((hop(a, a_axis, 1), hop(a, a_axis, -1), hop(b, b_axis, 1), hop(b, b_axis, -1)), also)
    )
    a_below, a_above, b_below, b_above = got
    far = (
        hop(a_below[:cut], a_axis, 1),
        hop(a_above[cut:], a_axis, -1),
        hop(b_below[:cut], b_axis, 1),
        hop(b_above[cut:], b_axis, -1),
    )
    return (a, a_above, far[:2], a_below), (b, b_above, far[2:], b_below), also


def last_rings(a, b):
    one = (hop(a[0], "y", 1), hop(a[1], "y", -1), hop(b[0], "x", 1), hop(b[1], "x", -1))
    two = (hop(a[1], "y", 1), hop(a[0], "y", -1), hop(b[1], "x", 1), hop(b[0], "x", -1))
    one, two = lax.optimization_barrier((one, two))
    a_near = (a, (two[1], one[1]), None, (one[0], two[0]))
    b_near = (b, (two[3], one[3]), None, (one[2], two[2]))
    a_far = (hop(one[0], "y", 1), hop(one[1], "y", -1))
    b_far = (hop(one[2], "x", 1), hop(one[3], "x", -1))
    last = (a_near[:2] + (a_far, a_near[3]), b_near[:2] + (b_far, b_near[3]))
    return (a_near, b_near), last


def gather_proj(w_uvqk, also):
    half = w_uvqk.shape[0] // 2
    rows = w_uvqk.T
    other = lax.ppermute(rows, ("zh", "zl"), ACROSS)
    both = jnp.stack([rows, other])
    a_line, b_line, also = first_rings(both[:, :, :half], "x", both[:, :, half:], "y", 1, also)

    def halves(pieces):
        own, above, far, below = pieces
        return jnp.stack([own, above]), jnp.stack([jnp.concatenate(far, 0), below])

    return last_rings(halves(a_line), halves(b_line)), also


def place_of(pieces, major, minor):
    return pieces[major][minor // 2], minor % 2


def uvqk_call(place, own, away, a_pieces, b_pieces, offsets):
    count, model = own.shape
    half = model // 2
    arrays, steps = [], []

    def seat(array):
        for i, seen in enumerate(arrays):
            if seen is array:
                return i
        arrays.append(array)
        return len(arrays) - 1

    for y_off, x_off in offsets:
        a_from, a_at = place_of(a_pieces, y_off, x_off)
        b_from, b_at = place_of(b_pieces, x_off, y_off)
        steps.append((y_off, x_off, (seat(a_from), a_at), (seat(b_from), b_at)))
    near = len(arrays)

    def kernel(place_ref, own_ref, away_ref, *refs):
        weights = refs[:near]
        out_own, out_away, w_buf, o_buf, w_sem, o_sem = refs[near:]
        loads = []
        for n, (_, _, a, b) in enumerate(steps):
            for side, (src, index) in enumerate((a, b)):
                for z_off in range(2):
                    z_at = place_ref[1] if z_off == 0 else 1 - place_ref[1]
                    c = pltpu.make_async_copy(
                        weights[src].at[index, z_off],
                        w_buf.at[n, z_at, :, side * half : (side + 1) * half],
                        w_sem.at[n, side, z_off],
                    )
                    c.start()
                    loads.append(c)
        stores = []
        for first in range(0, len(steps), 2):
            group = range(first, min(first + 2, len(steps)))
            for n in group:
                for c in loads[4 * n : 4 * n + 4]:
                    c.wait()
            rows = w_buf[first : first + len(group)].reshape(len(group) * 128, model)
            for who, (ev_ref, out_ref) in enumerate(((own_ref, out_own), (away_ref, out_away))):
                acc = lax.dot_general(ev_ref[...], rows, NT, preferred_element_type=F32)
                act = (0.5 * acc * (1.0 + jnp.tanh(0.5 * acc))).astype(BF16)
                for i, n in enumerate(group):
                    o_buf[n, who] = act[:, i * 128 : (i + 1) * 128]
                    c = pltpu.make_async_copy(o_buf.at[n, who], out_ref.at[n], o_sem.at[n, who])
                    c.start()
                    stores.append(c)
        for c in stores:
            c.wait()

    any_spec = pl.BlockSpec(memory_space=pltpu.HBM)
    vmem = pl.BlockSpec(memory_space=pltpu.VMEM)
    shape = jax.ShapeDtypeStruct((len(steps), count, 128), BF16)
    return pl.pallas_call(
        kernel,
        out_shape=(shape, shape),
        in_specs=[pl.BlockSpec(memory_space=pltpu.SMEM), vmem, vmem]
        + [any_spec] * near,
        out_specs=(any_spec, any_spec),
        scratch_shapes=[
            pltpu.VMEM((len(steps), 2, 64, model), BF16),
            pltpu.VMEM((len(steps), 2, count, 128), BF16),
            pltpu.SemaphoreType.DMA((len(steps), 2, 2)),
            pltpu.SemaphoreType.DMA((len(steps), 2)),
        ],
        cost_estimate=pl.CostEstimate(
            flops=4 * count * model * 128 * len(steps),
            bytes_accessed=model * 256 * len(steps),
            transcendentals=2 * count * 128 * len(steps),
        ),
        compiler_params=pltpu.CompilerParams(vmem_limit_bytes=60 * MIB),
    )(place, own, away, *arrays)


def silu(x):
    return 0.5 * x * (1.0 + jnp.tanh(0.5 * x))


def sigmoid(x):
    return 1.0 / (1.0 + jnp.exp(-x))


def block_kernel(
    place, own_hbm, par_hbm, w_out, events_hbm, targets_hbm, col, row, mixed_hbm, turned_hbm, grad_hbm, keep_u,
    send_u, own, par, events, targets, w_buf, attn, mixed_ref, mixed_t, outs, grad_ref,
    parts_u, digits, b_sem, e_sem, w_sem, m_sem, p_sem, d_sem
):
    core = place[3]
    count, model = events.shape
    tile = count // 4
    blocks = []
    for who, (groups, held) in enumerate(((own_hbm, own), (par_hbm, par))):
        done = 0
        for offsets, ref in zip(ORDER, groups):
            for n, (y_off, x_off) in enumerate(offsets):
                y_at, x_at = lax.rem(place[0] + y_off, 4), lax.rem(place[2] + x_off, 4)
                c = pltpu.make_async_copy(ref.at[n], held.at[y_at, x_at], b_sem.at[who, done])
                c.start()
                blocks.append(c)
                done += 1
    loads = [
        pltpu.make_async_copy(events_hbm, events, e_sem.at[0]),
        pltpu.make_async_copy(targets_hbm, targets, e_sem.at[1]),
    ]
    for c in loads:
        c.start()
    for cls in range(2):
        for x in range(4):
            for zh in range(2):
                c = pltpu.make_async_copy(
                    w_out.at[zh * 512 + x * 128 + cls * 64 : zh * 512 + x * 128 + cls * 64 + 64],
                    w_buf.at[cls * 512 + x * 128 + zh * 64 : cls * 512 + x * 128 + zh * 64 + 64],
                    w_sem.at[cls, x, zh],
                )
                c.start()
                loads.append(c)
    lane = lax.broadcasted_iota(jnp.int32, (tile, 256), 1)
    low = lax.rem(lane, 128) < 64
    scale = 1.0 / DH**0.5
    for c in blocks:
        c.wait()
    for i in range(4):
        lo, hi = max(0, (i - 1) * tile), (i + 1) * tile
        here = slice(i * tile, hi)
        at_i = i * tile + lax.broadcasted_iota(jnp.int32, (tile, hi - lo), 0)
        at_j = lo + lax.broadcasted_iota(jnp.int32, (tile, hi - lo), 1)
        allowed = (col[here, 0:1] == row[0:1, lo:hi]) & (at_j <= at_i)
        for x in range(4):
            q = jnp.concatenate([own[2, x, here], par[2, x, here]], 1)
            k = jnp.concatenate([own[3, x, lo:hi], par[3, x, lo:hi]], 1)
            v = jnp.concatenate([own[1, x, lo:hi], par[1, x, lo:hi]], 1)
            halves = []
            for pick in (low, ~low):
                qz = jnp.where(pick, q, jnp.zeros_like(q))
                s = lax.dot_general(qz, k, NT, preferred_element_type=F32) * scale
                p = jnp.where(allowed, silu(s) * (1.0 / 128.0), 0.0).astype(BF16)
                halves.append(lax.dot_general(p, v, NN, preferred_element_type=F32))
            o = jnp.where(low, halves[0], halves[1])
            attn[here, x * 128 : (x + 1) * 128] = o[:, :128]
            attn[here, 512 + x * 128 : 512 + (x + 1) * 128] = o[:, 128:]
        a = attn[here, :]
        mean = jnp.mean(a, axis=1, keepdims=True)
        a = a - mean
        a = a * lax.rsqrt(jnp.mean(a * a, axis=1, keepdims=True) + 1e-05)
        for side, src in ((core, own), (1 - core, par)):
            base = 0 if src is own else 512
            u = jnp.concatenate([src[0, x, here] for x in range(4)], 1).astype(F32)
            m = (a[:, base : base + 512] * u).astype(BF16)
            mixed_ref[here, pl.ds(pl.multiple_of(side * 512, 512), 512)] = m
    for c in loads:
        c.wait()
    for n in range(0, model, 512):
        cols = slice(n, n + 512)
        s = jnp.dot(mixed_ref[...], w_buf[:, cols], preferred_element_type=F32)
        outs[:, cols] = (events[:, cols].astype(F32) + s).astype(BF16)
    mixed_t[...] = mixed_ref[...].T
    count_copies = [
        pltpu.make_async_copy(mixed_ref, mixed_hbm, m_sem.at[0]),
        pltpu.make_async_copy(mixed_t, turned_hbm, m_sem.at[1]),
    ]
    scores = lax.dot_general(outs[...], targets[...], NT, preferred_element_type=F32)
    at_i = lax.broadcasted_iota(jnp.int32, (count, count), 0)
    at_j = lax.broadcasted_iota(jnp.int32, (count, count), 1)
    other = col[:, 1:2] != row[1:2, :]
    coef = sigmoid(jnp.where(at_i == at_j, -scores, scores))
    coef = jnp.where(
        at_i == at_j, -coef, jnp.where(other, coef * (1.0 / count), 0.0)
    ).astype(BF16)
    flagged = jnp.sum(row[2:3, :], axis=1, keepdims=True)
    high = jnp.floor(flagged * (1.0 / 32.0))
    at = lax.broadcasted_iota(jnp.int32, (512, 128), 1)
    digits[...] = jnp.where(at == 0, high, jnp.where(at == 1, flagged - 32.0 * high, 0.0)).astype(BF16)
    count_copies += [
        pltpu.make_async_copy(digits, ref.at[:, model : model + 128], d_sem.at[i])
        for i, ref in enumerate((keep_u, send_u))
    ]
    for c in count_copies:
        c.start()
    stores = [None, None]
    for turn, n in enumerate(range(0, model, 512)):
        cols = slice(n, n + 512)
        slot = turn % 2
        g = jnp.dot(coef, targets[:, cols], preferred_element_type=F32).astype(BF16)
        grad_ref[:, cols] = g
        unif = (g.astype(F32) * col[:, 2:3]).astype(BF16)
        g_u = jnp.dot(mixed_t[...], unif, preferred_element_type=F32)
        if stores[slot] is not None:
            for c in stores[slot]:
                c.wait()
        parts_u[slot] = g_u.astype(BF16).reshape(2, 512, 512)
        stores[slot] = []
        for which, (ref, src) in enumerate(
            (
                (keep_u, parts_u.at[slot, core]),
                (send_u, parts_u.at[slot, 1 - core]),
                (grad_hbm, grad_ref.at[:, cols]),
            )
        ):
            c = pltpu.make_async_copy(src, ref.at[:, cols], p_sem.at[slot, which])
            c.start()
            stores[slot].append(c)
    for pending in stores:
        for c in pending:
            c.wait()
    for c in count_copies:
        c.wait()


def block_call(place, own, par, events, targets, w_out, col, row):
    count, model = events.shape
    width = w_out.shape[0]
    any_spec = pl.BlockSpec(memory_space=pltpu.HBM)
    vmem = pl.BlockSpec(memory_space=pltpu.VMEM)
    part_u = jax.ShapeDtypeStruct((512, model + 128), BF16)
    groups = len(own)

    def kernel(place_ref, *refs):
        block_kernel(place_ref, refs[:groups], refs[groups : 2 * groups], *refs[2 * groups :])
    return pl.pallas_call(
        kernel,
        out_shape=(
            jax.ShapeDtypeStruct((count, width), BF16),
            jax.ShapeDtypeStruct((width, count), BF16),
            jax.ShapeDtypeStruct((count, model), BF16),
            part_u,
            part_u,
        ),
        in_specs=[pl.BlockSpec(memory_space=pltpu.SMEM)]
        + [any_spec] * (2 * groups + 3)
        + [vmem] * 2,
        out_specs=(any_spec,) * 5,
        scratch_shapes=[
            pltpu.VMEM((4, 4, count, 128), BF16),
            pltpu.VMEM((4, 4, count, 128), BF16),
            pltpu.VMEM((count, model), BF16),
            pltpu.VMEM((count, model), BF16),
            pltpu.VMEM((width, model), BF16),
            pltpu.VMEM((count, width), F32),
            pltpu.VMEM((count, width), BF16),
            pltpu.VMEM((width, count), BF16),
            pltpu.VMEM((count, model), BF16),
            pltpu.VMEM((count, model), BF16),
            pltpu.VMEM((2, 2, 512, 512), BF16),
            pltpu.VMEM((512, 128), BF16),
            pltpu.SemaphoreType.DMA((2, 16)),
            pltpu.SemaphoreType.DMA((2,)),
            pltpu.SemaphoreType.DMA((2, 4, 2)),
            pltpu.SemaphoreType.DMA((2,)),
            pltpu.SemaphoreType.DMA((2, 3)),
            pltpu.SemaphoreType.DMA((2,)),
        ],
        cost_estimate=pl.CostEstimate(
            flops=10 * 1024 * MIB, bytes_accessed=24 * MIB, transcendentals=2 * MIB
        ),
        compiler_params=pltpu.CompilerParams(vmem_limit_bytes=60 * MIB),
    )(place, *own, *par, w_out, events, targets, col, row)


def weighted_kernel(place, mixed_t, grad, col, keep_w, send_w, parts_w, p_sem):
    core = place[3]
    stores = [None, None]
    for turn, n in enumerate(range(0, grad.shape[1], 512)):
        cols = slice(n, n + 512)
        slot = turn % 2
        scaled = (grad[:, cols].astype(F32) * col[:, 3:4]).astype(BF16)
        g_w = jnp.dot(mixed_t[...], scaled, preferred_element_type=F32)
        if stores[slot] is not None:
            for c in stores[slot]:
                c.wait()
        for to in range(2):
            for q in range(32):
                x, y, zh = q // 8, q // 2 % 4, q % 2
                r = (y * 8 + zh * 4 + x) * 32 + to * 16
                w_at = (r // 64 % 2) * 512 + (r // 128 % 4) * 128 + (r // 512) * 64 + r % 64
                parts_w[slot, to, q * 16 : q * 16 + 16] = g_w[w_at : w_at + 16].astype(BF16)
        stores[slot] = []
        for which, (ref, side) in enumerate(((keep_w, core), (send_w, 1 - core))):
            c = pltpu.make_async_copy(
                parts_w.at[slot, side], ref.at[:, cols], p_sem.at[slot, which]
            )
            c.start()
            stores[slot].append(c)
    for pending in stores:
        for c in pending:
            c.wait()


def weighted_call(place, mixed_t, grad, col):
    any_spec = pl.BlockSpec(memory_space=pltpu.HBM)
    vmem = pl.BlockSpec(memory_space=pltpu.VMEM)
    part = jax.ShapeDtypeStruct((512, grad.shape[1]), BF16)
    return pl.pallas_call(
        weighted_kernel,
        out_shape=(part, part),
        in_specs=[pl.BlockSpec(memory_space=pltpu.SMEM), vmem, vmem, vmem],
        out_specs=(any_spec, any_spec),
        scratch_shapes=[
            pltpu.VMEM((2, 2, 512, 512), BF16),
            pltpu.SemaphoreType.DMA((2, 2)),
        ],
        cost_estimate=pl.CostEstimate(
            flops=2 * 1024 * MIB, bytes_accessed=8 * MIB, transcendentals=0
        ),
        compiler_params=pltpu.CompilerParams(vmem_limit_bytes=40 * MIB),
    )(place, mixed_t, grad, col)


def on_device(events, w_uvqk, w_out, targets, item_ids, uniform_flags, lengths, seq_weights):
    count = events.shape[0]
    core = lax.axis_index("c")
    flag = uniform_flags.astype(F32)
    spot = jnp.stack([lax.axis_index(n) for n in ("y", "zh", "x", "c")]).astype(jnp.int32)
    w_out_all = lax.all_gather(w_out, ("y", "zh", "x", "c"), axis=0, tiled=True)
    place = jnp.arange(count, dtype=jnp.int32)
    ends = jnp.cumsum(lengths[0])
    seqid = jnp.sum((place[:, None] >= ends[None, :]).astype(jnp.int32), axis=1)
    member = (seqid[:, None] == jnp.arange(seq_weights.shape[0], dtype=jnp.int32)[None, :]).astype(
        F32
    )
    weight_row = jnp.sum(member * seq_weights[None, :], axis=1) * (1.0 - flag)
    facts = [seqid.astype(F32), item_ids.astype(F32), flag, weight_row]
    row = jnp.stack(facts + [jnp.zeros_like(flag)] * 4)
    col = row.T

    away = lax.ppermute(events, "c", SWAP)
    phases, (spot, col, row) = gather_proj(w_uvqk, (spot, col, row))
    own, par = [], []
    for (a_pieces, b_pieces), offsets in zip(phases, ORDER):
        mine, for_away = uvqk_call(spot, events, away, a_pieces, b_pieces, offsets)
        own.append(mine)
        par.append(lax.ppermute(for_away, "c", SWAP))
    mixed, mixed_t, grad_out, keep_u, send_u = block_call(
        spot, own, par, events, targets, w_out_all, col, row
    )

    def add(mine, away):
        return (mine.astype(F32) + lax.ppermute(away, "c", SWAP).astype(F32)).astype(BF16)

    model = events.shape[1]
    chip_u, grad_later = lax.optimization_barrier((add(keep_u, send_u), grad_out))
    chip_w = add(*weighted_call(spot, mixed_t, grad_later, col))
    got = lax.all_to_all(chip_u.reshape(64, 8, -1), CHIPS, 0, 0, tiled=True)
    got, chip_w = lax.optimization_barrier((got, chip_w))
    part_w = lax.psum_scatter(chip_w, "x", scatter_dimension=0, tiled=True)
    total = jnp.sum(got.astype(F32), axis=0)
    n_unif = 32.0 * total[0, model] + total[0, model + 1]
    unif = jnp.broadcast_to(total[:, :model].astype(BF16)[None], (64, 8, model))
    unif_mine = lax.all_to_all(unif, CHIPS, 0, 0, tiled=True).reshape(512, -1)
    unif_mine, part_w = lax.optimization_barrier((unif_mine, part_w))
    got_w = lax.all_to_all(part_w.reshape(16, 8, model), ("y", "zh", "zl"), 0, 0, tiled=True)
    unif_away = lax.ppermute(unif_mine, "c", SWAP)
    mixed_mine = lax.dynamic_slice_in_dim(mixed, core * 512, 512, 1)
    mixed_away = lax.dynamic_slice_in_dim(mixed, (1 - core) * 512, 512, 1)
    proj_mine = jnp.dot(grad_out, unif_mine.T, preferred_element_type=F32)
    proj_away = jnp.dot(grad_out, unif_away.T, preferred_element_type=F32)
    per_row = jnp.sum(mixed_mine.astype(F32) * proj_mine, axis=1) + jnp.sum(
        mixed_away.astype(F32) * proj_away, axis=1
    )
    per_row = -per_row * (1.0 - flag) / n_unif
    hyper = jnp.sum(member * per_row[:, None], axis=0)
    hyper, got_w = lax.optimization_barrier((hyper, got_w))
    weighted_grad = jnp.sum(got_w.astype(F32), axis=0) / (jnp.float32(count * 128) - n_unif)
    return (hyper, weighted_grad)


def solution(mesh):
    fine = Mesh(mesh.devices.reshape(4, 2, 4, 2, 2), AXES)
    dp = ("y", "zh", "x", "c")
    return jax.shard_map(
        on_device,
        mesh=fine,
        in_specs=(
            P(AXES, None),
            P(None, dp),
            P(dp, None),
            P(AXES, None),
            P(AXES),
            P(AXES),
            P(AXES, None),
            P(AXES),
        ),
        out_specs=(P(AXES), P(AXES, None)),
        check_vma=False,
    )
```

```python
import jax
import jax.numpy as jnp
from jax import lax
from jax.experimental import pallas as pl
from jax.experimental.pallas import tpu as pltpu
from jax.sharding import Mesh
from jax.sharding import PartitionSpec as P

HEADS = 8
DH = 128
AXES = ("y", "zh", "x", "c", "zl")
CHIPS = ("y", "zh", "x", "zl")
SWAP = [(0, 1), (1, 0)]
ACROSS = [(0, 3), (3, 0), (1, 2), (2, 1)]
ORDER = (
    ((0, 0), (0, 1), (0, 3), (1, 0), (1, 1), (1, 3), (3, 0), (3, 1), (3, 3)),
    ((0, 2), (1, 2), (3, 2), (2, 0), (2, 1), (2, 3), (2, 2)),
)
F32 = jnp.float32
BF16 = jnp.bfloat16
MIB = 1024 * 1024
NT = (((1,), (1,)), ((), ()))
NN = (((1,), (0,)), ((), ()))


def hop(array, axis, step):
    return lax.ppermute(array, axis, [(i, (i + step) % 4) for i in range(4)])


def first_rings(a, a_axis, b, b_axis, cut, also):
    got, also = lax.optimization_barrier(
        ((hop(a, a_axis, 1), hop(a, a_axis, -1), hop(b, b_axis, 1), hop(b, b_axis, -1)), also)
    )
    a_below, a_above, b_below, b_above = got
    far = (
        hop(a_below[:cut], a_axis, 1),
        hop(a_above[cut:], a_axis, -1),
        hop(b_below[:cut], b_axis, 1),
        hop(b_above[cut:], b_axis, -1),
    )
    return (a, a_above, far[:2], a_below), (b, b_above, far[2:], b_below), also


def last_rings(a, b):
    one = (hop(a[0], "y", 1), hop(a[1], "y", -1), hop(b[0], "x", 1), hop(b[1], "x", -1))
    two = (hop(a[1], "y", 1), hop(a[0], "y", -1), hop(b[1], "x", 1), hop(b[0], "x", -1))
    one, two = lax.optimization_barrier((one, two))
    a_near = (a, (two[1], one[1]), None, (one[0], two[0]))
    b_near = (b, (two[3], one[3]), None, (one[2], two[2]))
    a_far = (hop(one[0], "y", 1), hop(one[1], "y", -1))
    b_far = (hop(one[2], "x", 1), hop(one[3], "x", -1))
    last = (a_near[:2] + (a_far, a_near[3]), b_near[:2] + (b_far, b_near[3]))
    return (a_near, b_near), last


def gather_proj(w_uvqk, also):
    half = w_uvqk.shape[0] // 2
    rows = w_uvqk.T
    other = lax.ppermute(rows, ("zh", "zl"), ACROSS)
    both = jnp.stack([rows, other])
    a_line, b_line, also = first_rings(both[:, :, :half], "x", both[:, :, half:], "y", 1, also)

    def halves(pieces):
        own, above, far, below = pieces
        return jnp.stack([own, above]), jnp.stack([jnp.concatenate(far, 0), below])

    return last_rings(halves(a_line), halves(b_line)), also


def place_of(pieces, major, minor):
    return pieces[major][minor // 2], minor % 2


def uvqk_call(place, own, away, a_pieces, b_pieces, offsets):
    count, model = own.shape
    half = model // 2
    arrays, steps = [], []

    def seat(array):
        for i, seen in enumerate(arrays):
            if seen is array:
                return i
        arrays.append(array)
        return len(arrays) - 1

    for y_off, x_off in offsets:
        a_from, a_at = place_of(a_pieces, y_off, x_off)
        b_from, b_at = place_of(b_pieces, x_off, y_off)
        steps.append((y_off, x_off, (seat(a_from), a_at), (seat(b_from), b_at)))
    near = len(arrays)

    def kernel(place_ref, own_ref, away_ref, *refs):
        weights = refs[:near]
        out_own, out_away, w_buf, o_buf, w_sem, o_sem = refs[near:]
        loads = []
        for n, (_, _, a, b) in enumerate(steps):
            for side, (src, index) in enumerate((a, b)):
                for z_off in range(2):
                    z_at = place_ref[1] if z_off == 0 else 1 - place_ref[1]
                    c = pltpu.make_async_copy(
                        weights[src].at[index, z_off],
                        w_buf.at[n, z_at, :, side * half : (side + 1) * half],
                        w_sem.at[n, side, z_off],
                    )
                    c.start()
                    loads.append(c)
        stores = []
        for first in range(0, len(steps), 2):
            group = range(first, min(first + 2, len(steps)))
            for n in group:
                for c in loads[4 * n : 4 * n + 4]:
                    c.wait()
            rows = w_buf[first : first + len(group)].reshape(len(group) * 128, model)
            for who, (ev_ref, out_ref) in enumerate(((own_ref, out_own), (away_ref, out_away))):
                acc = lax.dot_general(ev_ref[...], rows, NT, preferred_element_type=F32)
                act = (0.5 * acc * (1.0 + jnp.tanh(0.5 * acc))).astype(BF16)
                for i, n in enumerate(group):
                    o_buf[n, who] = act[:, i * 128 : (i + 1) * 128]
                    c = pltpu.make_async_copy(o_buf.at[n, who], out_ref.at[n], o_sem.at[n, who])
                    c.start()
                    stores.append(c)
        for c in stores:
            c.wait()

    any_spec = pl.BlockSpec(memory_space=pltpu.HBM)
    vmem = pl.BlockSpec(memory_space=pltpu.VMEM)
    shape = jax.ShapeDtypeStruct((len(steps), count, 128), BF16)
    return pl.pallas_call(
        kernel,
        out_shape=(shape, shape),
        in_specs=[pl.BlockSpec(memory_space=pltpu.SMEM), vmem, vmem]
        + [any_spec] * near,
        out_specs=(any_spec, any_spec),
        scratch_shapes=[
            pltpu.VMEM((len(steps), 2, 64, model), BF16),
            pltpu.VMEM((len(steps), 2, count, 128), BF16),
            pltpu.SemaphoreType.DMA((len(steps), 2, 2)),
            pltpu.SemaphoreType.DMA((len(steps), 2)),
        ],
        cost_estimate=pl.CostEstimate(
            flops=4 * count * model * 128 * len(steps),
            bytes_accessed=model * 256 * len(steps),
            transcendentals=2 * count * 128 * len(steps),
        ),
        compiler_params=pltpu.CompilerParams(vmem_limit_bytes=60 * MIB),
    )(place, own, away, *arrays)


def silu(x):
    return 0.5 * x * (1.0 + jnp.tanh(0.5 * x))


def sigmoid(x):
    return 1.0 / (1.0 + jnp.exp(-x))


def block_kernel(
    place, own_hbm, par_hbm, w_out, events_hbm, targets_hbm, col, row, mixed_hbm, grad_hbm, keep_u, send_u,
    keep_w, send_w, own, par, events, targets, w_buf, attn, mixed_ref, mixed_t, outs, grad_ref,
    parts_u, parts_w, digits, b_sem, e_sem, w_sem, m_sem, p_sem, d_sem
):
    core = place[3]
    count, model = events.shape
    tile = count // 4
    blocks = []
    for who, (groups, held) in enumerate(((own_hbm, own), (par_hbm, par))):
        done = 0
        for offsets, ref in zip(ORDER, groups):
            for n, (y_off, x_off) in enumerate(offsets):
                y_at, x_at = lax.rem(place[0] + y_off, 4), lax.rem(place[2] + x_off, 4)
                c = pltpu.make_async_copy(ref.at[n], held.at[y_at, x_at], b_sem.at[who, done])
                c.start()
                blocks.append(c)
                done += 1
    loads = [
        pltpu.make_async_copy(events_hbm, events, e_sem.at[0]),
        pltpu.make_async_copy(targets_hbm, targets, e_sem.at[1]),
    ]
    for c in loads:
        c.start()
    for cls in range(2):
        for x in range(4):
            for zh in range(2):
                c = pltpu.make_async_copy(
                    w_out.at[zh * 512 + x * 128 + cls * 64 : zh * 512 + x * 128 + cls * 64 + 64],
                    w_buf.at[cls * 512 + x * 128 + zh * 64 : cls * 512 + x * 128 + zh * 64 + 64],
                    w_sem.at[cls, x, zh],
                )
                c.start()
                loads.append(c)
    lane = lax.broadcasted_iota(jnp.int32, (tile, 256), 1)
    low = lax.rem(lane, 128) < 64
    scale = 1.0 / DH**0.5
    for c in blocks:
        c.wait()
    for i in range(4):
        lo, hi = max(0, (i - 1) * tile), (i + 1) * tile
        here = slice(i * tile, hi)
        at_i = i * tile + lax.broadcasted_iota(jnp.int32, (tile, hi - lo), 0)
        at_j = lo + lax.broadcasted_iota(jnp.int32, (tile, hi - lo), 1)
        allowed = (col[here, 0:1] == row[0:1, lo:hi]) & (at_j <= at_i)
        for x in range(4):
            q = jnp.concatenate([own[2, x, here], par[2, x, here]], 1)
            k = jnp.concatenate([own[3, x, lo:hi], par[3, x, lo:hi]], 1)
            v = jnp.concatenate([own[1, x, lo:hi], par[1, x, lo:hi]], 1)
            halves = []
            for pick in (low, ~low):
                qz = jnp.where(pick, q, jnp.zeros_like(q))
                s = lax.dot_general(qz, k, NT, preferred_element_type=F32) * scale
                p = jnp.where(allowed, silu(s) * (1.0 / 128.0), 0.0).astype(BF16)
                halves.append(lax.dot_general(p, v, NN, preferred_element_type=F32))
            o = jnp.where(low, halves[0], halves[1])
            attn[here, x * 128 : (x + 1) * 128] = o[:, :128]
            attn[here, 512 + x * 128 : 512 + (x + 1) * 128] = o[:, 128:]
        a = attn[here, :]
        mean = jnp.mean(a, axis=1, keepdims=True)
        a = a - mean
        a = a * lax.rsqrt(jnp.mean(a * a, axis=1, keepdims=True) + 1e-05)
        for side, src in ((core, own), (1 - core, par)):
            base = 0 if src is own else 512
            u = jnp.concatenate([src[0, x, here] for x in range(4)], 1).astype(F32)
            m = (a[:, base : base + 512] * u).astype(BF16)
            mixed_ref[here, pl.ds(pl.multiple_of(side * 512, 512), 512)] = m
    for c in loads:
        c.wait()
    for n in range(0, model, 512):
        cols = slice(n, n + 512)
        s = jnp.dot(mixed_ref[...], w_buf[:, cols], preferred_element_type=F32)
        outs[:, cols] = (events[:, cols].astype(F32) + s).astype(BF16)
    mixed_t[...] = mixed_ref[...].T
    count_copies = [pltpu.make_async_copy(mixed_ref, mixed_hbm, m_sem)]
    scores = lax.dot_general(outs[...], targets[...], NT, preferred_element_type=F32)
    at_i = lax.broadcasted_iota(jnp.int32, (count, count), 0)
    at_j = lax.broadcasted_iota(jnp.int32, (count, count), 1)
    other = col[:, 1:2] != row[1:2, :]
    coef = sigmoid(jnp.where(at_i == at_j, -scores, scores))
    coef = jnp.where(
        at_i == at_j, -coef, jnp.where(other, coef * (1.0 / count), 0.0)
    ).astype(BF16)
    flagged = jnp.sum(row[2:3, :], axis=1, keepdims=True)
    high = jnp.floor(flagged * (1.0 / 32.0))
    at = lax.broadcasted_iota(jnp.int32, (512, 128), 1)
    digits[...] = jnp.where(at == 0, high, jnp.where(at == 1, flagged - 32.0 * high, 0.0)).astype(BF16)
    count_copies += [
        pltpu.make_async_copy(digits, ref.at[:, model : model + 128], d_sem.at[i])
        for i, ref in enumerate((keep_u, send_u))
    ]
    for c in count_copies:
        c.start()
    stores = [None, None]
    for turn, n in enumerate(range(0, model, 512)):
        cols = slice(n, n + 512)
        slot = turn % 2
        g = jnp.dot(coef, targets[:, cols], preferred_element_type=F32).astype(BF16)
        grad_ref[:, cols] = g
        unif = (g.astype(F32) * col[:, 2:3]).astype(BF16)
        scaled = (g.astype(F32) * col[:, 3:4]).astype(BF16)
        g_u = jnp.dot(mixed_t[...], unif, preferred_element_type=F32)
        g_w = jnp.dot(mixed_t[...], scaled, preferred_element_type=F32)
        if stores[slot] is not None:
            for c in stores[slot]:
                c.wait()
        parts_u[slot] = g_u.astype(BF16).reshape(2, 512, 512)
        for to in range(2):
            for q in range(32):
                x, y, zh = q // 8, q // 2 % 4, q % 2
                r = (y * 8 + zh * 4 + x) * 32 + to * 16
                w_at = (r // 64 % 2) * 512 + (r // 128 % 4) * 128 + (r // 512) * 64 + r % 64
                parts_w[slot, to, q * 16 : q * 16 + 16] = g_w[w_at : w_at + 16].astype(BF16)
        stores[slot] = []
        for which, (ref, src) in enumerate(
            (
                (keep_u, parts_u.at[slot, core]),
                (send_u, parts_u.at[slot, 1 - core]),
                (keep_w, parts_w.at[slot, core]),
                (send_w, parts_w.at[slot, 1 - core]),
                (grad_hbm, grad_ref.at[:, cols]),
            )
        ):
            c = pltpu.make_async_copy(src, ref.at[:, cols], p_sem.at[slot, which])
            c.start()
            stores[slot].append(c)
    for pending in stores:
        for c in pending:
            c.wait()
    for c in count_copies:
        c.wait()


def block_call(place, own, par, events, targets, w_out, col, row):
    count, model = events.shape
    width = w_out.shape[0]
    any_spec = pl.BlockSpec(memory_space=pltpu.HBM)
    vmem = pl.BlockSpec(memory_space=pltpu.VMEM)
    part_u = jax.ShapeDtypeStruct((512, model + 128), BF16)
    part_w = jax.ShapeDtypeStruct((512, model), BF16)
    groups = len(own)

    def kernel(place_ref, *refs):
        block_kernel(place_ref, refs[:groups], refs[groups : 2 * groups], *refs[2 * groups :])
    return pl.pallas_call(
        kernel,
        out_shape=(
            jax.ShapeDtypeStruct((count, width), BF16),
            jax.ShapeDtypeStruct((count, model), BF16),
            part_u,
            part_u,
            part_w,
            part_w,
        ),
        in_specs=[pl.BlockSpec(memory_space=pltpu.SMEM)]
        + [any_spec] * (2 * groups + 3)
        + [vmem] * 2,
        out_specs=(any_spec,) * 2 + (pl.BlockSpec(memory_space=pl.ANY),) * 2 + (any_spec,) * 2,
        scratch_shapes=[
            pltpu.VMEM((4, 4, count, 128), BF16),
            pltpu.VMEM((4, 4, count, 128), BF16),
            pltpu.VMEM((count, model), BF16),
            pltpu.VMEM((count, model), BF16),
            pltpu.VMEM((width, model), BF16),
            pltpu.VMEM((count, width), F32),
            pltpu.VMEM((count, width), BF16),
            pltpu.VMEM((width, count), BF16),
            pltpu.VMEM((count, model), BF16),
            pltpu.VMEM((count, model), BF16),
            pltpu.VMEM((2, 2, 512, 512), BF16),
            pltpu.VMEM((2, 2, 512, 512), BF16),
            pltpu.VMEM((512, 128), BF16),
            pltpu.SemaphoreType.DMA((2, 16)),
            pltpu.SemaphoreType.DMA((2,)),
            pltpu.SemaphoreType.DMA((2, 4, 2)),
            pltpu.SemaphoreType.DMA,
            pltpu.SemaphoreType.DMA((2, 5)),
            pltpu.SemaphoreType.DMA((2,)),
        ],
        cost_estimate=pl.CostEstimate(
            flops=10 * 1024 * MIB, bytes_accessed=24 * MIB, transcendentals=2 * MIB
        ),
        compiler_params=pltpu.CompilerParams(vmem_limit_bytes=60 * MIB),
    )(place, *own, *par, w_out, events, targets, col, row)


def on_device(events, w_uvqk, w_out, targets, item_ids, uniform_flags, lengths, seq_weights):
    count = events.shape[0]
    core = lax.axis_index("c")
    flag = uniform_flags.astype(F32)
    spot = jnp.stack([lax.axis_index(n) for n in ("y", "zh", "x", "c")]).astype(jnp.int32)
    w_out_all = lax.all_gather(w_out, ("y", "zh", "x", "c"), axis=0, tiled=True)
    place = jnp.arange(count, dtype=jnp.int32)
    ends = jnp.cumsum(lengths[0])
    seqid = jnp.sum((place[:, None] >= ends[None, :]).astype(jnp.int32), axis=1)
    member = (seqid[:, None] == jnp.arange(seq_weights.shape[0], dtype=jnp.int32)[None, :]).astype(
        F32
    )
    weight_row = jnp.sum(member * seq_weights[None, :], axis=1) * (1.0 - flag)
    facts = [seqid.astype(F32), item_ids.astype(F32), flag, weight_row]
    row = jnp.stack(facts + [jnp.zeros_like(flag)] * 4)
    col = row.T

    away = lax.ppermute(events, "c", SWAP)
    phases, (spot, col, row) = gather_proj(w_uvqk, (spot, col, row))
    own, par = [], []
    for (a_pieces, b_pieces), offsets in zip(phases, ORDER):
        mine, for_away = uvqk_call(spot, events, away, a_pieces, b_pieces, offsets)
        own.append(mine)
        par.append(lax.ppermute(for_away, "c", SWAP))
    mixed, grad_out, keep_u, send_u, keep_w, send_w = block_call(
        spot, own, par, events, targets, w_out_all, col, row
    )

    def add(mine, away):
        return (mine.astype(F32) + lax.ppermute(away, "c", SWAP).astype(F32)).astype(BF16)

    model = events.shape[1]
    chip_u, chip_w = add(keep_u, send_u), add(keep_w, send_w)
    part_w = lax.psum_scatter(chip_w, "x", scatter_dimension=0, tiled=True)
    got = lax.all_to_all(chip_u.reshape(64, 8, -1), CHIPS, 0, 0, tiled=True)
    total = jnp.sum(got.astype(F32), axis=0)
    n_unif = 32.0 * total[0, model] + total[0, model + 1]
    unif = jnp.broadcast_to(total[:, :model].astype(BF16)[None], (64, 8, model))
    unif_mine = lax.all_to_all(unif, CHIPS, 0, 0, tiled=True).reshape(512, -1)
    unif_mine, part_w = lax.optimization_barrier((unif_mine, part_w))
    got_w = lax.all_to_all(part_w.reshape(16, 8, model), ("y", "zh", "zl"), 0, 0, tiled=True)
    unif_away = lax.ppermute(unif_mine, "c", SWAP)
    mixed_mine = lax.dynamic_slice_in_dim(mixed, core * 512, 512, 1)
    mixed_away = lax.dynamic_slice_in_dim(mixed, (1 - core) * 512, 512, 1)
    proj_mine = jnp.dot(grad_out, unif_mine.T, preferred_element_type=F32)
    proj_away = jnp.dot(grad_out, unif_away.T, preferred_element_type=F32)
    per_row = jnp.sum(mixed_mine.astype(F32) * proj_mine, axis=1) + jnp.sum(
        mixed_away.astype(F32) * proj_away, axis=1
    )
    per_row = -per_row * (1.0 - flag) / n_unif
    hyper = jnp.sum(member * per_row[:, None], axis=0)
    hyper, got_w = lax.optimization_barrier((hyper, got_w))
    weighted_grad = jnp.sum(got_w.astype(F32), axis=0) / (jnp.float32(count * 128) - n_unif)
    return (hyper, weighted_grad)


def solution(mesh):
    fine = Mesh(mesh.devices.reshape(4, 2, 4, 2, 2), AXES)
    dp = ("y", "zh", "x", "c")
    return jax.shard_map(
        on_device,
        mesh=fine,
        in_specs=(
            P(AXES, None),
            P(None, dp),
            P(dp, None),
            P(AXES, None),
            P(AXES),
            P(AXES),
            P(AXES, None),
            P(AXES),
        ),
        out_specs=(P(AXES), P(AXES, None)),
        check_vma=False,
    )
```

```python
import jax
import jax.numpy as jnp
from jax import lax
from jax.experimental import pallas as pl
from jax.experimental.pallas import tpu as pltpu
from jax.sharding import Mesh
from jax.sharding import PartitionSpec as P

HEADS = 8
DH = 128
AXES = ("y", "zh", "x", "c", "zl")
CHIPS = ("y", "zh", "x", "zl")
SWAP = [(0, 1), (1, 0)]
ACROSS = [(0, 3), (3, 0), (1, 2), (2, 1)]
ORDER = (
    ((0, 0), (0, 1), (0, 3), (1, 0), (1, 1), (1, 3), (3, 0), (3, 1), (3, 3)),
    ((0, 2), (1, 2), (3, 2), (2, 0), (2, 1), (2, 3), (2, 2)),
)
F32 = jnp.float32
BF16 = jnp.bfloat16
MIB = 1024 * 1024
NT = (((1,), (1,)), ((), ()))
NN = (((1,), (0,)), ((), ()))


def hop(array, axis, step):
    return lax.ppermute(array, axis, [(i, (i + step) % 4) for i in range(4)])


def first_rings(a, a_axis, b, b_axis, cut, also):
    got, also = lax.optimization_barrier(
        ((hop(a, a_axis, 1), hop(a, a_axis, -1), hop(b, b_axis, 1), hop(b, b_axis, -1)), also)
    )
    a_below, a_above, b_below, b_above = got
    far = (
        hop(a_below[:cut], a_axis, 1),
        hop(a_above[cut:], a_axis, -1),
        hop(b_below[:cut], b_axis, 1),
        hop(b_above[cut:], b_axis, -1),
    )
    return (a, a_above, far[:2], a_below), (b, b_above, far[2:], b_below), also


def last_rings(a, b):
    one = (hop(a[0], "y", 1), hop(a[1], "y", -1), hop(b[0], "x", 1), hop(b[1], "x", -1))
    two = (hop(a[1], "y", 1), hop(a[0], "y", -1), hop(b[1], "x", 1), hop(b[0], "x", -1))
    one, two = lax.optimization_barrier((one, two))
    a_near = (a, (two[1], one[1]), None, (one[0], two[0]))
    b_near = (b, (two[3], one[3]), None, (one[2], two[2]))
    a_far = (hop(one[0], "y", 1), hop(one[1], "y", -1))
    b_far = (hop(one[2], "x", 1), hop(one[3], "x", -1))
    last = (a_near[:2] + (a_far, a_near[3]), b_near[:2] + (b_far, b_near[3]))
    return (a_near, b_near), last


def gather_proj(w_uvqk, also):
    half = w_uvqk.shape[0] // 2
    rows = w_uvqk.T
    other = lax.ppermute(rows, ("zh", "zl"), ACROSS)
    both = jnp.stack([rows, other])
    a_line, b_line, also = first_rings(both[:, :, :half], "x", both[:, :, half:], "y", 1, also)

    def halves(pieces):
        own, above, far, below = pieces
        return jnp.stack([own, above]), jnp.stack([jnp.concatenate(far, 0), below])

    return last_rings(halves(a_line), halves(b_line)), also


def place_of(pieces, major, minor):
    return pieces[major][minor // 2], minor % 2


def uvqk_call(place, own, away, a_pieces, b_pieces, offsets):
    count, model = own.shape
    half = model // 2
    arrays, steps = [], []

    def seat(array):
        for i, seen in enumerate(arrays):
            if seen is array:
                return i
        arrays.append(array)
        return len(arrays) - 1

    for y_off, x_off in offsets:
        a_from, a_at = place_of(a_pieces, y_off, x_off)
        b_from, b_at = place_of(b_pieces, x_off, y_off)
        steps.append((y_off, x_off, (seat(a_from), a_at), (seat(b_from), b_at)))
    near = len(arrays)

    def kernel(place_ref, own_hbm, away_hbm, *refs):
        weights = refs[:near]
        out_own, out_away, own_ref, away_ref, w_buf, o_buf, w_sem, o_sem, e_sem = refs[near:]
        sides = [
            pltpu.make_async_copy(own_hbm, own_ref, e_sem.at[0]),
            pltpu.make_async_copy(away_hbm, away_ref, e_sem.at[1]),
        ]
        sides[0].start()
        loads = []
        for n, (_, _, a, b) in enumerate(steps):
            for side, (src, index) in enumerate((a, b)):
                for z_off in range(2):
                    z_at = place_ref[1] if z_off == 0 else 1 - place_ref[1]
                    c = pltpu.make_async_copy(
                        weights[src].at[index, z_off],
                        w_buf.at[n, z_at, :, side * half : (side + 1) * half],
                        w_sem.at[n, side, z_off],
                    )
                    c.start()
                    loads.append(c)
            if n == 1:
                sides[1].start()
        stores = []
        for first in range(0, len(steps), 2):
            group = range(first, min(first + 2, len(steps)))
            for n in group:
                for c in loads[4 * n : 4 * n + 4]:
                    c.wait()
            rows = w_buf[first : first + len(group)].reshape(len(group) * 128, model)
            for who, (ev_ref, out_ref) in enumerate(((own_ref, out_own), (away_ref, out_away))):
                if first == 0:
                    sides[who].wait()
                acc = lax.dot_general(ev_ref[...], rows, NT, preferred_element_type=F32)
                act = (0.5 * acc * (1.0 + jnp.tanh(0.5 * acc))).astype(BF16)
                for i, n in enumerate(group):
                    o_buf[n, who] = act[:, i * 128 : (i + 1) * 128]
                    c = pltpu.make_async_copy(o_buf.at[n, who], out_ref.at[n], o_sem.at[n, who])
                    c.start()
                    stores.append(c)
        for c in stores:
            c.wait()

    any_spec = pl.BlockSpec(memory_space=pltpu.HBM)
    shape = jax.ShapeDtypeStruct((len(steps), count, 128), BF16)
    return pl.pallas_call(
        kernel,
        out_shape=(shape, shape),
        in_specs=[pl.BlockSpec(memory_space=pltpu.SMEM)] + [any_spec] * (near + 2),
        out_specs=(any_spec, any_spec),
        scratch_shapes=[
            pltpu.VMEM((count, model), BF16),
            pltpu.VMEM((count, model), BF16),
            pltpu.VMEM((len(steps), 2, 64, model), BF16),
            pltpu.VMEM((len(steps), 2, count, 128), BF16),
            pltpu.SemaphoreType.DMA((len(steps), 2, 2)),
            pltpu.SemaphoreType.DMA((len(steps), 2)),
            pltpu.SemaphoreType.DMA((2,)),
        ],
        cost_estimate=pl.CostEstimate(
            flops=4 * count * model * 128 * len(steps),
            bytes_accessed=model * 256 * len(steps),
            transcendentals=2 * count * 128 * len(steps),
        ),
        compiler_params=pltpu.CompilerParams(vmem_limit_bytes=60 * MIB),
    )(place, own, away, *arrays)


def silu(x):
    return 0.5 * x * (1.0 + jnp.tanh(0.5 * x))


def sigmoid(x):
    return 1.0 / (1.0 + jnp.exp(-x))


def block_kernel(
    place, own_hbm, par_hbm, w_out, events_hbm, targets_hbm, row, mixed_hbm, grad_hbm, keep_u, send_u,
    keep_w, send_w, col, own, par, events, targets, w_buf, attn, mixed_ref, mixed_t, outs, grad_ref,
    parts_u, parts_w, digits, b_sem, e_sem, w_sem, m_sem, p_sem, d_sem
):
    core = place[3]
    count, model = events.shape
    tile = count // 4
    blocks = []
    for who, (groups, held) in enumerate(((own_hbm, own), (par_hbm, par))):
        done = 0
        for offsets, ref in zip(ORDER, groups):
            for n, (y_off, x_off) in enumerate(offsets):
                y_at, x_at = lax.rem(place[0] + y_off, 4), lax.rem(place[2] + x_off, 4)
                c = pltpu.make_async_copy(ref.at[n], held.at[y_at, x_at], b_sem.at[who, done])
                c.start()
                blocks.append(c)
                done += 1
    loads = [
        pltpu.make_async_copy(events_hbm, events, e_sem.at[0]),
        pltpu.make_async_copy(targets_hbm, targets, e_sem.at[1]),
    ]
    for c in loads:
        c.start()
    for cls in range(2):
        for x in range(4):
            for zh in range(2):
                c = pltpu.make_async_copy(
                    w_out.at[zh * 512 + x * 128 + cls * 64 : zh * 512 + x * 128 + cls * 64 + 64],
                    w_buf.at[cls * 512 + x * 128 + zh * 64 : cls * 512 + x * 128 + zh * 64 + 64],
                    w_sem.at[cls, x, zh],
                )
                c.start()
                loads.append(c)
    col[...] = row[...].T
    lane = lax.broadcasted_iota(jnp.int32, (tile, 256), 1)
    low = lax.rem(lane, 128) < 64
    scale = 1.0 / DH**0.5
    for c in blocks:
        c.wait()
    for i in range(4):
        lo, hi = max(0, (i - 1) * tile), (i + 1) * tile
        here = slice(i * tile, hi)
        at_i = i * tile + lax.broadcasted_iota(jnp.int32, (tile, hi - lo), 0)
        at_j = lo + lax.broadcasted_iota(jnp.int32, (tile, hi - lo), 1)
        allowed = (col[here, 0:1] == row[0:1, lo:hi]) & (at_j <= at_i)
        for x in range(4):
            q = jnp.concatenate([own[2, x, here], par[2, x, here]], 1)
            k = jnp.concatenate([own[3, x, lo:hi], par[3, x, lo:hi]], 1)
            v = jnp.concatenate([own[1, x, lo:hi], par[1, x, lo:hi]], 1)
            halves = []
            for pick in (low, ~low):
                qz = jnp.where(pick, q, jnp.zeros_like(q))
                s = lax.dot_general(qz, k, NT, preferred_element_type=F32) * scale
                p = jnp.where(allowed, silu(s) * (1.0 / 128.0), 0.0).astype(BF16)
                halves.append(lax.dot_general(p, v, NN, preferred_element_type=F32))
            o = jnp.where(low, halves[0], halves[1])
            attn[here, x * 128 : (x + 1) * 128] = o[:, :128]
            attn[here, 512 + x * 128 : 512 + (x + 1) * 128] = o[:, 128:]
        a = attn[here, :]
        mean = jnp.mean(a, axis=1, keepdims=True)
        a = a - mean
        a = a * lax.rsqrt(jnp.mean(a * a, axis=1, keepdims=True) + 1e-05)
        for side, src in ((core, own), (1 - core, par)):
            base = 0 if src is own else 512
            u = jnp.concatenate([src[0, x, here] for x in range(4)], 1).astype(F32)
            m = (a[:, base : base + 512] * u).astype(BF16)
            mixed_ref[here, pl.ds(pl.multiple_of(side * 512, 512), 512)] = m
    for c in loads:
        c.wait()
    for n in range(0, model, 512):
        cols = slice(n, n + 512)
        s = jnp.dot(mixed_ref[...], w_buf[:, cols], preferred_element_type=F32)
        outs[:, cols] = (events[:, cols].astype(F32) + s).astype(BF16)
    mixed_t[...] = mixed_ref[...].T
    count_copies = [pltpu.make_async_copy(mixed_ref, mixed_hbm, m_sem)]
    scores = lax.dot_general(outs[...], targets[...], NT, preferred_element_type=F32)
    at_i = lax.broadcasted_iota(jnp.int32, (count, count), 0)
    at_j = lax.broadcasted_iota(jnp.int32, (count, count), 1)
    other = col[:, 1:2] != row[1:2, :]
    coef = sigmoid(jnp.where(at_i == at_j, -scores, scores))
    coef = jnp.where(
        at_i == at_j, -coef, jnp.where(other, coef * (1.0 / count), 0.0)
    ).astype(BF16)
    flagged = jnp.sum(row[2:3, :], axis=1, keepdims=True)
    high = jnp.floor(flagged * (1.0 / 32.0))
    at = lax.broadcasted_iota(jnp.int32, (512, 128), 1)
    digits[...] = jnp.where(at == 0, high, jnp.where(at == 1, flagged - 32.0 * high, 0.0)).astype(BF16)
    count_copies += [
        pltpu.make_async_copy(digits, ref.at[:, model : model + 128], d_sem.at[i])
        for i, ref in enumerate((keep_u, send_u))
    ]
    for c in count_copies:
        c.start()
    stores = [None, None]
    for turn, n in enumerate(range(0, model, 512)):
        cols = slice(n, n + 512)
        slot = turn % 2
        g = jnp.dot(coef, targets[:, cols], preferred_element_type=F32).astype(BF16)
        grad_ref[:, cols] = g
        unif = (g.astype(F32) * col[:, 2:3]).astype(BF16)
        scaled = (g.astype(F32) * col[:, 3:4]).astype(BF16)
        g_u = jnp.dot(mixed_t[...], unif, preferred_element_type=F32)
        g_w = jnp.dot(mixed_t[...], scaled, preferred_element_type=F32)
        if stores[slot] is not None:
            for c in stores[slot]:
                c.wait()
        parts_u[slot] = g_u.astype(BF16).reshape(2, 512, 512)
        for to in range(2):
            for q in range(32):
                x, y, zh = q // 8, q // 2 % 4, q % 2
                r = (y * 8 + zh * 4 + x) * 32 + to * 16
                w_at = (r // 64 % 2) * 512 + (r // 128 % 4) * 128 + (r // 512) * 64 + r % 64
                parts_w[slot, to, q * 16 : q * 16 + 16] = g_w[w_at : w_at + 16].astype(BF16)
        stores[slot] = []
        for which, (ref, src) in enumerate(
            (
                (keep_u, parts_u.at[slot, core]),
                (send_u, parts_u.at[slot, 1 - core]),
                (keep_w, parts_w.at[slot, core]),
                (send_w, parts_w.at[slot, 1 - core]),
                (grad_hbm, grad_ref.at[:, cols]),
            )
        ):
            c = pltpu.make_async_copy(src, ref.at[:, cols], p_sem.at[slot, which])
            c.start()
            stores[slot].append(c)
    for pending in stores:
        for c in pending:
            c.wait()
    for c in count_copies:
        c.wait()


def block_call(place, own, par, events, targets, w_out, row):
    count, model = events.shape
    width = w_out.shape[0]
    any_spec = pl.BlockSpec(memory_space=pltpu.HBM)
    vmem = pl.BlockSpec(memory_space=pltpu.VMEM)
    part_u = jax.ShapeDtypeStruct((512, model + 128), BF16)
    part_w = jax.ShapeDtypeStruct((512, model), BF16)
    groups = len(own)

    def kernel(place_ref, *refs):
        block_kernel(place_ref, refs[:groups], refs[groups : 2 * groups], *refs[2 * groups :])
    return pl.pallas_call(
        kernel,
        out_shape=(
            jax.ShapeDtypeStruct((count, width), BF16),
            jax.ShapeDtypeStruct((count, model), BF16),
            part_u,
            part_u,
            part_w,
            part_w,
        ),
        in_specs=[pl.BlockSpec(memory_space=pltpu.SMEM)]
        + [any_spec] * (2 * groups + 3)
        + [vmem],
        out_specs=(any_spec,) * 2 + (pl.BlockSpec(memory_space=pl.ANY),) * 2 + (any_spec,) * 2,
        scratch_shapes=[
            pltpu.VMEM((count, row.shape[0]), F32),
            pltpu.VMEM((4, 4, count, 128), BF16),
            pltpu.VMEM((4, 4, count, 128), BF16),
            pltpu.VMEM((count, model), BF16),
            pltpu.VMEM((count, model), BF16),
            pltpu.VMEM((width, model), BF16),
            pltpu.VMEM((count, width), F32),
            pltpu.VMEM((count, width), BF16),
            pltpu.VMEM((width, count), BF16),
            pltpu.VMEM((count, model), BF16),
            pltpu.VMEM((count, model), BF16),
            pltpu.VMEM((2, 2, 512, 512), BF16),
            pltpu.VMEM((2, 2, 512, 512), BF16),
            pltpu.VMEM((512, 128), BF16),
            pltpu.SemaphoreType.DMA((2, 16)),
            pltpu.SemaphoreType.DMA((2,)),
            pltpu.SemaphoreType.DMA((2, 4, 2)),
            pltpu.SemaphoreType.DMA,
            pltpu.SemaphoreType.DMA((2, 5)),
            pltpu.SemaphoreType.DMA((2,)),
        ],
        cost_estimate=pl.CostEstimate(
            flops=10 * 1024 * MIB, bytes_accessed=24 * MIB, transcendentals=2 * MIB
        ),
        compiler_params=pltpu.CompilerParams(vmem_limit_bytes=60 * MIB),
    )(place, *own, *par, w_out, events, targets, row)


def on_device(events, w_uvqk, w_out, targets, item_ids, uniform_flags, lengths, seq_weights):
    count = events.shape[0]
    core = lax.axis_index("c")
    flag = uniform_flags.astype(F32)
    spot = jnp.stack([lax.axis_index(n) for n in ("y", "zh", "x", "c")]).astype(jnp.int32)
    w_out_all = lax.all_gather(w_out, ("y", "zh", "x", "c"), axis=0, tiled=True)
    place = jnp.arange(count, dtype=jnp.int32)
    ends = jnp.cumsum(lengths[0])
    seqid = jnp.sum((place[:, None] >= ends[None, :]).astype(jnp.int32), axis=1)
    member = (seqid[:, None] == jnp.arange(seq_weights.shape[0], dtype=jnp.int32)[None, :]).astype(
        F32
    )
    weight_row = jnp.sum(member * seq_weights[None, :], axis=1) * (1.0 - flag)
    facts = [seqid.astype(F32), item_ids.astype(F32), flag, weight_row]
    row = jnp.stack(facts + [jnp.zeros_like(flag)] * 4)

    away = lax.ppermute(events, "c", SWAP)
    phases, (spot, row) = gather_proj(w_uvqk, (spot, row))
    own, par = [], []
    for (a_pieces, b_pieces), offsets in zip(phases, ORDER):
        mine, for_away = uvqk_call(spot, events, away, a_pieces, b_pieces, offsets)
        own.append(mine)
        par.append(lax.ppermute(for_away, "c", SWAP))
    mixed, grad_out, keep_u, send_u, keep_w, send_w = block_call(
        spot, own, par, events, targets, w_out_all, row
    )

    def add(mine, away):
        return (mine.astype(F32) + lax.ppermute(away, "c", SWAP).astype(F32)).astype(BF16)

    model = events.shape[1]
    chip_u, chip_w = add(keep_u, send_u), add(keep_w, send_w)
    part_w = lax.psum_scatter(chip_w, "x", scatter_dimension=0, tiled=True)
    got = lax.all_to_all(chip_u.reshape(64, 8, -1), CHIPS, 0, 0, tiled=True)
    total = jnp.sum(got.astype(F32), axis=0)
    n_unif = 32.0 * total[0, model] + total[0, model + 1]
    unif = jnp.broadcast_to(total[:, :model].astype(BF16)[None], (64, 8, model))
    unif_mine = lax.all_to_all(unif, CHIPS, 0, 0, tiled=True).reshape(512, -1)
    unif_mine, part_w = lax.optimization_barrier((unif_mine, part_w))
    got_w = lax.all_to_all(part_w.reshape(16, 8, model), ("y", "zh", "zl"), 0, 0, tiled=True)
    unif_away = lax.ppermute(unif_mine, "c", SWAP)
    mixed_mine = lax.dynamic_slice_in_dim(mixed, core * 512, 512, 1)
    mixed_away = lax.dynamic_slice_in_dim(mixed, (1 - core) * 512, 512, 1)
    proj_mine = jnp.dot(grad_out, unif_mine.T, preferred_element_type=F32)
    proj_away = jnp.dot(grad_out, unif_away.T, preferred_element_type=F32)
    per_row = jnp.sum(mixed_mine.astype(F32) * proj_mine, axis=1) + jnp.sum(
        mixed_away.astype(F32) * proj_away, axis=1
    )
    per_row = -per_row * (1.0 - flag) / n_unif
    hyper = jnp.sum(member * per_row[:, None], axis=0)
    hyper, got_w = lax.optimization_barrier((hyper, got_w))
    weighted_grad = jnp.sum(got_w.astype(F32), axis=0) / (jnp.float32(count * 128) - n_unif)
    return (hyper, weighted_grad)


def solution(mesh):
    fine = Mesh(mesh.devices.reshape(4, 2, 4, 2, 2), AXES)
    dp = ("y", "zh", "x", "c")
    return jax.shard_map(
        on_device,
        mesh=fine,
        in_specs=(
            P(AXES, None),
            P(None, dp),
            P(dp, None),
            P(AXES, None),
            P(AXES),
            P(AXES),
            P(AXES, None),
            P(AXES),
        ),
        out_specs=(P(AXES), P(AXES, None)),
        check_vma=False,
    )
```

```python
import jax
import jax.numpy as jnp
from jax import lax
from jax.experimental import pallas as pl
from jax.experimental.pallas import tpu as pltpu
from jax.sharding import Mesh
from jax.sharding import PartitionSpec as P

HEADS = 8
DH = 128
AXES = ("y", "zh", "x", "c", "zl")
CHIPS = ("y", "zh", "x", "zl")
SWAP = [(0, 1), (1, 0)]
ACROSS = [(0, 3), (3, 0), (1, 2), (2, 1)]
ORDER = (
    ((0, 0), (0, 1), (0, 3), (1, 0), (1, 1), (1, 3), (3, 0), (3, 1), (3, 3)),
    ((0, 2), (1, 2), (3, 2), (2, 0), (2, 1), (2, 3), (2, 2)),
)
F32 = jnp.float32
BF16 = jnp.bfloat16
MIB = 1024 * 1024
NT = (((1,), (1,)), ((), ()))
NN = (((1,), (0,)), ((), ()))


def hop(array, axis, step):
    return lax.ppermute(array, axis, [(i, (i + step) % 4) for i in range(4)])


def first_rings(a, a_axis, b, b_axis, cut, also):
    got, also = lax.optimization_barrier(
        ((hop(a, a_axis, 1), hop(a, a_axis, -1), hop(b, b_axis, 1), hop(b, b_axis, -1)), also)
    )
    a_below, a_above, b_below, b_above = got
    far = (
        hop(a_below[:cut], a_axis, 1),
        hop(a_above[cut:], a_axis, -1),
        hop(b_below[:cut], b_axis, 1),
        hop(b_above[cut:], b_axis, -1),
    )
    return (a, a_above, far[:2], a_below), (b, b_above, far[2:], b_below), also


def last_rings(a, b):
    one = (hop(a[0], "y", 1), hop(a[1], "y", -1), hop(b[0], "x", 1), hop(b[1], "x", -1))
    two = (hop(a[1], "y", 1), hop(a[0], "y", -1), hop(b[1], "x", 1), hop(b[0], "x", -1))
    one, two = lax.optimization_barrier((one, two))
    a_near = (a, (two[1], one[1]), None, (one[0], two[0]))
    b_near = (b, (two[3], one[3]), None, (one[2], two[2]))
    a_far = (hop(one[0], "y", 1), hop(one[1], "y", -1))
    b_far = (hop(one[2], "x", 1), hop(one[3], "x", -1))
    last = (a_near[:2] + (a_far, a_near[3]), b_near[:2] + (b_far, b_near[3]))
    return (a_near, b_near), last


def gather_proj(w_uvqk, also):
    half = w_uvqk.shape[0] // 2
    rows = w_uvqk.T
    other = lax.ppermute(rows, ("zh", "zl"), ACROSS)
    both = jnp.stack([rows, other])
    a_line, b_line, also = first_rings(both[:, :, :half], "x", both[:, :, half:], "y", 1, also)

    def halves(pieces):
        own, above, far, below = pieces
        return jnp.stack([own, above]), jnp.stack([jnp.concatenate(far, 0), below])

    return last_rings(halves(a_line), halves(b_line)), also


def place_of(pieces, major, minor):
    return pieces[major][minor // 2], minor % 2


def uvqk_call(place, own, away, a_pieces, b_pieces, offsets):
    count, model = own.shape
    half = model // 2
    arrays, steps = [], []

    def seat(array):
        for i, seen in enumerate(arrays):
            if seen is array:
                return i
        arrays.append(array)
        return len(arrays) - 1

    for y_off, x_off in offsets:
        a_from, a_at = place_of(a_pieces, y_off, x_off)
        b_from, b_at = place_of(b_pieces, x_off, y_off)
        steps.append((y_off, x_off, (seat(a_from), a_at), (seat(b_from), b_at)))
    near = len(arrays)

    def kernel(place_ref, own_ref, away_ref, *refs):
        weights = refs[:near]
        out_own, out_away, w_buf, o_buf, w_sem, o_sem = refs[near:]
        loads = []
        for n, (_, _, a, b) in enumerate(steps):
            for side, (src, index) in enumerate((a, b)):
                for z_off in range(2):
                    z_at = place_ref[1] if z_off == 0 else 1 - place_ref[1]
                    c = pltpu.make_async_copy(
                        weights[src].at[index, z_off],
                        w_buf.at[n, z_at, :, side * half : (side + 1) * half],
                        w_sem.at[n, side, z_off],
                    )
                    c.start()
                    loads.append(c)
        stores = []
        for first in range(0, len(steps), 2):
            group = range(first, min(first + 2, len(steps)))
            for n in group:
                for c in loads[4 * n : 4 * n + 4]:
                    c.wait()
            rows = w_buf[first : first + len(group)].reshape(len(group) * 128, model)
            for who, (ev_ref, out_ref) in enumerate(((own_ref, out_own), (away_ref, out_away))):
                acc = lax.dot_general(ev_ref[...], rows, NT, preferred_element_type=F32)
                act = (0.5 * acc * (1.0 + jnp.tanh(0.5 * acc))).astype(BF16)
                for i, n in enumerate(group):
                    o_buf[n, who] = act[:, i * 128 : (i + 1) * 128]
                    c = pltpu.make_async_copy(o_buf.at[n, who], out_ref.at[n], o_sem.at[n, who])
                    c.start()
                    stores.append(c)
        for c in stores:
            c.wait()

    any_spec = pl.BlockSpec(memory_space=pltpu.HBM)
    vmem = pl.BlockSpec(memory_space=pltpu.VMEM)
    shape = jax.ShapeDtypeStruct((len(steps), count, 128), BF16)
    return pl.pallas_call(
        kernel,
        out_shape=(shape, shape),
        in_specs=[pl.BlockSpec(memory_space=pltpu.SMEM), vmem, vmem]
        + [any_spec] * near,
        out_specs=(any_spec, any_spec),
        scratch_shapes=[
            pltpu.VMEM((len(steps), 2, 64, model), BF16),
            pltpu.VMEM((len(steps), 2, count, 128), BF16),
            pltpu.SemaphoreType.DMA((len(steps), 2, 2)),
            pltpu.SemaphoreType.DMA((len(steps), 2)),
        ],
        cost_estimate=pl.CostEstimate(
            flops=4 * count * model * 128 * len(steps),
            bytes_accessed=model * 256 * len(steps),
            transcendentals=2 * count * 128 * len(steps),
        ),
        compiler_params=pltpu.CompilerParams(vmem_limit_bytes=60 * MIB),
    )(place, own, away, *arrays)


def silu(x):
    return 0.5 * x * (1.0 + jnp.tanh(0.5 * x))


def sigmoid(x):
    return 1.0 / (1.0 + jnp.exp(-x))


def block_kernel(
    place, own_hbm, par_hbm, w_out, events_hbm, targets_hbm, row, mixed_hbm, grad_hbm, keep_u, send_u,
    keep_w, send_w, col, own, par, events, targets, w_buf, attn, mixed_ref, mixed_t, outs, grad_ref,
    parts_u, parts_w, digits, b_sem, e_sem, w_sem, m_sem, p_sem, d_sem
):
    core = place[3]
    count, model = events.shape
    tile = count // 4
    blocks = []
    for who, (groups, held) in enumerate(((own_hbm, own), (par_hbm, par))):
        done = 0
        for offsets, ref in zip(ORDER, groups):
            for n, (y_off, x_off) in enumerate(offsets):
                y_at, x_at = lax.rem(place[0] + y_off, 4), lax.rem(place[2] + x_off, 4)
                c = pltpu.make_async_copy(ref.at[n], held.at[y_at, x_at], b_sem.at[who, done])
                c.start()
                blocks.append(c)
                done += 1
    loads = [
        pltpu.make_async_copy(events_hbm, events, e_sem.at[0]),
        pltpu.make_async_copy(targets_hbm, targets, e_sem.at[1]),
    ]
    for c in loads:
        c.start()
    for cls in range(2):
        for x in range(4):
            for zh in range(2):
                c = pltpu.make_async_copy(
                    w_out.at[zh * 512 + x * 128 + cls * 64 : zh * 512 + x * 128 + cls * 64 + 64],
                    w_buf.at[cls * 512 + x * 128 + zh * 64 : cls * 512 + x * 128 + zh * 64 + 64],
                    w_sem.at[cls, x, zh],
                )
                c.start()
                loads.append(c)
    col[...] = row[...].T
    lane = lax.broadcasted_iota(jnp.int32, (tile, 256), 1)
    low = lax.rem(lane, 128) < 64
    scale = 1.0 / DH**0.5
    for c in blocks:
        c.wait()
    for i in range(4):
        lo, hi = max(0, (i - 1) * tile), (i + 1) * tile
        here = slice(i * tile, hi)
        at_i = i * tile + lax.broadcasted_iota(jnp.int32, (tile, hi - lo), 0)
        at_j = lo + lax.broadcasted_iota(jnp.int32, (tile, hi - lo), 1)
        allowed = (col[here, 0:1] == row[0:1, lo:hi]) & (at_j <= at_i)
        for x in range(4):
            q = jnp.concatenate([own[2, x, here], par[2, x, here]], 1)
            k = jnp.concatenate([own[3, x, lo:hi], par[3, x, lo:hi]], 1)
            v = jnp.concatenate([own[1, x, lo:hi], par[1, x, lo:hi]], 1)
            halves = []
            for pick in (low, ~low):
                qz = jnp.where(pick, q, jnp.zeros_like(q))
                s = lax.dot_general(qz, k, NT, preferred_element_type=F32) * scale
                p = jnp.where(allowed, silu(s) * (1.0 / 128.0), 0.0).astype(BF16)
                halves.append(lax.dot_general(p, v, NN, preferred_element_type=F32))
            o = jnp.where(low, halves[0], halves[1])
            attn[here, x * 128 : (x + 1) * 128] = o[:, :128]
            attn[here, 512 + x * 128 : 512 + (x + 1) * 128] = o[:, 128:]
        a = attn[here, :]
        mean = jnp.mean(a, axis=1, keepdims=True)
        a = a - mean
        a = a * lax.rsqrt(jnp.mean(a * a, axis=1, keepdims=True) + 1e-05)
        for side, src in ((core, own), (1 - core, par)):
            base = 0 if src is own else 512
            u = jnp.concatenate([src[0, x, here] for x in range(4)], 1).astype(F32)
            m = (a[:, base : base + 512] * u).astype(BF16)
            mixed_ref[here, pl.ds(pl.multiple_of(side * 512, 512), 512)] = m
    for c in loads:
        c.wait()
    for n in range(0, model, 512):
        cols = slice(n, n + 512)
        s = jnp.dot(mixed_ref[...], w_buf[:, cols], preferred_element_type=F32)
        outs[:, cols] = (events[:, cols].astype(F32) + s).astype(BF16)
    mixed_t[...] = mixed_ref[...].T
    count_copies = [pltpu.make_async_copy(mixed_ref, mixed_hbm, m_sem)]
    scores = lax.dot_general(outs[...], targets[...], NT, preferred_element_type=F32)
    at_i = lax.broadcasted_iota(jnp.int32, (count, count), 0)
    at_j = lax.broadcasted_iota(jnp.int32, (count, count), 1)
    other = col[:, 1:2] != row[1:2, :]
    coef = sigmoid(jnp.where(at_i == at_j, -scores, scores))
    coef = jnp.where(
        at_i == at_j, -coef, jnp.where(other, coef * (1.0 / count), 0.0)
    ).astype(BF16)
    flagged = jnp.sum(row[2:3, :], axis=1, keepdims=True)
    high = jnp.floor(flagged * (1.0 / 32.0))
    at = lax.broadcasted_iota(jnp.int32, (512, 128), 1)
    digits[...] = jnp.where(at == 0, high, jnp.where(at == 1, flagged - 32.0 * high, 0.0)).astype(BF16)
    count_copies += [
        pltpu.make_async_copy(digits, ref.at[:, model : model + 128], d_sem.at[i])
        for i, ref in enumerate((keep_u, send_u))
    ]
    for c in count_copies:
        c.start()
    stores = [None, None]
    for turn, n in enumerate(range(0, model, 512)):
        cols = slice(n, n + 512)
        slot = turn % 2
        g = jnp.dot(coef, targets[:, cols], preferred_element_type=F32).astype(BF16)
        grad_ref[:, cols] = g
        unif = (g.astype(F32) * col[:, 2:3]).astype(BF16)
        scaled = (g.astype(F32) * col[:, 3:4]).astype(BF16)
        g_u = jnp.dot(mixed_t[...], unif, preferred_element_type=F32)
        g_w = jnp.dot(mixed_t[...], scaled, preferred_element_type=F32)
        if stores[slot] is not None:
            for c in stores[slot]:
                c.wait()
        parts_u[slot] = g_u.astype(BF16).reshape(2, 512, 512)
        for to in range(2):
            for q in range(32):
                x, y, zh = q // 8, q // 2 % 4, q % 2
                r = (y * 8 + zh * 4 + x) * 32 + to * 16
                w_at = (r // 64 % 2) * 512 + (r // 128 % 4) * 128 + (r // 512) * 64 + r % 64
                parts_w[slot, to, q * 16 : q * 16 + 16] = g_w[w_at : w_at + 16].astype(BF16)
        stores[slot] = []
        for which, (ref, src) in enumerate(
            (
                (keep_u, parts_u.at[slot, core]),
                (send_u, parts_u.at[slot, 1 - core]),
                (keep_w, parts_w.at[slot, core]),
                (send_w, parts_w.at[slot, 1 - core]),
                (grad_hbm, grad_ref.at[:, cols]),
            )
        ):
            c = pltpu.make_async_copy(src, ref.at[:, cols], p_sem.at[slot, which])
            c.start()
            stores[slot].append(c)
    for pending in stores:
        for c in pending:
            c.wait()
    for c in count_copies:
        c.wait()


def block_call(place, own, par, events, targets, w_out, row):
    count, model = events.shape
    width = w_out.shape[0]
    any_spec = pl.BlockSpec(memory_space=pltpu.HBM)
    vmem = pl.BlockSpec(memory_space=pltpu.VMEM)
    part_u = jax.ShapeDtypeStruct((512, model + 128), BF16)
    part_w = jax.ShapeDtypeStruct((512, model), BF16)
    groups = len(own)

    def kernel(place_ref, *refs):
        block_kernel(place_ref, refs[:groups], refs[groups : 2 * groups], *refs[2 * groups :])
    return pl.pallas_call(
        kernel,
        out_shape=(
            jax.ShapeDtypeStruct((count, width), BF16),
            jax.ShapeDtypeStruct((count, model), BF16),
            part_u,
            part_u,
            part_w,
            part_w,
        ),
        in_specs=[pl.BlockSpec(memory_space=pltpu.SMEM)]
        + [any_spec] * (2 * groups + 3)
        + [vmem],
        out_specs=(any_spec,) * 2 + (pl.BlockSpec(memory_space=pl.ANY),) * 2 + (any_spec,) * 2,
        scratch_shapes=[
            pltpu.VMEM((count, row.shape[0]), F32),
            pltpu.VMEM((4, 4, count, 128), BF16),
            pltpu.VMEM((4, 4, count, 128), BF16),
            pltpu.VMEM((count, model), BF16),
            pltpu.VMEM((count, model), BF16),
            pltpu.VMEM((width, model), BF16),
            pltpu.VMEM((count, width), F32),
            pltpu.VMEM((count, width), BF16),
            pltpu.VMEM((width, count), BF16),
            pltpu.VMEM((count, model), BF16),
            pltpu.VMEM((count, model), BF16),
            pltpu.VMEM((2, 2, 512, 512), BF16),
            pltpu.VMEM((2, 2, 512, 512), BF16),
            pltpu.VMEM((512, 128), BF16),
            pltpu.SemaphoreType.DMA((2, 16)),
            pltpu.SemaphoreType.DMA((2,)),
            pltpu.SemaphoreType.DMA((2, 4, 2)),
            pltpu.SemaphoreType.DMA,
            pltpu.SemaphoreType.DMA((2, 5)),
            pltpu.SemaphoreType.DMA((2,)),
        ],
        cost_estimate=pl.CostEstimate(
            flops=10 * 1024 * MIB, bytes_accessed=24 * MIB, transcendentals=2 * MIB
        ),
        compiler_params=pltpu.CompilerParams(vmem_limit_bytes=50 * MIB),
    )(place, *own, *par, w_out, events, targets, row)


def on_device(events, w_uvqk, w_out, targets, item_ids, uniform_flags, lengths, seq_weights):
    count = events.shape[0]
    core = lax.axis_index("c")
    flag = uniform_flags.astype(F32)
    spot = jnp.stack([lax.axis_index(n) for n in ("y", "zh", "x", "c")]).astype(jnp.int32)
    w_out_all = lax.all_gather(w_out, ("y", "zh", "x", "c"), axis=0, tiled=True)
    place = jnp.arange(count, dtype=jnp.int32)
    ends = jnp.cumsum(lengths[0])
    seqid = jnp.sum((place[:, None] >= ends[None, :]).astype(jnp.int32), axis=1)
    member = (seqid[:, None] == jnp.arange(seq_weights.shape[0], dtype=jnp.int32)[None, :]).astype(
        F32
    )
    weight_row = jnp.sum(member * seq_weights[None, :], axis=1) * (1.0 - flag)
    facts = [seqid.astype(F32), item_ids.astype(F32), flag, weight_row]
    row = jnp.stack(facts + [jnp.zeros_like(flag)] * 4)

    away = lax.ppermute(events, "c", SWAP)
    phases, (spot, row) = gather_proj(w_uvqk, (spot, row))
    own, par = [], []
    for (a_pieces, b_pieces), offsets in zip(phases, ORDER):
        mine, for_away = uvqk_call(spot, events, away, a_pieces, b_pieces, offsets)
        own.append(mine)
        par.append(lax.ppermute(for_away, "c", SWAP))
    mixed, grad_out, keep_u, send_u, keep_w, send_w = block_call(
        spot, own, par, events, targets, w_out_all, row
    )

    def add(mine, away):
        return (mine.astype(F32) + lax.ppermute(away, "c", SWAP).astype(F32)).astype(BF16)

    model = events.shape[1]
    chip_u, chip_w = add(keep_u, send_u), add(keep_w, send_w)
    part_w = lax.psum_scatter(chip_w, "x", scatter_dimension=0, tiled=True)
    got = lax.all_to_all(chip_u.reshape(64, 8, -1), CHIPS, 0, 0, tiled=True)
    total = jnp.sum(got.astype(F32), axis=0)
    n_unif = 32.0 * total[0, model] + total[0, model + 1]
    unif = jnp.broadcast_to(total[:, :model].astype(BF16)[None], (64, 8, model))
    unif_mine = lax.all_to_all(unif, CHIPS, 0, 0, tiled=True).reshape(512, -1)
    unif_mine, part_w = lax.optimization_barrier((unif_mine, part_w))
    got_w = lax.all_to_all(part_w.reshape(16, 8, model), ("y", "zh", "zl"), 0, 0, tiled=True)
    unif_away = lax.ppermute(unif_mine, "c", SWAP)
    mixed_mine = lax.dynamic_slice_in_dim(mixed, core * 512, 512, 1)
    mixed_away = lax.dynamic_slice_in_dim(mixed, (1 - core) * 512, 512, 1)
    proj_mine = jnp.dot(grad_out, unif_mine.T, preferred_element_type=F32)
    proj_away = jnp.dot(grad_out, unif_away.T, preferred_element_type=F32)
    per_row = jnp.sum(mixed_mine.astype(F32) * proj_mine, axis=1) + jnp.sum(
        mixed_away.astype(F32) * proj_away, axis=1
    )
    per_row = -per_row * (1.0 - flag) / n_unif
    hyper = jnp.sum(member * per_row[:, None], axis=0)
    hyper, got_w = lax.optimization_barrier((hyper, got_w))
    weighted_grad = jnp.sum(got_w.astype(F32), axis=0) / (jnp.float32(count * 128) - n_unif)
    return (hyper, weighted_grad)


def solution(mesh):
    fine = Mesh(mesh.devices.reshape(4, 2, 4, 2, 2), AXES)
    dp = ("y", "zh", "x", "c")
    return jax.shard_map(
        on_device,
        mesh=fine,
        in_specs=(
            P(AXES, None),
            P(None, dp),
            P(dp, None),
            P(AXES, None),
            P(AXES),
            P(AXES),
            P(AXES, None),
            P(AXES),
        ),
        out_specs=(P(AXES), P(AXES, None)),
        check_vma=False,
    )
```

```python
import jax
import jax.numpy as jnp
from jax import lax
from jax.experimental import pallas as pl
from jax.experimental.pallas import tpu as pltpu
from jax.sharding import Mesh
from jax.sharding import PartitionSpec as P

HEADS = 8
DH = 128
AXES = ("y", "zh", "x", "c", "zl")
CHIPS = ("y", "zh", "x", "zl")
SWAP = [(0, 1), (1, 0)]
ACROSS = [(0, 3), (3, 0), (1, 2), (2, 1)]
ORDER = (
    ((0, 0), (0, 1), (0, 3), (1, 0), (1, 1), (1, 3), (3, 0), (3, 1), (3, 3)),
    ((0, 2), (1, 2), (3, 2), (2, 0), (2, 1), (2, 3), (2, 2)),
)
F32 = jnp.float32
BF16 = jnp.bfloat16
MIB = 1024 * 1024
NT = (((1,), (1,)), ((), ()))
NN = (((1,), (0,)), ((), ()))


def hop(array, axis, step):
    return lax.ppermute(array, axis, [(i, (i + step) % 4) for i in range(4)])


def first_rings(a, a_axis, b, b_axis, cut, also):
    got, also = lax.optimization_barrier(
        ((hop(a, a_axis, 1), hop(a, a_axis, -1), hop(b, b_axis, 1), hop(b, b_axis, -1)), also)
    )
    a_below, a_above, b_below, b_above = got
    far = (
        hop(a_below[:cut], a_axis, 1),
        hop(a_above[cut:], a_axis, -1),
        hop(b_below[:cut], b_axis, 1),
        hop(b_above[cut:], b_axis, -1),
    )
    return (a, a_above, far[:2], a_below), (b, b_above, far[2:], b_below), also


def last_rings(a, b):
    one = (hop(a[0], "y", 1), hop(a[1], "y", -1), hop(b[0], "x", 1), hop(b[1], "x", -1))
    two = (hop(a[1], "y", 1), hop(a[0], "y", -1), hop(b[1], "x", 1), hop(b[0], "x", -1))
    one = lax.optimization_barrier(one)
    a_near = (a, (two[1], one[1]), None, (one[0], two[0]))
    b_near = (b, (two[3], one[3]), None, (one[2], two[2]))
    a_far = (hop(one[0], "y", 1), hop(one[1], "y", -1))
    b_far = (hop(one[2], "x", 1), hop(one[3], "x", -1))
    last = (a_near[:2] + (a_far, a_near[3]), b_near[:2] + (b_far, b_near[3]))
    return (a_near, b_near), last


def gather_proj(w_uvqk, also):
    half = w_uvqk.shape[0] // 2
    rows = w_uvqk.T
    other = lax.ppermute(rows, ("zh", "zl"), ACROSS)
    both = jnp.stack([rows, other])
    a_line, b_line, also = first_rings(both[:, :, :half], "x", both[:, :, half:], "y", 1, also)

    def halves(pieces):
        own, above, far, below = pieces
        return jnp.stack([own, above]), jnp.stack([jnp.concatenate(far, 0), below])

    return last_rings(halves(a_line), halves(b_line)), also


def place_of(pieces, major, minor):
    return pieces[major][minor // 2], minor % 2


def uvqk_call(place, own, away, a_pieces, b_pieces, offsets):
    count, model = own.shape
    half = model // 2
    arrays, steps = [], []

    def seat(array):
        for i, seen in enumerate(arrays):
            if seen is array:
                return i
        arrays.append(array)
        return len(arrays) - 1

    for y_off, x_off in offsets:
        a_from, a_at = place_of(a_pieces, y_off, x_off)
        b_from, b_at = place_of(b_pieces, x_off, y_off)
        steps.append((y_off, x_off, (seat(a_from), a_at), (seat(b_from), b_at)))
    near = len(arrays)

    def kernel(place_ref, own_ref, away_ref, *refs):
        weights = refs[:near]
        out_own, out_away, w_buf, o_buf, w_sem, o_sem = refs[near:]
        loads = []
        for n, (_, _, a, b) in enumerate(steps):
            for side, (src, index) in enumerate((a, b)):
                for z_off in range(2):
                    z_at = place_ref[1] if z_off == 0 else 1 - place_ref[1]
                    c = pltpu.make_async_copy(
                        weights[src].at[index, z_off],
                        w_buf.at[n, z_at, :, side * half : (side + 1) * half],
                        w_sem.at[n, side, z_off],
                    )
                    c.start()
                    loads.append(c)
        stores = []
        for first in range(0, len(steps), 2):
            group = range(first, min(first + 2, len(steps)))
            for n in group:
                for c in loads[4 * n : 4 * n + 4]:
                    c.wait()
            rows = w_buf[first : first + len(group)].reshape(len(group) * 128, model)
            for who, (ev_ref, out_ref) in enumerate(((own_ref, out_own), (away_ref, out_away))):
                acc = lax.dot_general(ev_ref[...], rows, NT, preferred_element_type=F32)
                act = (0.5 * acc * (1.0 + jnp.tanh(0.5 * acc))).astype(BF16)
                for i, n in enumerate(group):
                    o_buf[n, who] = act[:, i * 128 : (i + 1) * 128]
                    c = pltpu.make_async_copy(o_buf.at[n, who], out_ref.at[n], o_sem.at[n, who])
                    c.start()
                    stores.append(c)
        for c in stores:
            c.wait()

    any_spec = pl.BlockSpec(memory_space=pltpu.HBM)
    vmem = pl.BlockSpec(memory_space=pltpu.VMEM)
    shape = jax.ShapeDtypeStruct((len(steps), count, 128), BF16)
    return pl.pallas_call(
        kernel,
        out_shape=(shape, shape),
        in_specs=[pl.BlockSpec(memory_space=pltpu.SMEM), vmem, vmem]
        + [any_spec] * near,
        out_specs=(any_spec, any_spec),
        scratch_shapes=[
            pltpu.VMEM((len(steps), 2, 64, model), BF16),
            pltpu.VMEM((len(steps), 2, count, 128), BF16),
            pltpu.SemaphoreType.DMA((len(steps), 2, 2)),
            pltpu.SemaphoreType.DMA((len(steps), 2)),
        ],
        cost_estimate=pl.CostEstimate(
            flops=4 * count * model * 128 * len(steps),
            bytes_accessed=model * 256 * len(steps),
            transcendentals=2 * count * 128 * len(steps),
        ),
        compiler_params=pltpu.CompilerParams(vmem_limit_bytes=60 * MIB),
    )(place, own, away, *arrays)


def silu(x):
    return 0.5 * x * (1.0 + jnp.tanh(0.5 * x))


def sigmoid(x):
    return 1.0 / (1.0 + jnp.exp(-x))


def block_kernel(
    place, own_hbm, par_hbm, w_out, events_hbm, targets_hbm, col, row, mixed_hbm, grad_hbm, keep_u, send_u,
    keep_w, send_w, own, par, events, targets, w_buf, attn, mixed_ref, mixed_t, outs, grad_ref,
    parts_u, parts_w, digits, b_sem, e_sem, w_sem, m_sem, p_sem, d_sem
):
    core = place[3]
    count, model = events.shape
    tile = count // 4
    blocks = []
    for who, (groups, held) in enumerate(((own_hbm, own), (par_hbm, par))):
        done = 0
        for offsets, ref in zip(ORDER, groups):
            for n, (y_off, x_off) in enumerate(offsets):
                y_at, x_at = lax.rem(place[0] + y_off, 4), lax.rem(place[2] + x_off, 4)
                c = pltpu.make_async_copy(ref.at[n], held.at[y_at, x_at], b_sem.at[who, done])
                c.start()
                blocks.append(c)
                done += 1
    loads = [
        pltpu.make_async_copy(events_hbm, events, e_sem.at[0]),
        pltpu.make_async_copy(targets_hbm, targets, e_sem.at[1]),
    ]
    for c in loads:
        c.start()
    for cls in range(2):
        for x in range(4):
            for zh in range(2):
                c = pltpu.make_async_copy(
                    w_out.at[zh * 512 + x * 128 + cls * 64 : zh * 512 + x * 128 + cls * 64 + 64],
                    w_buf.at[cls * 512 + x * 128 + zh * 64 : cls * 512 + x * 128 + zh * 64 + 64],
                    w_sem.at[cls, x, zh],
                )
                c.start()
                loads.append(c)
    lane = lax.broadcasted_iota(jnp.int32, (tile, 256), 1)
    low = lax.rem(lane, 128) < 64
    scale = 1.0 / DH**0.5
    for c in blocks:
        c.wait()
    for i in range(4):
        lo, hi = max(0, (i - 1) * tile), (i + 1) * tile
        here = slice(i * tile, hi)
        at_i = i * tile + lax.broadcasted_iota(jnp.int32, (tile, hi - lo), 0)
        at_j = lo + lax.broadcasted_iota(jnp.int32, (tile, hi - lo), 1)
        allowed = (col[here, 0:1] == row[0:1, lo:hi]) & (at_j <= at_i)
        for x in range(4):
            q = jnp.concatenate([own[2, x, here], par[2, x, here]], 1)
            k = jnp.concatenate([own[3, x, lo:hi], par[3, x, lo:hi]], 1)
            v = jnp.concatenate([own[1, x, lo:hi], par[1, x, lo:hi]], 1)
            halves = []
            for pick in (low, ~low):
                qz = jnp.where(pick, q, jnp.zeros_like(q))
                s = lax.dot_general(qz, k, NT, preferred_element_type=F32) * scale
                p = jnp.where(allowed, silu(s) * (1.0 / 128.0), 0.0).astype(BF16)
                halves.append(lax.dot_general(p, v, NN, preferred_element_type=F32))
            o = jnp.where(low, halves[0], halves[1])
            attn[here, x * 128 : (x + 1) * 128] = o[:, :128]
            attn[here, 512 + x * 128 : 512 + (x + 1) * 128] = o[:, 128:]
        a = attn[here, :]
        mean = jnp.mean(a, axis=1, keepdims=True)
        a = a - mean
        a = a * lax.rsqrt(jnp.mean(a * a, axis=1, keepdims=True) + 1e-05)
        for side, src in ((core, own), (1 - core, par)):
            base = 0 if src is own else 512
            u = jnp.concatenate([src[0, x, here] for x in range(4)], 1).astype(F32)
            m = (a[:, base : base + 512] * u).astype(BF16)
            mixed_ref[here, pl.ds(pl.multiple_of(side * 512, 512), 512)] = m
    for c in loads:
        c.wait()
    for n in range(0, model, 512):
        cols = slice(n, n + 512)
        s = jnp.dot(mixed_ref[...], w_buf[:, cols], preferred_element_type=F32)
        outs[:, cols] = (events[:, cols].astype(F32) + s).astype(BF16)
    mixed_t[...] = mixed_ref[...].T
    count_copies = [pltpu.make_async_copy(mixed_ref, mixed_hbm, m_sem)]
    scores = lax.dot_general(outs[...], targets[...], NT, preferred_element_type=F32)
    at_i = lax.broadcasted_iota(jnp.int32, (count, count), 0)
    at_j = lax.broadcasted_iota(jnp.int32, (count, count), 1)
    other = col[:, 1:2] != row[1:2, :]
    coef = sigmoid(jnp.where(at_i == at_j, -scores, scores))
    coef = jnp.where(
        at_i == at_j, -coef, jnp.where(other, coef * (1.0 / count), 0.0)
    ).astype(BF16)
    flagged = jnp.sum(row[2:3, :], axis=1, keepdims=True)
    high = jnp.floor(flagged * (1.0 / 32.0))
    at = lax.broadcasted_iota(jnp.int32, (512, 128), 1)
    digits[...] = jnp.where(at == 0, high, jnp.where(at == 1, flagged - 32.0 * high, 0.0)).astype(BF16)
    count_copies += [
        pltpu.make_async_copy(digits, ref.at[:, model : model + 128], d_sem.at[i])
        for i, ref in enumerate((keep_u, send_u))
    ]
    for c in count_copies:
        c.start()
    stores = [None, None]
    for turn, n in enumerate(range(0, model, 512)):
        cols = slice(n, n + 512)
        slot = turn % 2
        g = jnp.dot(coef, targets[:, cols], preferred_element_type=F32).astype(BF16)
        grad_ref[:, cols] = g
        unif = (g.astype(F32) * col[:, 2:3]).astype(BF16)
        scaled = (g.astype(F32) * col[:, 3:4]).astype(BF16)
        g_u = jnp.dot(mixed_t[...], unif, preferred_element_type=F32)
        g_w = jnp.dot(mixed_t[...], scaled, preferred_element_type=F32)
        if stores[slot] is not None:
            for c in stores[slot]:
                c.wait()
        parts_u[slot] = g_u.astype(BF16).reshape(2, 512, 512)
        for to in range(2):
            for q in range(32):
                x, y, zh = q // 8, q // 2 % 4, q % 2
                r = (y * 8 + zh * 4 + x) * 32 + to * 16
                w_at = (r // 64 % 2) * 512 + (r // 128 % 4) * 128 + (r // 512) * 64 + r % 64
                parts_w[slot, to, q * 16 : q * 16 + 16] = g_w[w_at : w_at + 16].astype(BF16)
        stores[slot] = []
        for which, (ref, src) in enumerate(
            (
                (keep_u, parts_u.at[slot, core]),
                (send_u, parts_u.at[slot, 1 - core]),
                (keep_w, parts_w.at[slot, core]),
                (send_w, parts_w.at[slot, 1 - core]),
                (grad_hbm, grad_ref.at[:, cols]),
            )
        ):
            c = pltpu.make_async_copy(src, ref.at[:, cols], p_sem.at[slot, which])
            c.start()
            stores[slot].append(c)
    for pending in stores:
        for c in pending:
            c.wait()
    for c in count_copies:
        c.wait()


def block_call(place, own, par, events, targets, w_out, col, row):
    count, model = events.shape
    width = w_out.shape[0]
    any_spec = pl.BlockSpec(memory_space=pltpu.HBM)
    vmem = pl.BlockSpec(memory_space=pltpu.VMEM)
    part_u = jax.ShapeDtypeStruct((512, model + 128), BF16)
    part_w = jax.ShapeDtypeStruct((512, model), BF16)
    groups = len(own)

    def kernel(place_ref, *refs):
        block_kernel(place_ref, refs[:groups], refs[groups : 2 * groups], *refs[2 * groups :])
    return pl.pallas_call(
        kernel,
        out_shape=(
            jax.ShapeDtypeStruct((count, width), BF16),
            jax.ShapeDtypeStruct((count, model), BF16),
            part_u,
            part_u,
            part_w,
            part_w,
        ),
        in_specs=[pl.BlockSpec(memory_space=pltpu.SMEM)]
        + [any_spec] * (2 * groups + 3)
        + [vmem] * 2,
        out_specs=(any_spec,) * 2 + (pl.BlockSpec(memory_space=pl.ANY),) * 2 + (any_spec,) * 2,
        scratch_shapes=[
            pltpu.VMEM((4, 4, count, 128), BF16),
            pltpu.VMEM((4, 4, count, 128), BF16),
            pltpu.VMEM((count, model), BF16),
            pltpu.VMEM((count, model), BF16),
            pltpu.VMEM((width, model), BF16),
            pltpu.VMEM((count, width), F32),
            pltpu.VMEM((count, width), BF16),
            pltpu.VMEM((width, count), BF16),
            pltpu.VMEM((count, model), BF16),
            pltpu.VMEM((count, model), BF16),
            pltpu.VMEM((2, 2, 512, 512), BF16),
            pltpu.VMEM((2, 2, 512, 512), BF16),
            pltpu.VMEM((512, 128), BF16),
            pltpu.SemaphoreType.DMA((2, 16)),
            pltpu.SemaphoreType.DMA((2,)),
            pltpu.SemaphoreType.DMA((2, 4, 2)),
            pltpu.SemaphoreType.DMA,
            pltpu.SemaphoreType.DMA((2, 5)),
            pltpu.SemaphoreType.DMA((2,)),
        ],
        cost_estimate=pl.CostEstimate(
            flops=10 * 1024 * MIB, bytes_accessed=24 * MIB, transcendentals=2 * MIB
        ),
        compiler_params=pltpu.CompilerParams(vmem_limit_bytes=60 * MIB),
    )(place, *own, *par, w_out, events, targets, col, row)


def on_device(events, w_uvqk, w_out, targets, item_ids, uniform_flags, lengths, seq_weights):
    count = events.shape[0]
    core = lax.axis_index("c")
    flag = uniform_flags.astype(F32)
    spot = jnp.stack([lax.axis_index(n) for n in ("y", "zh", "x", "c")]).astype(jnp.int32)
    w_out_all = lax.all_gather(w_out, ("y", "zh", "x", "c"), axis=0, tiled=True)
    place = jnp.arange(count, dtype=jnp.int32)
    ends = jnp.cumsum(lengths[0])
    seqid = jnp.sum((place[:, None] >= ends[None, :]).astype(jnp.int32), axis=1)
    member = (seqid[:, None] == jnp.arange(seq_weights.shape[0], dtype=jnp.int32)[None, :]).astype(
        F32
    )
    weight_row = jnp.sum(member * seq_weights[None, :], axis=1) * (1.0 - flag)
    facts = [seqid.astype(F32), item_ids.astype(F32), flag, weight_row]
    row = jnp.stack(facts + [jnp.zeros_like(flag)] * 4)
    col = row.T

    away = lax.ppermute(events, "c", SWAP)
    phases, (spot, col, row) = gather_proj(w_uvqk, (spot, col, row))
    own, par = [], []
    for (a_pieces, b_pieces), offsets in zip(phases, ORDER):
        mine, for_away = uvqk_call(spot, events, away, a_pieces, b_pieces, offsets)
        own.append(mine)
        par.append(lax.ppermute(for_away, "c", SWAP))
    mixed, grad_out, keep_u, send_u, keep_w, send_w = block_call(
        spot, own, par, events, targets, w_out_all, col, row
    )

    def add(mine, away):
        return (mine.astype(F32) + lax.ppermute(away, "c", SWAP).astype(F32)).astype(BF16)

    model = events.shape[1]
    chip_u, chip_w = add(keep_u, send_u), add(keep_w, send_w)
    part_w = lax.psum_scatter(chip_w, "x", scatter_dimension=0, tiled=True)
    got = lax.all_to_all(chip_u.reshape(64, 8, -1), CHIPS, 0, 0, tiled=True)
    total = jnp.sum(got.astype(F32), axis=0)
    n_unif = 32.0 * total[0, model] + total[0, model + 1]
    unif = jnp.broadcast_to(total[:, :model].astype(BF16)[None], (64, 8, model))
    unif_mine = lax.all_to_all(unif, CHIPS, 0, 0, tiled=True).reshape(512, -1)
    unif_mine, part_w = lax.optimization_barrier((unif_mine, part_w))
    got_w = lax.all_to_all(part_w.reshape(16, 8, model), ("y", "zh", "zl"), 0, 0, tiled=True)
    unif_away = lax.ppermute(unif_mine, "c", SWAP)
    mixed_mine = lax.dynamic_slice_in_dim(mixed, core * 512, 512, 1)
    mixed_away = lax.dynamic_slice_in_dim(mixed, (1 - core) * 512, 512, 1)
    proj_mine = jnp.dot(grad_out, unif_mine.T, preferred_element_type=F32)
    proj_away = jnp.dot(grad_out, unif_away.T, preferred_element_type=F32)
    per_row = jnp.sum(mixed_mine.astype(F32) * proj_mine, axis=1) + jnp.sum(
        mixed_away.astype(F32) * proj_away, axis=1
    )
    per_row = -per_row * (1.0 - flag) / n_unif
    hyper = jnp.sum(member * per_row[:, None], axis=0)
    hyper, got_w = lax.optimization_barrier((hyper, got_w))
    weighted_grad = jnp.sum(got_w.astype(F32), axis=0) / (jnp.float32(count * 128) - n_unif)
    return (hyper, weighted_grad)


def solution(mesh):
    fine = Mesh(mesh.devices.reshape(4, 2, 4, 2, 2), AXES)
    dp = ("y", "zh", "x", "c")
    return jax.shard_map(
        on_device,
        mesh=fine,
        in_specs=(
            P(AXES, None),
            P(None, dp),
            P(dp, None),
            P(AXES, None),
            P(AXES),
            P(AXES),
            P(AXES, None),
            P(AXES),
        ),
        out_specs=(P(AXES), P(AXES, None)),
        check_vma=False,
    )
```
